32 devices in a mesh: group: 2 (over y), pix: 16 (over z, x, core).
Axes of the slice: x: 2, y: 2, z: 4, core: 2. Of those that a mesh axis runs over, the one named last changes fastest.
Arguments:
- images: bfloat16 [256, 2, 120, 840], P(('group', 'pix')), parts along dimension 0, may hold values from -170 to 170
- valid_mask: int32 [256, 840], P(('group', 'pix')), parts along dimension 0, may hold values from 0 to 1
Outputs:
- look_coherence: bfloat16 [128, 40, 2, 120, 120], P(('group', 'pix')), parts along dimension 0
- slab_coherence: float32 [4, 120, 120], P('group'), parts along dimension 0
The draws below stay inside these ranges and needn't reach their ends.
There are 2 independent parts, one for each index of `group`. The reference program is written for one: setup_inputs(seed, part) draws one part's arguments, and reference() takes and returns one part's arrays. A program takes and returns all parts, laid end to end along the dimension named above; each array names one. Nothing has to cross between parts.
All inputs are finite; a program needn't handle non-finite values.
Results may differ from the reference program's by a relative error of at most 0.001.
Values may be sent and summed in bfloat16 or wider, within the bound.
No kernel may reach another device: no remote copies, remote signals or barrier semaphores. Data moves between devices by JAX's collectives and lax.ppermute only.
A program may use at most 128 MiB of HBM per device.

```python
import math
import jax
import jax.numpy as jnp
from jax import lax

M = 120
ROWS = 128
COLS = 840


def draw_images(key, part):
    keys = jax.random.split(key, 6)
    signal = jnp.clip(jax.random.normal(keys[0], (ROWS, 2, 1, COLS), jnp.float32), -3.5, 3.5)
    noise = jnp.clip(jax.random.normal(keys[1], (ROWS, 2, M, COLS), jnp.float32), -5.0, 5.0)
    common = 2.0
    rate_block = jnp.exp(jax.random.uniform(keys[2], (ROWS // 4, COLS // 21), jnp.float32, math.log(0.005), math.log(0.2)))
    rates = jnp.repeat(jnp.repeat(rate_block, 4, axis=0), 21, axis=1)
    acq_index = jnp.arange(M, dtype=jnp.float32)
    weights = common * jnp.exp(-rates[:, None, :] * acq_index[None, :, None])
    phase_block = jax.random.uniform(keys[5], (ROWS // 4, M), jnp.float32, -math.pi, math.pi)
    phases = jnp.repeat(phase_block, 4, axis=0)
    cosine = jnp.cos(phases)[:, :, None]
    sine = jnp.sin(phases)[:, :, None]
    sig_re = signal[:, 0]
    sig_im = signal[:, 1]
    rot_re = weights * (sig_re * cosine - sig_im * sine)
    rot_im = weights * (sig_re * sine + sig_im * cosine)
    rotated = jnp.stack([rot_re, rot_im], axis=1)
    acq_scale = jnp.exp(jax.random.uniform(keys[3], (M,), jnp.float32, math.log(0.5), math.log(2.0)))
    rough = jnp.exp(jax.random.uniform(keys[4], (ROWS, COLS), jnp.float32, math.log(0.7), math.log(1.4)))
    pixel_scale = rough
    values = (rotated + noise) * acq_scale[None, None, :, None] * pixel_scale[:, None, None, :]
    return values.astype(jnp.bfloat16)


def draw_valid_mask(key, part):
    keys = jax.random.split(key, 3)
    first = jax.random.randint(keys[0], (ROWS, COLS), 0, 12)
    second = jax.random.randint(keys[1], (ROWS, COLS), 0, 12)
    level_draw = jax.random.randint(keys[2], (ROWS // 4, COLS // 21), 0, 24)
    levels = jnp.where(level_draw == 0, 0, jnp.where(level_draw == 1, 3, 11 + level_draw % 2))
    levels = jnp.repeat(jnp.repeat(levels, 4, axis=0), 21, axis=1)
    band = 11 + 2 * jnp.arange(ROWS, dtype=jnp.int32) // ROWS
    valid = (first < levels) & (second < band[:, None])
    return valid.astype(jnp.int32)


def setup_inputs(seed: int = 0, part: int = 0) -> dict:
    key_list = jax.random.split(jax.random.key(seed), 3)
    own_keys = jax.random.split(jax.random.fold_in(key_list[2], part), 3)
    images = draw_images(jax.random.fold_in(jax.random.fold_in(key_list[2], part), 71), part)
    valid_mask = draw_valid_mask(jax.random.fold_in(jax.random.fold_in(key_list[2], part), 71), part)
    return {"images": images, "valid_mask": valid_mask}


floor_power = 30.0

def split_parts(grams):
    real_part = grams[..., 0, :, 0, :] + grams[..., 1, :, 1, :]
    imag_part = grams[..., 1, :, 0, :] - grams[..., 0, :, 1, :]
    return (real_part, imag_part)

def coherence(real_part, imag_part, with_floor):
    powers = jnp.diagonal(real_part, axis1=-2, axis2=-1)
    if with_floor:
        powers = jnp.maximum(powers, floor_power)
    scaled = jnp.sqrt(powers[..., :, None] * powers[..., None, :])
    return jnp.stack([real_part / scaled, imag_part / scaled], axis=-3)

def reference(images, valid_mask):
    masked = images * valid_mask[:, None, None, :].astype(jnp.bfloat16)
    widened = masked.astype(jnp.float32)
    slab_grams = jnp.einsum('rkic,rhjc->kihj', widened, widened)
    slab_real, slab_imag = split_parts(slab_grams)
    slab_coherence = coherence(slab_real, slab_imag, False)
    padded = jnp.pad(widened, ((3, 3), (0, 0), (0, 0), (0, 0)))
    acq_count = images.shape[2]
    look_cols = images.shape[3] // 21

    def one_look(look_index):
        window_data = lax.dynamic_slice_in_dim(padded, (2 * look_index).astype(jnp.int32), 7, 0)
        blocks = window_data.reshape(7, 2, acq_count, look_cols, 21)
        grams = jnp.einsum('rkilq,rhjlq->lkihj', blocks, blocks)
        real_part, imag_part = split_parts(grams)
        return coherence(real_part, imag_part, True).astype(jnp.bfloat16)
    look_coherence = lax.map(one_look, jnp.arange(ROWS // 2, dtype=jnp.int32))
    return (look_coherence, slab_coherence)
```

```python
import functools
import jax
import jax.numpy as jnp
from jax import lax
from jax.experimental import pallas as pl
from jax.experimental.pallas import tpu as pltpu
from jax.sharding import PartitionSpec as P

floor_power = 30.0

LOOK = 21
LANES = 128
PER = LANES // LOOK
SPAN = PER * LOOK
ROWS = 8
SKEW = (5, 0, 1, 2, 3, 4, 1, 2)
BEFORE, AFTER = 3, 2
NT = (((1,), (1,)), ((), ()))


def skew_kernel(first, columns, has_sum, *refs):
    if has_sum:
        prev_ref, cur_ref, mask_prev_ref, mask_cur_ref, sum_ref, top_ref, mid_ref, low_ref, gram_ref, z_ref, acc_ref = refs
    else:
        prev_ref, cur_ref, mask_prev_ref, mask_cur_ref, top_ref, mid_ref, low_ref, gram_ref, z_ref, acc_ref = refs
    step = pl.program_id(0)
    g = step + first
    count = cur_ref.shape[2]

    @pl.when(step == 0)
    def _():
        z_ref[...] = jnp.zeros_like(z_ref)
        acc_ref[...] = jnp.zeros_like(acc_ref)

    lane = lax.broadcasted_iota(jnp.int32, (1, LANES), 1)
    from_prev = lane >= LANES - 2 * g
    place = jnp.where(from_prev, lane + 2 * g - LANES, lane + 2 * g)
    used = (place < SPAN) & (SPAN * g + place < columns)
    mask = jnp.where(from_prev, mask_prev_ref[...], mask_cur_ref[...])
    keep = jnp.where(used, mask, 0).astype(jnp.float32)
    prev_keep = jnp.broadcast_to(from_prev.astype(jnp.float32), (count, LANES)).astype(jnp.bfloat16) != 0
    zero = jnp.zeros((count, LANES), jnp.bfloat16)
    for r in range(ROWS):
        keep_r = jnp.broadcast_to(keep[r : r + 1], (count, LANES)).astype(jnp.bfloat16) != 0
        for k in range(2):
            row = jnp.where(prev_keep, prev_ref[r, k], cur_ref[r, k])
            row = jnp.where(keep_r, row, zero)
            row = pltpu.roll(row, 2 * g + LOOK * SKEW[r], 1)
            z_ref[pl.ds(k * LANES, count), pl.ds(r * LANES, LANES)] = row
            if r < AFTER:
                top_ref[0, r, k] = row
            elif r >= ROWS - BEFORE:
                low_ref[0, r - (ROWS - BEFORE), k] = row
            else:
                mid_ref[0, r - AFTER, k] = row
    z = z_ref[...]
    acc_ref[...] += lax.dot_general(z, z, NT, preferred_element_type=jnp.float32)

    @pl.when(step == pl.num_programs(0) - 1)
    def _():
        real = acc_ref[:LANES, :LANES] + acc_ref[LANES:, LANES:]
        imag = acc_ref[LANES:, :LANES] - acc_ref[:LANES, LANES:]
        i = lax.broadcasted_iota(jnp.int32, real.shape, 0)
        j = lax.broadcasted_iota(jnp.int32, real.shape, 1)
        packed = jnp.where(i <= j, real, imag)
        if has_sum:
            packed = packed + sum_ref[...]
        gram_ref[...] = packed


def skewed(images, valid_mask, first, groups, total):
    count, columns = images.shape[2:]
    block = (ROWS, 2, count, LANES)

    def rows_out(n):
        return jax.ShapeDtypeStruct((groups, n, 2, count, LANES), jnp.bfloat16)

    def rows_spec(n):
        return pl.BlockSpec((1, n, 2, count, LANES), lambda s: (s, 0, 0, 0, 0))

    middle = ROWS - AFTER - BEFORE
    in_specs = [
        pl.BlockSpec(block, lambda s: (0, 0, 0, jnp.maximum(s + first - 1, 0))),
        pl.BlockSpec(block, lambda s: (0, 0, 0, s + first)),
        pl.BlockSpec((ROWS, LANES), lambda s: (0, jnp.maximum(s + first - 1, 0))),
        pl.BlockSpec((ROWS, LANES), lambda s: (0, s + first)),
    ]
    operands = [images, images, valid_mask, valid_mask]
    if total is not None:
        in_specs.append(pl.BlockSpec((LANES, LANES), lambda s: (0, 0)))
        operands.append(total)
    return pl.pallas_call(
        functools.partial(skew_kernel, first, columns, total is not None),
        grid=(groups,),
        in_specs=in_specs,
        out_specs=[
            rows_spec(AFTER),
            rows_spec(middle),
            rows_spec(BEFORE),
            pl.BlockSpec((LANES, LANES), lambda s: (0, 0)),
        ],
        out_shape=[
            rows_out(AFTER),
            rows_out(middle),
            rows_out(BEFORE),
            jax.ShapeDtypeStruct((LANES, LANES), jnp.float32),
        ],
        scratch_shapes=[
            pltpu.VMEM((2 * LANES, ROWS * LANES), jnp.bfloat16),
            pltpu.VMEM((2 * LANES, 2 * LANES), jnp.float32),
        ],
        compiler_params=pltpu.CompilerParams(vmem_limit_bytes=48 * 2**20),
        cost_estimate=pl.CostEstimate(
            flops=2 * groups * 256 * 256 * 1024, bytes_accessed=groups * 3 * ROWS * 2 * count * LANES * 2, transcendentals=0
        ),
        name="skew",
    )(*operands)


def looks_kernel(aliased, *refs):
    if aliased:
        before_ref, top_ref, mid_ref, low_ref, after_ref, _, out_ref, w_ref, m_ref = refs
    else:
        before_ref, top_ref, mid_ref, low_ref, after_ref, out_ref, w_ref, m_ref = refs
    count = top_ref.shape[3]

    @pl.when(pl.program_id(0) == 0)
    def _():
        w_ref[...] = jnp.zeros_like(w_ref)
        m_ref[...] = jnp.zeros_like(m_ref)

    rows = {}
    for r in range(ROWS):
        if r < AFTER:
            rows[r] = top_ref.at[0, r]
        elif r >= ROWS - BEFORE:
            rows[r] = low_ref.at[0, r - (ROWS - BEFORE)]
        else:
            rows[r] = mid_ref.at[0, r - AFTER]
    for r in range(BEFORE):
        rows[r - BEFORE] = before_ref.at[0, r]
    for r in range(AFTER):
        rows[ROWS + r] = after_ref.at[0, r]

    lane = lax.broadcasted_iota(jnp.int32, (1, LANES), 1)

    def lanes_of(turn):
        place = lane + (-LOOK * turn) % LANES
        place = jnp.where(place >= LANES, place - LANES, place)
        return place < LOOK

    def widened(which):
        return jnp.broadcast_to(which.astype(jnp.float32), (count, LANES)).astype(jnp.bfloat16) != 0

    single = [lanes_of(t) for t in range(2 * PER - 1)]
    wide = [widened(s) for s in single]
    zero = jnp.zeros((count, LANES), jnp.bfloat16)

    def turn(l, r):
        return l + SKEW[r % ROWS]

    def gathered(l, k, which):
        out = zero
        for r in which:
            out = jnp.where(wide[turn(l, r)], rows[r][k], out)
        return out

    def kept(l, value, which):
        select = single[turn(l, which[0])]
        for r in which[1:]:
            select = select | single[turn(l, r)]
        return jnp.where(widened(select), value, zero)

    i = lax.broadcasted_iota(jnp.int32, (count, LANES), 0)
    j = lax.broadcasted_iota(jnp.int32, (count, LANES), 1)
    eye = i == j

    def normalised(real, imag, w, l):
        power = jnp.sum(jnp.where(eye, real, 0.0), axis=0, keepdims=True)
        across = lax.rsqrt(jnp.maximum(power, floor_power))
        down = jnp.sum(jnp.where(eye, across, 0.0), axis=1, keepdims=True)
        out_ref[w, l, 0] = (real * down * across).astype(jnp.bfloat16)[:, :count]
        out_ref[w, l, 1] = (imag * down * across).astype(jnp.bfloat16)[:, :count]

    for l in range(PER):
        common = [gathered(l, k, (1, 2, 3, 4, 5)) for k in range(2)]
        for half in range(2):
            outer_rows = (-3, -2, -1, 0) if half == 0 else (6, 7, 8, 9)
            slot = (2 * l + half) % 2
            for k in range(2):
                outer = gathered(l, k, outer_rows)
                w_ref[slot, k, pl.ds(0, count), pl.ds(0, LANES)] = common[k]
                w_ref[slot, k, pl.ds(0, count), pl.ds(LANES, LANES)] = outer
                if half == 0:
                    pairs = ((kept(l, common[k], (1, 2, 3)), outer), (common[k], kept(l, outer, (-1, 0))))
                else:
                    pairs = ((common[k], kept(l, outer, (6, 7))), (kept(l, common[k], (3, 4, 5)), outer))
                for w, (inner, rest) in enumerate(pairs):
                    m_ref[slot, w, k, pl.ds(0, count), pl.ds(0, LANES)] = inner
                    m_ref[slot, w, k, pl.ds(0, count), pl.ds(LANES, LANES)] = rest
            gram = lax.dot_general(
                m_ref[slot].reshape(4 * LANES, 2 * LANES),
                w_ref[slot].reshape(2 * LANES, 2 * LANES),
                NT,
                preferred_element_type=jnp.float32,
            )
            for w in range(2):
                base = 2 * w * LANES
                re = gram[base : base + count]
                im = gram[base + LANES : base + LANES + count]
                real = re[:, :LANES] + im[:, LANES:]
                imag = im[:, :LANES] - re[:, LANES:]
                normalised(real, imag, 2 * half + w, l)


def looked(before, parts, after, first, looks, previous):
    top, mid, low = parts
    groups, _, _, count, _ = top.shape

    def spec(array):
        return pl.BlockSpec((1,) + array.shape[1:], lambda s: (s, 0, 0, 0, 0))

    operands = [before, top, mid, low, after]
    in_specs = [spec(a) for a in operands]
    aliases = {}
    if previous is not None:
        aliases = {len(operands): 0}
        operands.append(previous)
        in_specs.append(pl.BlockSpec(memory_space=pl.ANY))
    return pl.pallas_call(
        functools.partial(looks_kernel, previous is not None),
        grid=(groups,),
        in_specs=in_specs,
        out_specs=pl.BlockSpec((ROWS // 2, PER, 2, count, count), lambda s: (0, s + first, 0, 0, 0)),
        out_shape=jax.ShapeDtypeStruct((ROWS // 2, looks, 2, count, count), jnp.bfloat16),
        input_output_aliases=aliases,
        scratch_shapes=[
            pltpu.VMEM((2, 2, LANES, 2 * LANES), jnp.bfloat16),
            pltpu.VMEM((2, 2, 2, LANES, 2 * LANES), jnp.bfloat16),
        ],
        compiler_params=pltpu.CompilerParams(vmem_limit_bytes=48 * 2**20),
        cost_estimate=pl.CostEstimate(
            flops=2 * groups * PER * 2 * 512 * 256 * 256, bytes_accessed=groups * 2 * 10**6, transcendentals=0
        ),
        name="looks",
    )(*operands)


def slab_kernel(packed_ref, out_ref):
    packed = packed_ref[...]
    flipped = packed.T
    i = lax.broadcasted_iota(jnp.int32, packed.shape, 0)
    j = lax.broadcasted_iota(jnp.int32, packed.shape, 1)
    real = jnp.where(i <= j, packed, flipped)
    imag = jnp.where(i > j, packed, jnp.where(i < j, -flipped, 0.0))
    powers = jnp.where(i == j, packed, 0.0)
    scaled = jnp.sqrt(jnp.sum(powers, axis=1, keepdims=True) * jnp.sum(powers, axis=0, keepdims=True))
    count = out_ref.shape[1]
    out_ref[0] = (real / scaled)[:count, :count]
    out_ref[1] = (imag / scaled)[:count, :count]


def axis_sum(value, axis):
    size = lax.axis_size(axis)
    stride = 1
    while size > stride:
        left = size // stride
        if left % 2:
            return lax.psum(value, axis)
        radix = 4 if left % 4 == 0 else 2
        got = []
        for shift in range(1, radix):
            pairs = []
            for i in range(size):
                place = (i // stride) % radix
                pairs.append((i, i + ((place + shift) % radix - place) * stride))
            got.append(lax.ppermute(value, axis, pairs))
        if radix == 4:
            value = (value + got[1]) + (got[0] + got[2])
        else:
            value = value + got[0]
        stride *= radix
    return value


def shards(images, valid_mask):
    count, columns = images.shape[2:]
    looks = columns // LOOK
    groups = -(-looks // PER)
    cuts = [0, -(-groups // 2), groups]
    size = lax.axis_size("pix")
    forward = [(i, i + 1) for i in range(size - 1)]
    backward = [(i + 1, i) for i in range(size - 1)]
    pieces = []
    total = None
    for start, stop in zip(cuts[:-1], cuts[1:]):
        top, mid, low, total = skewed(images, valid_mask, start, stop - start, total)
        before = lax.ppermute(low, "pix", forward)
        after = lax.ppermute(top, "pix", backward)
        pieces.append((start, (top, mid, low), before, after))
    total = axis_sum(total, "pix")
    slab_coherence = pl.pallas_call(
        slab_kernel, out_shape=jax.ShapeDtypeStruct((2, count, count), jnp.float32), name="slab"
    )(total)
    out = None
    for start, parts, before, after in pieces:
        out = looked(before, parts, after, start, looks, out)
    return (out, slab_coherence)


def solution(mesh):
    in_specs = (P(("group", "pix"), None, None, None), P(("group", "pix"), None))
    out_specs = (P(("group", "pix"), None, None, None, None), P("group", None, None))
    return jax.shard_map(shards, mesh=mesh, in_specs=in_specs, out_specs=out_specs, check_vma=False)
```

```python
import functools
import jax
import jax.numpy as jnp
from jax import lax
from jax.experimental import pallas as pl
from jax.experimental.pallas import tpu as pltpu
from jax.sharding import PartitionSpec as P

floor_power = 30.0

LOOK = 21
LANES = 128
PER = LANES // LOOK
SPAN = PER * LOOK
ROWS = 8
SKEW = (5, 0, 1, 2, 3, 4, 1, 2)
BEFORE, AFTER = 3, 2
NT = (((1,), (1,)), ((), ()))


def turned(image, mask, skew, columns, put):
    count = image[0].shape[0]
    zero = jnp.zeros((count, LANES), jnp.bfloat16)
    lane = lax.broadcasted_iota(jnp.int32, (1, LANES), 1)

    def tile(value, g):
        start, stop = g * LANES, min((g + 1) * LANES, columns)
        part = value[:, start:stop]
        if stop - start < LANES:
            rest = jnp.zeros((part.shape[0], LANES - (stop - start)), part.dtype)
            part = jnp.concatenate([part, rest], axis=1)
        return part

    def widened(which):
        return jnp.broadcast_to(which.astype(jnp.float32), (count, LANES)).astype(jnp.bfloat16) != 0

    tiles = -(-columns // LANES)
    for g in range(-(-columns // SPAN)):
        slide = (LANES - SPAN) * g
        place = (lane + slide) % LANES
        used = (place < SPAN) & (SPAN * g + place < columns)
        prior = lane >= LANES - slide
        sides = [t for t in (g - 1, g) if 0 <= t < tiles]

        def joined(value):
            parts = [tile(value, t) for t in sides]
            if len(parts) == 1:
                return parts[0]
            which = prior if value.shape[0] == 1 else widened(prior)
            return jnp.where(which, parts[0], parts[1])

        keep = widened(used & (joined(mask) != 0))
        for k in range(2):
            row = jnp.where(keep, joined(image[k]), zero)
            put(g, k, pltpu.roll(row, slide + LOOK * skew, 1))


def pick(table, step):
    value = table[0]
    for i, entry in enumerate(table[1:]):
        value = jnp.where(step > i, entry, value)
    return value


def edge_kernel(cuts, image_ref, mask_ref, *outs):
    step = pl.program_id(0)
    low_refs, top_refs = outs[: len(cuts) - 1], outs[len(cuts) - 1 :]
    row = lax.rem(step + ROWS - BEFORE, ROWS)
    mask = mask_ref[pl.ds(row, 1), :]
    skew = pick(SKEW[ROWS - BEFORE :] + SKEW[:AFTER], step)

    def work(refs):
        def put(g, k, value):
            c = max(i for i in range(len(cuts) - 1) if cuts[i] <= g)
            refs[c][g - cuts[c], 0, k] = value

        turned([image_ref.at[0, 0], image_ref.at[0, 1]], mask, skew, mask.shape[1], put)

    @pl.when(step < BEFORE)
    def _():
        work(low_refs)

    @pl.when(step >= BEFORE)
    def _():
        work(top_refs)


def edges(images, valid_mask, cuts):
    count, columns = images.shape[2:]
    sizes = [b - a for a, b in zip(cuts[:-1], cuts[1:])]

    def shape(n, rows):
        return jax.ShapeDtypeStruct((n, rows, 2, count, LANES), jnp.bfloat16)

    def spec(n, index):
        return pl.BlockSpec((n, 1, 2, count, LANES), lambda s: (0, index(s), 0, 0, 0))

    outs = pl.pallas_call(
        functools.partial(edge_kernel, cuts),
        grid=(BEFORE + AFTER,),
        in_specs=[
            pl.BlockSpec((1, 2, count, columns), lambda s: (lax.rem(s + ROWS - BEFORE, ROWS), 0, 0, 0)),
            pl.BlockSpec((ROWS, columns), lambda s: (0, 0)),
        ],
        out_specs=[spec(n, lambda s: jnp.minimum(s, BEFORE - 1)) for n in sizes]
        + [spec(n, lambda s: jnp.maximum(s - BEFORE, 0)) for n in sizes],
        out_shape=[shape(n, BEFORE) for n in sizes] + [shape(n, AFTER) for n in sizes],
        cost_estimate=pl.CostEstimate(flops=10**6, bytes_accessed=4 * 10**6, transcendentals=0),
        name="edges",
    )(images, valid_mask)
    return outs[: len(sizes)], outs[len(sizes) :]


def middle_kernel(cuts, image_ref, mask_ref, *refs):
    step = pl.program_id(0)
    pieces = len(cuts) - 1
    low_refs, top_refs = refs[:pieces], refs[pieces : 2 * pieces]
    mid_ref, gram_ref, z_ref, acc_ref = refs[2 * pieces :]
    groups = cuts[-1]
    count = image_ref.shape[2]

    @pl.when(step == 0)
    def _():
        z_ref[...] = jnp.zeros_like(z_ref)
        acc_ref[...] = jnp.zeros_like(acc_ref)

    row = step + AFTER
    mask = mask_ref[pl.ds(row, 1), :]

    def place(at, g, k, value):
        z_ref[pl.ds(k * LANES, count), pl.ds((at * groups + g) * LANES, LANES)] = value

    def put(g, k, value):
        mid_ref[g, 0, k] = value
        place(0, g, k, value)

    turned([image_ref.at[0, 0], image_ref.at[0, 1]], mask, pick(SKEW[AFTER : ROWS - BEFORE], step), mask.shape[1], put)
    for c in range(pieces):
        for g in range(cuts[c], cuts[c + 1]):
            for k in range(2):
                place(1, g, k, low_refs[c][g - cuts[c], 0, k])
                place(2, g, k, top_refs[c][g - cuts[c], 0, k])

    def add(rows):
        z = z_ref[:, : rows * groups * LANES]
        acc_ref[...] += lax.dot_general(z, z, NT, preferred_element_type=jnp.float32)

    @pl.when(step < AFTER)
    def _():
        add(3)

    @pl.when(step >= AFTER)
    def _():
        add(2)

    @pl.when(step == pl.num_programs(0) - 1)
    def _():
        real = acc_ref[:LANES, :LANES] + acc_ref[LANES:, LANES:]
        imag = acc_ref[LANES:, :LANES] - acc_ref[:LANES, LANES:]
        i = lax.broadcasted_iota(jnp.int32, real.shape, 0)
        j = lax.broadcasted_iota(jnp.int32, real.shape, 1)
        gram_ref[...] = jnp.where(i <= j, real, imag)


def middle(images, valid_mask, lows, tops, cuts):
    count, columns = images.shape[2:]
    groups = cuts[-1]
    rows = ROWS - AFTER - BEFORE

    def spec(array, last):
        return pl.BlockSpec((array.shape[0], 1, 2, count, LANES), lambda s: (0, jnp.minimum(s, last), 0, 0, 0))

    return pl.pallas_call(
        functools.partial(middle_kernel, cuts),
        grid=(rows,),
        in_specs=[
            pl.BlockSpec((1, 2, count, columns), lambda s: (s + AFTER, 0, 0, 0)),
            pl.BlockSpec((ROWS, columns), lambda s: (0, 0)),
        ]
        + [spec(a, BEFORE - 1) for a in lows]
        + [spec(a, AFTER - 1) for a in tops],
        out_specs=[
            pl.BlockSpec((groups, 1, 2, count, LANES), lambda s: (0, s, 0, 0, 0)),
            pl.BlockSpec((LANES, LANES), lambda s: (0, 0)),
        ],
        out_shape=[
            jax.ShapeDtypeStruct((groups, rows, 2, count, LANES), jnp.bfloat16),
            jax.ShapeDtypeStruct((LANES, LANES), jnp.float32),
        ],
        scratch_shapes=[
            pltpu.VMEM((2 * LANES, 3 * groups * LANES), jnp.bfloat16),
            pltpu.VMEM((2 * LANES, 2 * LANES), jnp.float32),
        ],
        cost_estimate=pl.CostEstimate(flops=10**9, bytes_accessed=5 * 10**6, transcendentals=0),
        name="middle",
    )(images, valid_mask, *lows, *tops)


def looks_kernel(aliased, *refs):
    if aliased:
        before_ref, top_ref, mid_ref, low_ref, after_ref, _, out_ref, w_ref, m_ref = refs
    else:
        before_ref, top_ref, mid_ref, low_ref, after_ref, out_ref, w_ref, m_ref = refs
    count = top_ref.shape[3]

    @pl.when(pl.program_id(0) == 0)
    def _():
        w_ref[...] = jnp.zeros_like(w_ref)
        m_ref[...] = jnp.zeros_like(m_ref)

    rows = {}
    for r in range(ROWS):
        if r < AFTER:
            rows[r] = top_ref.at[0, r]
        elif r >= ROWS - BEFORE:
            rows[r] = low_ref.at[0, r - (ROWS - BEFORE)]
        else:
            rows[r] = mid_ref.at[0, r - AFTER]
    for r in range(BEFORE):
        rows[r - BEFORE] = before_ref.at[0, r]
    for r in range(AFTER):
        rows[ROWS + r] = after_ref.at[0, r]

    lane = lax.broadcasted_iota(jnp.int32, (1, LANES), 1)

    def lanes_of(turn):
        place = lane + (-LOOK * turn) % LANES
        place = jnp.where(place >= LANES, place - LANES, place)
        return place < LOOK

    def widened(which):
        return jnp.broadcast_to(which.astype(jnp.float32), (count, LANES)).astype(jnp.bfloat16) != 0

    single = [lanes_of(t) for t in range(2 * PER - 1)]
    wide = [widened(s) for s in single]
    zero = jnp.zeros((count, LANES), jnp.bfloat16)

    def turn(l, r):
        return l + SKEW[r % ROWS]

    def gathered(l, k, which):
        out = zero
        for r in which:
            out = jnp.where(wide[turn(l, r)], rows[r][k], out)
        return out

    def kept(l, value, which):
        select = single[turn(l, which[0])]
        for r in which[1:]:
            select = select | single[turn(l, r)]
        return jnp.where(widened(select), value, zero)

    i = lax.broadcasted_iota(jnp.int32, (count, LANES), 0)
    j = lax.broadcasted_iota(jnp.int32, (count, LANES), 1)
    eye = i == j

    def normalised(real, imag, w, l):
        power = jnp.sum(jnp.where(eye, real, 0.0), axis=0, keepdims=True)
        across = lax.rsqrt(jnp.maximum(power, floor_power))
        down = jnp.sum(jnp.where(eye, across, 0.0), axis=1, keepdims=True)
        out_ref[w, l, 0] = (real * down * across).astype(jnp.bfloat16)[:, :count]
        out_ref[w, l, 1] = (imag * down * across).astype(jnp.bfloat16)[:, :count]

    for l in range(PER):
        common = [gathered(l, k, (1, 2, 3, 4, 5)) for k in range(2)]
        for half in range(2):
            outer_rows = (-3, -2, -1, 0) if half == 0 else (6, 7, 8, 9)
            slot = (2 * l + half) % 2
            for k in range(2):
                outer = gathered(l, k, outer_rows)
                w_ref[slot, k, pl.ds(0, count), pl.ds(0, LANES)] = common[k]
                w_ref[slot, k, pl.ds(0, count), pl.ds(LANES, LANES)] = outer
                if half == 0:
                    pairs = ((kept(l, common[k], (1, 2, 3)), outer), (common[k], kept(l, outer, (-1, 0))))
                else:
                    pairs = ((common[k], kept(l, outer, (6, 7))), (kept(l, common[k], (3, 4, 5)), outer))
                for w, (inner, rest) in enumerate(pairs):
                    m_ref[slot, w, k, pl.ds(0, count), pl.ds(0, LANES)] = inner
                    m_ref[slot, w, k, pl.ds(0, count), pl.ds(LANES, LANES)] = rest
            gram = lax.dot_general(
                m_ref[slot].reshape(4 * LANES, 2 * LANES),
                w_ref[slot].reshape(2 * LANES, 2 * LANES),
                NT,
                preferred_element_type=jnp.float32,
            )
            for w in range(2):
                base = 2 * w * LANES
                re = gram[base : base + count]
                im = gram[base + LANES : base + LANES + count]
                real = re[:, :LANES] + im[:, LANES:]
                imag = im[:, :LANES] - re[:, LANES:]
                normalised(real, imag, 2 * half + w, l)


def looked(before, parts, after, first, looks, previous):
    top, mid, low = parts
    groups, _, _, count, _ = top.shape

    def spec(array, offset):
        return pl.BlockSpec((1,) + array.shape[1:], lambda s: (s + offset, 0, 0, 0, 0))

    operands = [before, top, mid, low, after]
    in_specs = [spec(a, first if a is mid else 0) for a in operands]
    aliases = {}
    if previous is not None:
        aliases = {len(operands): 0}
        operands.append(previous)
        in_specs.append(pl.BlockSpec(memory_space=pl.ANY))
    return pl.pallas_call(
        functools.partial(looks_kernel, previous is not None),
        grid=(groups,),
        in_specs=in_specs,
        out_specs=pl.BlockSpec((ROWS // 2, PER, 2, count, count), lambda s: (0, s + first, 0, 0, 0)),
        out_shape=jax.ShapeDtypeStruct((ROWS // 2, looks, 2, count, count), jnp.bfloat16),
        input_output_aliases=aliases,
        scratch_shapes=[
            pltpu.VMEM((2, 2, LANES, 2 * LANES), jnp.bfloat16),
            pltpu.VMEM((2, 2, 2, LANES, 2 * LANES), jnp.bfloat16),
        ],
        cost_estimate=pl.CostEstimate(
            flops=2 * groups * PER * 2 * 512 * 256 * 256, bytes_accessed=groups * 2 * 10**6, transcendentals=0
        ),
        name="looks",
    )(*operands)


def slab_kernel(packed_ref, out_ref):
    packed = packed_ref[...]
    flipped = packed.T
    i = lax.broadcasted_iota(jnp.int32, packed.shape, 0)
    j = lax.broadcasted_iota(jnp.int32, packed.shape, 1)
    real = jnp.where(i <= j, packed, flipped)
    imag = jnp.where(i > j, packed, jnp.where(i < j, -flipped, 0.0))
    powers = jnp.where(i == j, packed, 0.0)
    scaled = jnp.sqrt(jnp.sum(powers, axis=1, keepdims=True) * jnp.sum(powers, axis=0, keepdims=True))
    count = out_ref.shape[1]
    out_ref[0] = (real / scaled)[:count, :count]
    out_ref[1] = (imag / scaled)[:count, :count]


def axis_sum(value, axis):
    size = lax.axis_size(axis)
    rows, columns = value.shape
    if rows % size:
        return lax.psum(value, axis)
    parts = lax.all_to_all(value.reshape(size, rows // size, columns), axis, 0, 0)
    mine = jnp.sum(parts, axis=0, keepdims=True)
    return lax.all_to_all(jnp.broadcast_to(mine, parts.shape), axis, 0, 0).reshape(rows, columns)


def shards(images, valid_mask):
    count, columns = images.shape[2:]
    looks = columns // LOOK
    groups = -(-looks // PER)
    cuts = (0, -(-groups // 2), groups)
    size = lax.axis_size("pix")
    forward = [(i, i + 1) for i in range(size - 1)]
    backward = [(i + 1, i) for i in range(size - 1)]
    lows, tops = edges(images, valid_mask, cuts)
    befores, afters = [], []
    for low, top in zip(lows, tops):
        befores.append(lax.ppermute(low, "pix", forward))
        afters.append(lax.ppermute(top, "pix", backward))
    mid, total = middle(images, valid_mask, lows, tops, cuts)
    total = axis_sum(total, "pix")
    slab_coherence = pl.pallas_call(
        slab_kernel, out_shape=jax.ShapeDtypeStruct((2, count, count), jnp.float32), name="slab"
    )(total)
    out = None
    for c, start in enumerate(cuts[:-1]):
        out = looked(befores[c], (tops[c], mid, lows[c]), afters[c], start, looks, out)
    return (out, slab_coherence)


def solution(mesh):
    in_specs = (P(("group", "pix"), None, None, None), P(("group", "pix"), None))
    out_specs = (P(("group", "pix"), None, None, None, None), P("group", None, None))
    return jax.shard_map(shards, mesh=mesh, in_specs=in_specs, out_specs=out_specs, check_vma=False)
```

```python
import functools
import jax
import jax.numpy as jnp
from jax import lax
from jax.experimental import pallas as pl
from jax.experimental.pallas import tpu as pltpu
from jax.sharding import PartitionSpec as P

floor_power = 30.0

LOOK = 21
LANES = 128
PER = LANES // LOOK
SPAN = PER * LOOK
ROWS = 8
SKEW = (5, 0, 1, 2, 3, 4, 1, 2)
BEFORE, AFTER = 3, 2
NT = (((1,), (1,)), ((), ()))


def turned(image, mask, skew, columns, put):
    count = image[0].shape[0]
    zero = jnp.zeros((count, LANES), jnp.bfloat16)
    lane = lax.broadcasted_iota(jnp.int32, (1, LANES), 1)

    def tile(value, g):
        start, stop = g * LANES, min((g + 1) * LANES, columns)
        part = value[:, start:stop]
        if stop - start < LANES:
            rest = jnp.zeros((part.shape[0], LANES - (stop - start)), part.dtype)
            part = jnp.concatenate([part, rest], axis=1)
        return part

    def widened(which):
        return jnp.broadcast_to(which.astype(jnp.float32), (count, LANES)).astype(jnp.bfloat16) != 0

    tiles = -(-columns // LANES)
    for g in range(-(-columns // SPAN)):
        slide = (LANES - SPAN) * g
        place = (lane + slide) % LANES
        used = (place < SPAN) & (SPAN * g + place < columns)
        prior = lane >= LANES - slide
        sides = [t for t in (g - 1, g) if 0 <= t < tiles]

        def joined(value):
            parts = [tile(value, t) for t in sides]
            if len(parts) == 1:
                return parts[0]
            which = prior if value.shape[0] == 1 else widened(prior)
            return jnp.where(which, parts[0], parts[1])

        keep = widened(used & (joined(mask) != 0))
        for k in range(2):
            row = jnp.where(keep, joined(image[k]), zero)
            put(g, k, pltpu.roll(row, slide + LOOK * skew, 1))


def edge_kernel(image_ref, mask_ref, top_ref, low_ref, rows_ref, top_out, low_out, in_sems, out_sems):
    order = [(r, top_out, top_ref, r) for r in range(AFTER)]
    order += [(ROWS - BEFORE + r, low_out, low_ref, r) for r in range(BEFORE)]
    fetches = []
    for at, (row, _, _, _) in enumerate(order):
        fetch = pltpu.make_async_copy(image_ref.at[row], rows_ref.at[at], in_sems.at[at])
        fetch.start()
        fetches.append(fetch)
    stores = []
    for at, (row, out, target, i) in enumerate(order):
        fetches[at].wait()

        def put(g, k, value):
            out[i, g, k] = value

        rows = [rows_ref.at[at, 0], rows_ref.at[at, 1]]
        turned(rows, mask_ref[row : row + 1, :], SKEW[row], mask_ref.shape[1], put)
        store = pltpu.make_async_copy(out.at[i], target.at[i], out_sems.at[at])
        store.start()
        stores.append(store)
    for store in stores:
        store.wait()


def edges(images, valid_mask, groups):
    count, columns = images.shape[2:]

    def shape(rows):
        return (rows, groups, 2, count, LANES)

    return pl.pallas_call(
        edge_kernel,
        in_specs=[pl.BlockSpec(memory_space=pl.ANY), pl.BlockSpec(memory_space=pltpu.VMEM)],
        out_specs=[pl.BlockSpec(memory_space=pl.ANY)] * 2,
        out_shape=[jax.ShapeDtypeStruct(shape(rows), jnp.bfloat16) for rows in (AFTER, BEFORE)],
        scratch_shapes=[
            pltpu.VMEM((BEFORE + AFTER, 2, count, columns), jnp.bfloat16),
            pltpu.VMEM(shape(AFTER), jnp.bfloat16),
            pltpu.VMEM(shape(BEFORE), jnp.bfloat16),
            pltpu.SemaphoreType.DMA((BEFORE + AFTER,)),
            pltpu.SemaphoreType.DMA((BEFORE + AFTER,)),
        ],
        cost_estimate=pl.CostEstimate(flops=10**6, bytes_accessed=4 * 10**6, transcendentals=0),
        name="edges",
    )(images, valid_mask)


def middle_kernel(image_ref, mask_ref, top_ref, low_ref, mid_ref, gram_ref, rows_ref, z_ref, in_sems):
    count = image_ref.shape[2]
    groups = low_ref.shape[1]
    middle_rows = ROWS - BEFORE - AFTER
    fetches = []
    for at in range(middle_rows):
        fetch = pltpu.make_async_copy(image_ref.at[AFTER + at], rows_ref.at[at], in_sems.at[at])
        fetch.start()
        fetches.append(fetch)
    z_ref[...] = jnp.zeros_like(z_ref)

    def place(at, g, k, value):
        z_ref[at, pl.ds(k * LANES, count), pl.ds(g * LANES, LANES)] = value

    for i in range(AFTER):
        for g in range(groups):
            for k in range(2):
                place(i, g, k, top_ref[i, g, k])
    for i in range(BEFORE):
        for g in range(groups):
            for k in range(2):
                place(AFTER + i, g, k, low_ref[i, g, k])
    for at in range(middle_rows):
        row = AFTER + at
        fetches[at].wait()

        def put(g, k, value):
            mid_ref[at, g, k] = value
            place(AFTER + BEFORE + at, g, k, value)

        turned([rows_ref.at[at, 0], rows_ref.at[at, 1]], mask_ref[row : row + 1, :], SKEW[row], mask_ref.shape[1], put)
    total = None
    for r in range(ROWS):
        z = z_ref[r]
        part = lax.dot_general(z, z, NT, preferred_element_type=jnp.float32)
        total = part if total is None else total + part
    real = total[:LANES, :LANES] + total[LANES:, LANES:]
    imag = total[LANES:, :LANES] - total[:LANES, LANES:]
    i = lax.broadcasted_iota(jnp.int32, real.shape, 0)
    j = lax.broadcasted_iota(jnp.int32, real.shape, 1)
    gram_ref[...] = jnp.where(i <= j, real, imag)


def middle(images, valid_mask, top, low):
    count, columns = images.shape[2:]
    groups = low.shape[1]
    rows = ROWS - AFTER - BEFORE
    vmem = pl.BlockSpec(memory_space=pltpu.VMEM)
    return pl.pallas_call(
        middle_kernel,
        in_specs=[pl.BlockSpec(memory_space=pl.ANY), vmem, vmem, vmem],
        out_specs=[vmem, vmem],
        out_shape=[
            jax.ShapeDtypeStruct((rows, groups, 2, count, LANES), jnp.bfloat16),
            jax.ShapeDtypeStruct((LANES, LANES), jnp.float32),
        ],
        scratch_shapes=[
            pltpu.VMEM((rows, 2, count, columns), jnp.bfloat16),
            pltpu.VMEM((ROWS, 2 * LANES, groups * LANES), jnp.bfloat16),
            pltpu.SemaphoreType.DMA((rows,)),
        ],
        cost_estimate=pl.CostEstimate(flops=10**9, bytes_accessed=5 * 10**6, transcendentals=0),
        name="middle",
    )(images, valid_mask, top, low)


def added(terms):
    if len(terms) == 4:
        return (terms[0] + terms[2]) + (terms[1] + terms[3])
    return functools.reduce(jnp.add, terms)


def slab_values(terms):
    packed = added(terms)
    flipped = packed.T
    i = lax.broadcasted_iota(jnp.int32, packed.shape, 0)
    j = lax.broadcasted_iota(jnp.int32, packed.shape, 1)
    real = jnp.where(i <= j, packed, flipped)
    imag = jnp.where(i > j, packed, jnp.where(i < j, -flipped, 0.0))
    powers = jnp.where(i == j, packed, 0.0)
    scaled = jnp.sqrt(jnp.sum(powers, axis=1, keepdims=True) * jnp.sum(powers, axis=0, keepdims=True))
    return real / scaled, imag / scaled


INNER = (1, 2, 3, 4, 5)
HALVES = (
    ((-3, -2, -1, 0), (((1, 2, 3), None), (None, (-1, 0)))),
    ((6, 7, 8, 9), ((None, (6, 7)), ((3, 4, 5), None))),
)


def looks_kernel(half, aliased, terms, *refs):
    other_ref, top_ref, mid_ref, low_ref = refs[:4]
    refs = refs[4 + aliased :]
    term_refs, refs = refs[:terms], refs[terms:]
    if terms:
        out_ref, slab_ref, w_ref, m_ref = refs
    else:
        out_ref, w_ref, m_ref = refs
    count = top_ref.shape[3]

    @pl.when(pl.program_id(0) == 0)
    def _():
        w_ref[...] = jnp.zeros_like(w_ref)
        m_ref[...] = jnp.zeros_like(m_ref)
        if terms:
            real, imag = slab_values([t[...] for t in term_refs])
            slab_ref[0] = real[:count, :count]
            slab_ref[1] = imag[:count, :count]

    rows = {}
    for r in range(ROWS):
        if r < AFTER:
            rows[r] = top_ref.at[r, 0]
        elif r >= ROWS - BEFORE:
            rows[r] = low_ref.at[r - (ROWS - BEFORE), 0]
        else:
            rows[r] = mid_ref.at[r - AFTER, 0]
    for r in range(other_ref.shape[0]):
        rows[ROWS + r if half else r - BEFORE] = other_ref.at[r, 0]

    lane = lax.broadcasted_iota(jnp.int32, (1, LANES), 1)

    def lanes_of(turn):
        place = lane + (-LOOK * turn) % LANES
        place = jnp.where(place >= LANES, place - LANES, place)
        return place < LOOK

    def widened(which):
        return jnp.broadcast_to(which.astype(jnp.float32), (count, LANES)).astype(jnp.bfloat16) != 0

    single = [lanes_of(t) for t in range(2 * PER - 1)]
    wide = [widened(s) for s in single]
    zero = jnp.zeros((count, LANES), jnp.bfloat16)

    def turn(l, r):
        return l + SKEW[r % ROWS]

    def gathered(l, k, which):
        out = zero
        for r in which:
            out = jnp.where(wide[turn(l, r)], rows[r][k], out)
        return out

    def kept(l, value, which):
        if which is None:
            return value
        select = single[turn(l, which[0])]
        for r in which[1:]:
            select = select | single[turn(l, r)]
        return jnp.where(widened(select), value, zero)

    i = lax.broadcasted_iota(jnp.int32, (count, LANES), 0)
    j = lax.broadcasted_iota(jnp.int32, (count, LANES), 1)
    eye = i == j

    def normalised(real, imag, w, l):
        power = jnp.sum(jnp.where(eye, real, 0.0), axis=0, keepdims=True)
        across = lax.rsqrt(jnp.maximum(power, floor_power))
        down = jnp.sum(jnp.where(eye, across, 0.0), axis=1, keepdims=True)
        out_ref[w, l, 0] = (real * down * across).astype(jnp.bfloat16)[:, :count]
        out_ref[w, l, 1] = (imag * down * across).astype(jnp.bfloat16)[:, :count]

    outer_rows, windows = HALVES[half]
    for l in range(PER):
        slot = l % 2
        for k in range(2):
            inner = gathered(l, k, INNER)
            outer = gathered(l, k, outer_rows)
            w_ref[slot, k, pl.ds(0, count), pl.ds(0, LANES)] = inner
            w_ref[slot, k, pl.ds(0, count), pl.ds(LANES, LANES)] = outer
            for w, (inner_rows, rest_rows) in enumerate(windows):
                m_ref[slot, w, k, pl.ds(0, count), pl.ds(0, LANES)] = kept(l, inner, inner_rows)
                m_ref[slot, w, k, pl.ds(0, count), pl.ds(LANES, LANES)] = kept(l, outer, rest_rows)
        gram = lax.dot_general(
            m_ref[slot].reshape(4 * LANES, 2 * LANES),
            w_ref[slot].reshape(2 * LANES, 2 * LANES),
            NT,
            preferred_element_type=jnp.float32,
        )
        for w in range(2):
            base = 2 * w * LANES
            re = gram[base : base + count]
            im = gram[base + LANES : base + LANES + count]
            normalised(re[:, :LANES] + im[:, LANES:], im[:, :LANES] - re[:, LANES:], w, l)


def looked(half, other, top, mid, low, looks, previous, terms):
    groups, _, count, _ = top.shape[1:]

    def spec(array):
        return pl.BlockSpec((array.shape[0], 1) + array.shape[2:], lambda s: (0, s, 0, 0, 0))

    operands = [other, top, mid, low]
    in_specs = [spec(a) for a in operands]
    aliases = {}
    if previous is not None:
        aliases = {len(operands): 0}
        operands.append(previous)
        in_specs.append(pl.BlockSpec(memory_space=pl.ANY))
    for term in terms:
        operands.append(term)
        in_specs.append(pl.BlockSpec(term.shape, lambda s: (0, 0)))
    out_specs = [pl.BlockSpec((2, PER, 2, count, count), lambda s: (half, s, 0, 0, 0))]
    out_shape = [jax.ShapeDtypeStruct((ROWS // 2, looks, 2, count, count), jnp.bfloat16)]
    if terms:
        out_specs.append(pl.BlockSpec((2, count, count), lambda s: (0, 0, 0)))
        out_shape.append(jax.ShapeDtypeStruct((2, count, count), jnp.float32))
    return pl.pallas_call(
        functools.partial(looks_kernel, half, previous is not None, len(terms)),
        grid=(groups,),
        in_specs=in_specs,
        out_specs=out_specs,
        out_shape=out_shape,
        input_output_aliases=aliases,
        scratch_shapes=[
            pltpu.VMEM((2, 2, LANES, 2 * LANES), jnp.bfloat16),
            pltpu.VMEM((2, 2, 2, LANES, 2 * LANES), jnp.bfloat16),
        ],
        compiler_params=pltpu.CompilerParams(vmem_limit_bytes=32 * 2**20),
        cost_estimate=pl.CostEstimate(
            flops=groups * PER * 2 * 512 * 256 * 256, bytes_accessed=groups * 10**6, transcendentals=0
        ),
        name="looks",
    )(*operands)


def axis_terms(value, axis):
    size = lax.axis_size(axis)
    stride = 1
    terms = [value]
    while size > stride:
        left = size // stride
        if left % 2:
            return [lax.psum(value, axis)]
        radix = 4 if left % 4 == 0 else 2
        part = added(terms)
        terms = [part]
        for shift in range(1, radix):
            pairs = []
            for i in range(size):
                place = (i // stride) % radix
                pairs.append((i, i + ((place + shift) % radix - place) * stride))
            terms.append(lax.ppermute(part, axis, pairs))
        stride *= radix
    return terms


def shards(images, valid_mask):
    looks = images.shape[3] // LOOK
    groups = -(-looks // PER)
    size = lax.axis_size("pix")
    top, low = edges(images, valid_mask, groups)
    after = lax.ppermute(top, "pix", [(i + 1, i) for i in range(size - 1)])
    before = lax.ppermute(low, "pix", [(i, i + 1) for i in range(size - 1)])
    mid, total = middle(images, valid_mask, top, low)
    terms = axis_terms(total, "pix")
    (out,) = looked(1, after, top, mid, low, looks, None, [])
    out, slab = looked(0, before, top, mid, low, looks, out, terms)
    return (out, slab)


def solution(mesh):
    in_specs = (P(("group", "pix"), None, None, None), P(("group", "pix"), None))
    out_specs = (P(("group", "pix"), None, None, None, None), P("group", None, None))
    return jax.shard_map(shards, mesh=mesh, in_specs=in_specs, out_specs=out_specs, check_vma=False)
```

```python
import functools
import jax
import jax.numpy as jnp
from jax import lax
from jax.experimental import pallas as pl
from jax.experimental.pallas import tpu as pltpu
from jax.sharding import PartitionSpec as P

floor_power = 30.0

LOOK = 21
LANES = 128
PER = LANES // LOOK
SPAN = PER * LOOK
ROWS = 8
SKEW = (5, 0, 1, 2, 3, 4, 1, 2)
BEFORE, AFTER = 3, 2
NT = (((1,), (1,)), ((), ()))


def turned(image, mask, skew, columns, put):
    count = image[0].shape[0]
    zero = jnp.zeros((count, LANES), jnp.bfloat16)
    lane = lax.broadcasted_iota(jnp.int32, (1, LANES), 1)

    def tile(value, g):
        start, stop = g * LANES, min((g + 1) * LANES, columns)
        part = value[:, start:stop]
        if stop - start < LANES:
            rest = jnp.zeros((part.shape[0], LANES - (stop - start)), part.dtype)
            part = jnp.concatenate([part, rest], axis=1)
        return part

    def widened(which):
        return jnp.broadcast_to(which.astype(jnp.float32), (count, LANES)).astype(jnp.bfloat16) != 0

    tiles = -(-columns // LANES)
    for g in range(-(-columns // SPAN)):
        slide = (LANES - SPAN) * g
        place = (lane + slide) % LANES
        used = (place < SPAN) & (SPAN * g + place < columns)
        prior = lane >= LANES - slide
        sides = [t for t in (g - 1, g) if 0 <= t < tiles]

        def joined(value):
            parts = [tile(value, t) for t in sides]
            if len(parts) == 1:
                return parts[0]
            which = prior if value.shape[0] == 1 else widened(prior)
            return jnp.where(which, parts[0], parts[1])

        keep = widened(used & (joined(mask) != 0))
        for k in range(2):
            row = jnp.where(keep, joined(image[k]), zero)
            put(g, k, pltpu.roll(row, slide + LOOK * skew, 1))


def edge_kernel(image_ref, mask_ref, top_ref, rows_ref, sems):
    fetches = []
    for r in range(AFTER):
        fetches.append(pltpu.make_async_copy(image_ref.at[r], rows_ref.at[r], sems.at[r]))
        fetches[r].start()
    for r in range(AFTER):
        fetches[r].wait()

        def put(g, k, value):
            top_ref[r, g, k] = value

        turned([rows_ref.at[r, 0], rows_ref.at[r, 1]], mask_ref[r : r + 1, :], SKEW[r], mask_ref.shape[1], put)


def edge(images, valid_mask, groups):
    count, columns = images.shape[2:]
    vmem = pl.BlockSpec(memory_space=pltpu.VMEM)
    return pl.pallas_call(
        edge_kernel,
        in_specs=[pl.BlockSpec(memory_space=pltpu.HBM), vmem],
        out_specs=vmem,
        out_shape=jax.ShapeDtypeStruct((AFTER, groups, 2, count, LANES), jnp.bfloat16),
        scratch_shapes=[
            pltpu.VMEM((AFTER, 2, count, columns), jnp.bfloat16),
            pltpu.SemaphoreType.DMA((AFTER,)),
        ],
        compiler_params=pltpu.CompilerParams(vmem_limit_bytes=61 * 2**20),
        cost_estimate=pl.CostEstimate(flops=10**6, bytes_accessed=2 * 10**6, transcendentals=0),
        name="edge",
    )(images, valid_mask)


def rest_kernel(cut, image_ref, mask_ref, top_ref, mid_ref, low0_ref, low1_ref, gram_ref, rows_ref, z_ref, sems):
    count = image_ref.shape[2]
    groups = top_ref.shape[1]
    order = list(range(ROWS - BEFORE, ROWS)) + list(range(AFTER, ROWS - BEFORE))
    fetches = []
    for at, row in enumerate(order):
        fetches.append(pltpu.make_async_copy(image_ref.at[row], rows_ref.at[at], sems.at[at]))
        fetches[at].start()
    z_ref[...] = jnp.zeros_like(z_ref)

    def place(row, g, k, value):
        z_ref[row, pl.ds(k * LANES, count), pl.ds(g * LANES, LANES)] = value

    for r in range(AFTER):
        for g in range(groups):
            for k in range(2):
                place(r, g, k, top_ref[r, g, k])
    for at, row in enumerate(order):
        fetches[at].wait()

        def put(g, k, value):
            if row < ROWS - BEFORE:
                mid_ref[row - AFTER, g, k] = value
            elif g < cut:
                low0_ref[row - (ROWS - BEFORE), g, k] = value
            else:
                low1_ref[row - (ROWS - BEFORE), g - cut, k] = value
            place(row, g, k, value)

        turned([rows_ref.at[at, 0], rows_ref.at[at, 1]], mask_ref[row : row + 1, :], SKEW[row], mask_ref.shape[1], put)
    total = None
    for r in range(ROWS):
        z = z_ref[r]
        part = lax.dot_general(z, z, NT, preferred_element_type=jnp.float32)
        total = part if total is None else total + part
    real = total[:LANES, :LANES] + total[LANES:, LANES:]
    imag = total[LANES:, :LANES] - total[:LANES, LANES:]
    i = lax.broadcasted_iota(jnp.int32, real.shape, 0)
    j = lax.broadcasted_iota(jnp.int32, real.shape, 1)
    gram_ref[...] = jnp.where(i <= j, real, imag)


def rest(images, valid_mask, top, cut):
    count, columns = images.shape[2:]
    groups = top.shape[1]
    vmem = pl.BlockSpec(memory_space=pltpu.VMEM)

    def shape(rows, n):
        return jax.ShapeDtypeStruct((rows, n, 2, count, LANES), jnp.bfloat16)

    return pl.pallas_call(
        functools.partial(rest_kernel, cut),
        in_specs=[pl.BlockSpec(memory_space=pltpu.HBM), vmem, vmem],
        out_specs=[vmem] * 4,
        out_shape=[
            shape(ROWS - AFTER - BEFORE, groups),
            shape(BEFORE, cut),
            shape(BEFORE, groups - cut),
            jax.ShapeDtypeStruct((LANES, LANES), jnp.float32),
        ],
        scratch_shapes=[
            pltpu.VMEM((ROWS - AFTER, 2, count, columns), jnp.bfloat16),
            pltpu.VMEM((ROWS, 2 * LANES, groups * LANES), jnp.bfloat16),
            pltpu.SemaphoreType.DMA((ROWS - AFTER,)),
        ],
        compiler_params=pltpu.CompilerParams(vmem_limit_bytes=58 * 2**20),
        cost_estimate=pl.CostEstimate(flops=10**9, bytes_accessed=5 * 10**6, transcendentals=0),
        name="rest",
    )(images, valid_mask, top)


def again_kernel(in_ref, out_ref):
    out_ref[...] = in_ref[...]


def again(array):
    vmem = pl.BlockSpec(memory_space=pltpu.VMEM)
    return pl.pallas_call(
        again_kernel,
        in_specs=[vmem],
        out_specs=vmem,
        out_shape=jax.ShapeDtypeStruct(array.shape, array.dtype),
        compiler_params=pltpu.CompilerParams(vmem_limit_bytes=16 * 2**20),
        cost_estimate=pl.CostEstimate(flops=0, bytes_accessed=2 * 10**6, transcendentals=0),
        name="again",
    )(array)


def added(terms):
    if len(terms) == 4:
        return (terms[0] + terms[2]) + (terms[1] + terms[3])
    return functools.reduce(jnp.add, terms)


def slab_values(terms):
    packed = added(terms)
    flipped = packed.T
    i = lax.broadcasted_iota(jnp.int32, packed.shape, 0)
    j = lax.broadcasted_iota(jnp.int32, packed.shape, 1)
    real = jnp.where(i <= j, packed, flipped)
    imag = jnp.where(i > j, packed, jnp.where(i < j, -flipped, 0.0))
    powers = jnp.where(i == j, packed, 0.0)
    scaled = jnp.sqrt(jnp.sum(powers, axis=1, keepdims=True) * jnp.sum(powers, axis=0, keepdims=True))
    return real / scaled, imag / scaled


INNER = (1, 2, 3, 4, 5)
HALVES = (
    ((-3, -2, -1, 0), (((1, 2, 3), None), (None, (-1, 0)))),
    ((6, 7, 8, 9), ((None, (6, 7)), ((3, 4, 5), None))),
)


def looks_kernel(half, aliased, terms, *refs):
    other_ref, top_ref, mid_ref, low_ref = refs[:4]
    refs = refs[4 + aliased :]
    term_refs, refs = refs[:terms], refs[terms:]
    if terms:
        out_ref, slab_ref, w_ref, m_ref = refs
    else:
        out_ref, w_ref, m_ref = refs
    count = top_ref.shape[3]

    @pl.when(pl.program_id(0) == 0)
    def _():
        w_ref[...] = jnp.zeros_like(w_ref)
        m_ref[...] = jnp.zeros_like(m_ref)
        if terms:
            real, imag = slab_values([t[...] for t in term_refs])
            slab_ref[0] = real[:count, :count]
            slab_ref[1] = imag[:count, :count]

    rows = {}
    for r in range(ROWS):
        if r < AFTER:
            rows[r] = top_ref.at[r, 0]
        elif r >= ROWS - BEFORE:
            rows[r] = low_ref.at[r - (ROWS - BEFORE), 0]
        else:
            rows[r] = mid_ref.at[r - AFTER, 0]
    for r in range(other_ref.shape[0]):
        rows[ROWS + r if half else r - BEFORE] = other_ref.at[r, 0]

    lane = lax.broadcasted_iota(jnp.int32, (1, LANES), 1)

    def lanes_of(turn):
        place = lane + (-LOOK * turn) % LANES
        place = jnp.where(place >= LANES, place - LANES, place)
        return place < LOOK

    def widened(which):
        return jnp.broadcast_to(which.astype(jnp.float32), (count, LANES)).astype(jnp.bfloat16) != 0

    single = [lanes_of(t) for t in range(2 * PER - 1)]
    wide = [widened(s) for s in single]
    zero = jnp.zeros((count, LANES), jnp.bfloat16)

    def turn(l, r):
        return l + SKEW[r % ROWS]

    def gathered(l, k, which):
        out = zero
        for r in which:
            out = jnp.where(wide[turn(l, r)], rows[r][k], out)
        return out

    def kept(l, value, which):
        if which is None:
            return value
        select = single[turn(l, which[0])]
        for r in which[1:]:
            select = select | single[turn(l, r)]
        return jnp.where(widened(select), value, zero)

    i = lax.broadcasted_iota(jnp.int32, (count, LANES), 0)
    j = lax.broadcasted_iota(jnp.int32, (count, LANES), 1)
    eye = i == j

    def normalised(real, imag, w, l):
        power = jnp.sum(jnp.where(eye, real, 0.0), axis=0, keepdims=True)
        across = lax.rsqrt(jnp.maximum(power, floor_power))
        down = jnp.sum(jnp.where(eye, across, 0.0), axis=1, keepdims=True)
        out_ref[w, l, 0] = (real * down * across).astype(jnp.bfloat16)[:, :count]
        out_ref[w, l, 1] = (imag * down * across).astype(jnp.bfloat16)[:, :count]

    outer_rows, windows = HALVES[half]
    for l in range(PER):
        slot = l % 2
        for k in range(2):
            inner = gathered(l, k, INNER)
            outer = gathered(l, k, outer_rows)
            w_ref[slot, k, pl.ds(0, count), pl.ds(0, LANES)] = inner
            w_ref[slot, k, pl.ds(0, count), pl.ds(LANES, LANES)] = outer
            for w, (inner_rows, rest_rows) in enumerate(windows):
                m_ref[slot, w, k, pl.ds(0, count), pl.ds(0, LANES)] = kept(l, inner, inner_rows)
                m_ref[slot, w, k, pl.ds(0, count), pl.ds(LANES, LANES)] = kept(l, outer, rest_rows)
        gram = lax.dot_general(
            m_ref[slot].reshape(4 * LANES, 2 * LANES),
            w_ref[slot].reshape(2 * LANES, 2 * LANES),
            NT,
            preferred_element_type=jnp.float32,
        )
        for w in range(2):
            base = 2 * w * LANES
            re = gram[base : base + count]
            im = gram[base + LANES : base + LANES + count]
            normalised(re[:, :LANES] + im[:, LANES:], im[:, :LANES] - re[:, LANES:], w, l)


def looked(half, other, top, mid, low, first, looks, previous, terms):
    groups, _, count, _ = other.shape[1:]

    def spec(array):
        offset = 0 if array.shape[1] == groups else first
        return pl.BlockSpec((array.shape[0], 1) + array.shape[2:], lambda s: (0, s + offset, 0, 0, 0))

    operands = [other, top, mid, low]
    in_specs = [spec(a) for a in operands]
    aliases = {}
    if previous is not None:
        aliases = {len(operands): 0}
        operands.append(previous)
        in_specs.append(pl.BlockSpec(memory_space=pl.ANY))
    for term in terms:
        operands.append(term)
        in_specs.append(pl.BlockSpec(term.shape, lambda s: (0, 0)))
    out_specs = [pl.BlockSpec((2, PER, 2, count, count), lambda s: (half, s + first, 0, 0, 0))]
    out_shape = [jax.ShapeDtypeStruct((ROWS // 2, looks, 2, count, count), jnp.bfloat16)]
    if terms:
        out_specs.append(pl.BlockSpec((2, count, count), lambda s: (0, 0, 0)))
        out_shape.append(jax.ShapeDtypeStruct((2, count, count), jnp.float32))
    return pl.pallas_call(
        functools.partial(looks_kernel, half, previous is not None, len(terms)),
        grid=(groups,),
        in_specs=in_specs,
        out_specs=out_specs,
        out_shape=out_shape,
        input_output_aliases=aliases,
        scratch_shapes=[
            pltpu.VMEM((2, 2, LANES, 2 * LANES), jnp.bfloat16),
            pltpu.VMEM((2, 2, 2, LANES, 2 * LANES), jnp.bfloat16),
        ],
        compiler_params=pltpu.CompilerParams(vmem_limit_bytes=32 * 2**20),
        cost_estimate=pl.CostEstimate(
            flops=groups * PER * 2 * 512 * 256 * 256, bytes_accessed=groups * 10**6, transcendentals=0
        ),
        name="looks",
    )(*operands)


def axis_terms(value, axis):
    size = lax.axis_size(axis)
    stride = 1
    terms = [value]
    while size > stride:
        left = size // stride
        if left % 2:
            return [lax.psum(value, axis)]
        radix = 4 if left % 4 == 0 else 2
        part = added(terms)
        terms = [part]
        for shift in range(1, radix):
            pairs = []
            for i in range(size):
                place = (i // stride) % radix
                pairs.append((i, i + ((place + shift) % radix - place) * stride))
            terms.append(lax.ppermute(part, axis, pairs))
        stride *= radix
    return terms


def shards(images, valid_mask):
    looks = images.shape[3] // LOOK
    groups = -(-looks // PER)
    size = lax.axis_size("pix")
    cut = -(-groups // 2)
    forward = [(i, i + 1) for i in range(size - 1)]
    top = edge(images, valid_mask, groups)
    after = lax.ppermute(top, "pix", [(i + 1, i) for i in range(size - 1)])
    mid, low0, low1, total = rest(images, valid_mask, top, cut)
    before0 = lax.ppermute(low0, "pix", forward)
    terms = axis_terms(total, "pix")
    before1 = lax.ppermute(again(low1), "pix", forward)
    low = jnp.concatenate([low0, low1], axis=1)
    (out,) = looked(1, after, top, mid, low, 0, looks, None, [])
    (out,) = looked(0, before0, top, mid, low0, 0, looks, out, [])
    out, slab = looked(0, before1, top, mid, low1, cut, looks, out, terms)
    return (out, slab)


def solution(mesh):
    in_specs = (P(("group", "pix"), None, None, None), P(("group", "pix"), None))
    out_specs = (P(("group", "pix"), None, None, None, None), P("group", None, None))
    return jax.shard_map(shards, mesh=mesh, in_specs=in_specs, out_specs=out_specs, check_vma=False)
```

```python
import functools
import jax
import jax.numpy as jnp
from jax import lax
from jax.experimental import pallas as pl
from jax.experimental.pallas import tpu as pltpu
from jax.sharding import PartitionSpec as P

floor_power = 30.0

LOOK = 21
LANES = 128
TILE = 16
PER = LANES // LOOK
SPAN = PER * LOOK
ROWS = 8
SKEW = (5, 0, 1, 2, 3, 4, 1, 2)
BEFORE, AFTER = 3, 2
NT = (((1,), (1,)), ((), ()))


def turned(image, mask, skew, columns, put):
    count = image[0].shape[0]
    zero = jnp.zeros((count, LANES), jnp.bfloat16)
    lane = lax.broadcasted_iota(jnp.int32, (1, LANES), 1)

    def tile(value, g):
        start, stop = g * LANES, min((g + 1) * LANES, columns)
        part = value[:, start:stop]
        if stop - start < LANES:
            rest = jnp.zeros((part.shape[0], LANES - (stop - start)), part.dtype)
            part = jnp.concatenate([part, rest], axis=1)
        return part

    def widened(which):
        return jnp.broadcast_to(which.astype(jnp.float32), (count, LANES)).astype(jnp.bfloat16) != 0

    tiles = -(-columns // LANES)
    for g in range(-(-columns // SPAN)):
        slide = (LANES - SPAN) * g
        place = (lane + slide) % LANES
        used = (place < SPAN) & (SPAN * g + place < columns)
        prior = lane >= LANES - slide
        sides = [t for t in (g - 1, g) if 0 <= t < tiles]

        def joined(value):
            parts = [tile(value, t) for t in sides]
            if len(parts) == 1:
                return parts[0]
            which = prior if value.shape[0] == 1 else widened(prior)
            return jnp.where(which, parts[0], parts[1])

        keep = widened(used & (joined(mask) != 0))
        for k in range(2):
            row = jnp.where(keep, joined(image[k]), zero)
            put(g, k, pltpu.roll(row, slide + LOOK * skew, 1))


def fetched(image_ref, mask_ref, rows_ref, masks_ref, sems, order):
    copies = [pltpu.make_async_copy(mask_ref, masks_ref, sems.at[len(order)])]
    for at, row in enumerate(order):
        copies.append(pltpu.make_async_copy(image_ref.at[row], rows_ref.at[at], sems.at[at]))
    for copy in copies:
        copy.start()
    return copies[0], copies[1:]


def rows_kernel(jobs, behind, image_ref, mask_ref, *refs):
    order = [row for row, _ in jobs]
    count = sum(len(targets) for _, targets in jobs)
    rows_ref, masks_ref, turned_ref, in_sems, out_sems = refs[-5:]
    outs = refs[behind:-5]
    mask_copy, fetches = fetched(image_ref, mask_ref, rows_ref, masks_ref, in_sems, order)
    mask_copy.wait()
    stores = []
    for at, (row, targets) in enumerate(jobs):
        fetches[at].wait()

        def put(g, k, value):
            turned_ref[at, g, k] = value

        turned([rows_ref.at[at, 0], rows_ref.at[at, 1]], masks_ref[row : row + 1, :], SKEW[row], masks_ref.shape[1], put)
        for out, i, start, stop in targets:
            store = pltpu.make_async_copy(turned_ref.at[at, start:stop], outs[out].at[i], out_sems.at[len(stores)])
            store.start()
            stores.append(store)
    for store in stores:
        store.wait()


def turned_rows(images, valid_mask, jobs, groups, shapes, name, behind=()):
    count, columns = images.shape[2:]
    far = pl.BlockSpec(memory_space=pl.ANY)
    stores = sum(len(targets) for _, targets in jobs)
    return pl.pallas_call(
        functools.partial(rows_kernel, jobs, len(behind)),
        in_specs=[far, far] + [far] * len(behind),
        out_specs=[far] * len(shapes),
        out_shape=[jax.ShapeDtypeStruct((rows, n, 2, count, LANES), jnp.bfloat16) for rows, n in shapes],
        scratch_shapes=[
            pltpu.VMEM((len(jobs), 2, count, columns), jnp.bfloat16),
            pltpu.VMEM(valid_mask.shape, jnp.int32),
            pltpu.VMEM((len(jobs), groups, 2, count, LANES), jnp.bfloat16),
            pltpu.SemaphoreType.DMA((len(jobs) + 1,)),
            pltpu.SemaphoreType.DMA((stores,)),
        ],
        compiler_params=pltpu.CompilerParams(vmem_limit_bytes=61 * 2**20),
        cost_estimate=pl.CostEstimate(flops=10**6, bytes_accessed=len(jobs) * 10**6, transcendentals=0),
        name=name,
    )(images, valid_mask, *behind)


def gram_kernel(image_ref, mask_ref, gram_ref, rows_ref, masks_ref, z_ref, sems):
    count, columns = image_ref.shape[2:]
    mask_copy, fetches = fetched(image_ref, mask_ref, rows_ref, masks_ref, sems, range(ROWS))
    z_ref[...] = jnp.zeros_like(z_ref)
    mask_copy.wait()
    zero = jnp.zeros((count, columns), jnp.bfloat16)
    total = None
    for r in range(ROWS):
        keep = masks_ref[r : r + 1, :] != 0
        keep = jnp.broadcast_to(keep.astype(jnp.float32), (count, columns)).astype(jnp.bfloat16) != 0
        fetches[r].wait()
        for k in range(2):
            z_ref[r % 2, pl.ds(k * LANES, count), pl.ds(0, columns)] = jnp.where(keep, rows_ref[r, k], zero)
        z = z_ref[r % 2]
        part = lax.dot_general(z, z, NT, preferred_element_type=jnp.float32)
        total = part if total is None else total + part
    real = total[:LANES, :LANES] + total[LANES:, LANES:]
    imag = total[LANES:, :LANES] - total[:LANES, LANES:]
    i = lax.broadcasted_iota(jnp.int32, real.shape, 0)
    j = lax.broadcasted_iota(jnp.int32, real.shape, 1)
    gram_ref[...] = jnp.where(i <= j, real, imag)


def local_gram(images, valid_mask):
    count, columns = images.shape[2:]
    far = pl.BlockSpec(memory_space=pl.ANY)
    return pl.pallas_call(
        gram_kernel,
        in_specs=[far, far],
        out_specs=pl.BlockSpec(memory_space=pltpu.VMEM),
        out_shape=jax.ShapeDtypeStruct((LANES, LANES), jnp.float32),
        scratch_shapes=[
            pltpu.VMEM(images.shape, jnp.bfloat16),
            pltpu.VMEM(valid_mask.shape, jnp.int32),
            pltpu.VMEM((2, 2 * LANES, -(-columns // LANES) * LANES), jnp.bfloat16),
            pltpu.SemaphoreType.DMA((ROWS + 1,)),
        ],
        compiler_params=pltpu.CompilerParams(vmem_limit_bytes=61 * 2**20),
        cost_estimate=pl.CostEstimate(flops=10**9, bytes_accessed=5 * 10**6, transcendentals=0),
        name="gram",
    )(images, valid_mask)


def added(terms):
    if len(terms) == 4:
        return (terms[0] + terms[2]) + (terms[1] + terms[3])
    return functools.reduce(jnp.add, terms)


def slab_values(terms):
    packed = added(terms)
    flipped = packed.T
    i = lax.broadcasted_iota(jnp.int32, packed.shape, 0)
    j = lax.broadcasted_iota(jnp.int32, packed.shape, 1)
    real = jnp.where(i <= j, packed, flipped)
    imag = jnp.where(i > j, packed, jnp.where(i < j, -flipped, 0.0))
    powers = jnp.where(i == j, packed, 0.0)
    scaled = jnp.sqrt(jnp.sum(powers, axis=1, keepdims=True) * jnp.sum(powers, axis=0, keepdims=True))
    return real / scaled, imag / scaled


INNER = (1, 2, 3, 4, 5)
HALVES = (
    ((-3, -2, -1, 0), (((1, 2, 3), None), (None, (-1, 0)))),
    ((6, 7, 8, 9), ((None, (6, 7)), ((3, 4, 5), None))),
)


def looks_kernel(half, aliased, terms, *refs):
    other_ref, top_ref, mid_ref, low_ref = refs[:4]
    refs = refs[4 + aliased :]
    term_refs, refs = refs[:terms], refs[terms:]
    out_ref, extra_ref, w_ref = refs
    count = top_ref.shape[3]

    @pl.when(pl.program_id(0) == 0)
    def _():
        w_ref[...] = jnp.zeros_like(w_ref)
        if terms:
            real, imag = slab_values([t[...] for t in term_refs])
            extra_ref[0] = real[:count, :count]
            extra_ref[1] = imag[:count, :count]
        else:
            extra_ref[...] = jnp.zeros_like(extra_ref)

    rows = {}
    for r in range(ROWS):
        if r < AFTER:
            rows[r] = top_ref.at[r, 0]
        elif r >= ROWS - BEFORE:
            rows[r] = low_ref.at[r - (ROWS - BEFORE), 0]
        else:
            rows[r] = mid_ref.at[r - AFTER, 0]
    for r in range(other_ref.shape[0]):
        rows[ROWS + r if half else r - BEFORE] = other_ref.at[r, 0]

    lane = lax.broadcasted_iota(jnp.int32, (1, LANES), 1)

    def lanes_of(turn):
        place = lane + (-LOOK * turn) % LANES
        place = jnp.where(place >= LANES, place - LANES, place)
        return place < LOOK

    def widened(which):
        return jnp.broadcast_to(which.astype(jnp.float32), (count, LANES)).astype(jnp.bfloat16) != 0

    single = [lanes_of(t) for t in range(2 * PER - 1)]
    wide = [widened(s) for s in single]
    zero = jnp.zeros((count, LANES), jnp.bfloat16)

    def turn(l, r):
        return l + SKEW[r % ROWS]

    def gathered(l, k, which):
        out = zero
        for r in which:
            out = jnp.where(wide[turn(l, r)], rows[r][k], out)
        return out

    def kept(l, which):
        select = jnp.ones((1, LANES), jnp.bool_)
        if which is not None:
            select = single[turn(l, which[0])]
            for r in which[1:]:
                select = select | single[turn(l, r)]
        return select.astype(jnp.float32)

    i = lax.broadcasted_iota(jnp.int32, (count, LANES), 0)
    j = lax.broadcasted_iota(jnp.int32, (count, LANES), 1)
    eye = i == j

    def normalised(real, imag, w, l):
        power = jnp.sum(jnp.where(eye, real, 0.0), axis=0, keepdims=True)
        across = lax.rsqrt(jnp.maximum(power, floor_power))
        down = jnp.sum(jnp.where(eye, across, 0.0), axis=1, keepdims=True)
        out_ref[w, l, 0] = (real * down * across).astype(jnp.bfloat16)[:, :count]
        out_ref[w, l, 1] = (imag * down * across).astype(jnp.bfloat16)[:, :count]

    outer_rows, windows = HALVES[half]
    for l in range(PER):
        slot = l % 2
        for k in range(2):
            w_ref[slot, k, pl.ds(0, count), pl.ds(0, LANES)] = gathered(l, k, INNER)
            w_ref[slot, k, pl.ds(0, count), pl.ds(LANES, LANES)] = gathered(l, k, outer_rows)
        every = w_ref[slot].reshape(2 * LANES, 2 * LANES)
        nothing = jnp.zeros_like(every)
        reads = []
        for inner_rows, rest_rows in windows:
            lanes = jnp.concatenate([kept(l, inner_rows), kept(l, rest_rows)], axis=1)
            lanes = jnp.broadcast_to(lanes, every.shape).astype(jnp.bfloat16) != 0
            read = jnp.where(lanes, every, nothing)
            for start in range(0, LANES, TILE):
                reads.append(read[start : start + TILE])
                reads.append(read[LANES + start : LANES + start + TILE])
        gram = lax.dot_general(jnp.concatenate(reads, axis=0), every, NT, preferred_element_type=jnp.float32)
        for w in range(2):
            real, imag = [], []
            for start in range(0, LANES, TILE):
                base = 2 * (w * LANES + start)
                re, im = gram[base : base + TILE], gram[base + TILE : base + 2 * TILE]
                real.append(re[:, :LANES] + im[:, LANES:])
                imag.append(im[:, :LANES] - re[:, LANES:])
            normalised(jnp.concatenate(real, axis=0)[:count], jnp.concatenate(imag, axis=0)[:count], w, l)


def looked(half, other, top, mid, low, first, looks, previous, terms):
    groups, _, count, _ = other.shape[1:]

    def spec(array):
        offset = 0 if array.shape[1] == groups else first
        return pl.BlockSpec((array.shape[0], 1) + array.shape[2:], lambda s: (0, s + offset, 0, 0, 0))

    operands = [other, top, mid, low]
    in_specs = [spec(a) for a in operands]
    aliases = {}
    if previous is not None:
        aliases = {len(operands): 0}
        operands.append(previous)
        in_specs.append(pl.BlockSpec(memory_space=pl.ANY))
    for term in terms:
        operands.append(term)
        in_specs.append(pl.BlockSpec(term.shape, lambda s: (0, 0)))
    extra = (2, count, count) if terms else (LANES, LANES)
    out_specs = [
        pl.BlockSpec((2, PER, 2, count, count), lambda s: (half, s + first, 0, 0, 0)),
        pl.BlockSpec(extra, lambda s: (0,) * len(extra)),
    ]
    out_shape = [
        jax.ShapeDtypeStruct((ROWS // 2, looks, 2, count, count), jnp.bfloat16),
        jax.ShapeDtypeStruct(extra, jnp.float32),
    ]
    return pl.pallas_call(
        functools.partial(looks_kernel, half, previous is not None, len(terms)),
        grid=(groups,),
        in_specs=in_specs,
        out_specs=out_specs,
        out_shape=out_shape,
        input_output_aliases=aliases,
        scratch_shapes=[
            pltpu.VMEM((2, 2, LANES, 2 * LANES), jnp.bfloat16),
        ],
        compiler_params=pltpu.CompilerParams(vmem_limit_bytes=32 * 2**20),
        cost_estimate=pl.CostEstimate(
            flops=groups * PER * 2 * 512 * 256 * 256, bytes_accessed=groups * 10**6, transcendentals=0
        ),
        name="looks",
    )(*operands)


def radices(size):
    found = []
    while size % 4 == 0:
        found.append(4)
        size //= 4
    if size == 2:
        found.append(2)
        size = 1
    return found if size == 1 else None


def round_terms(value, axis, stride, radix):
    size = lax.axis_size(axis)
    terms = [value]
    for shift in range(1, radix):
        pairs = []
        for i in range(size):
            place = (i // stride) % radix
            pairs.append((i, i + ((place + shift) % radix - place) * stride))
        terms.append(lax.ppermute(value, axis, pairs))
    return terms


def shards(images, valid_mask):
    looks = images.shape[3] // LOOK
    groups = -(-looks // PER)
    cut = -(-groups // 2)
    size = lax.axis_size("pix")
    forward = [(i, i + 1) for i in range(size - 1)]
    backward = [(i + 1, i) for i in range(size - 1)]
    (top,) = turned_rows(
        images, valid_mask, [(r, ((0, r, 0, groups),)) for r in range(AFTER)], groups, [(AFTER, groups)], "first_rows"
    )
    after = lax.ppermute(top, "pix", backward)

    total = local_gram(images, valid_mask)
    steps = radices(size)
    if steps:
        terms = round_terms(total, "pix", 1, steps[0])
    else:
        terms = [lax.psum(total, "pix")]

    jobs = []
    for r in range(BEFORE):
        jobs.append((ROWS - BEFORE + r, ((0, r, 0, cut), (1, r, cut, groups), (2, r, 0, groups))))
    for r in range(ROWS - BEFORE - AFTER):
        jobs.append((AFTER + r, ((3, r, 0, groups),)))
    shapes = [(BEFORE, cut), (BEFORE, groups - cut), (BEFORE, groups), (ROWS - BEFORE - AFTER, groups)]
    low0, low1, low, mid = turned_rows(images, valid_mask, jobs, groups, shapes, "last_rows", (total,))
    before0 = lax.ppermute(low0, "pix", forward)
    before1 = lax.ppermute(low1, "pix", forward)

    out, zeros = looked(1, after, top, mid, low, 0, looks, None, [])
    if steps:
        stride = steps[0]
        for radix in steps[1:]:
            terms = round_terms(added(terms) + zeros, "pix", stride, radix)
            stride *= radix
    out, _ = looked(0, before0, top, mid, low, 0, looks, out, [])
    out, slab = looked(0, before1, top, mid, low, cut, looks, out, terms)
    return (out, slab)


def solution(mesh):
    in_specs = (P(("group", "pix"), None, None, None), P(("group", "pix"), None))
    out_specs = (P(("group", "pix"), None, None, None, None), P("group", None, None))
    return jax.shard_map(shards, mesh=mesh, in_specs=in_specs, out_specs=out_specs, check_vma=False)
```

```python
import functools
import jax
import jax.numpy as jnp
from jax import lax
from jax.experimental import pallas as pl
from jax.experimental.pallas import tpu as pltpu
from jax.sharding import PartitionSpec as P

floor_power = 30.0

LOOK = 21
LANES = 128
TILE = 16
PER = LANES // LOOK
SPAN = PER * LOOK
ROWS = 8
SKEW = (5, 0, 1, 2, 3, 4, 1, 2)
BEFORE, AFTER = 3, 2
NT = (((1,), (1,)), ((), ()))


def turned(image, mask, skew, columns, put):
    count = image[0].shape[0]
    zero = jnp.zeros((count, LANES), jnp.bfloat16)
    lane = lax.broadcasted_iota(jnp.int32, (1, LANES), 1)

    def tile(value, g):
        start, stop = g * LANES, min((g + 1) * LANES, columns)
        part = value[:, start:stop]
        if stop - start < LANES:
            rest = jnp.zeros((part.shape[0], LANES - (stop - start)), part.dtype)
            part = jnp.concatenate([part, rest], axis=1)
        return part

    def widened(which):
        return jnp.broadcast_to(which.astype(jnp.float32), (count, LANES)).astype(jnp.bfloat16) != 0

    tiles = -(-columns // LANES)
    for g in range(-(-columns // SPAN)):
        slide = (LANES - SPAN) * g
        place = (lane + slide) % LANES
        used = (place < SPAN) & (SPAN * g + place < columns)
        prior = lane >= LANES - slide
        sides = [t for t in (g - 1, g) if 0 <= t < tiles]

        def joined(value):
            parts = [tile(value, t) for t in sides]
            if len(parts) == 1:
                return parts[0]
            which = prior if value.shape[0] == 1 else widened(prior)
            return jnp.where(which, parts[0], parts[1])

        keep = widened(used & (joined(mask) != 0))
        for k in range(2):
            row = jnp.where(keep, joined(image[k]), zero)
            put(g, k, pltpu.roll(row, slide + LOOK * skew, 1))


def fetched(image_ref, mask_ref, rows_ref, masks_ref, sems, order):
    mask_copy = pltpu.make_async_copy(mask_ref, masks_ref, sems.at[len(order)])
    mask_copy.start()
    copies = [pltpu.make_async_copy(image_ref.at[row], rows_ref.at[at], sems.at[at]) for at, row in enumerate(order)]
    for copy in copies:
        copy.start()
    mask_copy.wait()
    return copies


EDGE = tuple(range(AFTER)) + tuple(range(ROWS - BEFORE, ROWS))


def edge_kernel(image_ref, mask_ref, top_ref, low_ref, rows_ref, masks_ref, turned_ref, in_sems, out_sems):
    fetches = fetched(image_ref, mask_ref, rows_ref, masks_ref, in_sems, EDGE)
    stores = []
    for at, row in enumerate(EDGE):
        fetches[at].wait()

        def put(g, k, value):
            turned_ref[at, g, k] = value

        turned([rows_ref.at[at, 0], rows_ref.at[at, 1]], masks_ref[row : row + 1, :], SKEW[row], masks_ref.shape[1], put)
        target = top_ref.at[row] if row < AFTER else low_ref.at[row - (ROWS - BEFORE)]
        store = pltpu.make_async_copy(turned_ref.at[at], target, out_sems.at[at])
        store.start()
        stores.append(store)
    for store in stores:
        store.wait()


def rows_shape(rows, groups, count):
    return jax.ShapeDtypeStruct((rows, groups, 2, count, LANES), jnp.bfloat16)


def edge_rows(images, valid_mask, groups):
    count = images.shape[2]
    far = pl.BlockSpec(memory_space=pl.ANY)
    return pl.pallas_call(
        edge_kernel,
        in_specs=[far, far],
        out_specs=[far, far],
        out_shape=[rows_shape(AFTER, groups, count), rows_shape(BEFORE, groups, count)],
        scratch_shapes=[
            pltpu.VMEM((len(EDGE),) + images.shape[1:], jnp.bfloat16),
            pltpu.VMEM(valid_mask.shape, jnp.int32),
            pltpu.VMEM((len(EDGE), groups, 2, count, LANES), jnp.bfloat16),
            pltpu.SemaphoreType.DMA((len(EDGE) + 1,)),
            pltpu.SemaphoreType.DMA((len(EDGE),)),
        ],
        compiler_params=pltpu.CompilerParams(vmem_limit_bytes=61 * 2**20),
        cost_estimate=pl.CostEstimate(flops=10**6, bytes_accessed=4 * 10**6, transcendentals=0),
        name="edge_rows",
    )(images, valid_mask)


def middle_kernel(image_ref, mask_ref, edge_ref, mid_ref, gram_ref, rows_ref, masks_ref, turned_ref, z_ref, in_sems, out_sems):
    groups = mid_ref.shape[1]
    count, columns = image_ref.shape[2:]
    order = tuple(range(AFTER, ROWS - BEFORE)) + EDGE
    fetches = fetched(image_ref, mask_ref, rows_ref, masks_ref, in_sems, order)
    z_ref[...] = jnp.zeros_like(z_ref)
    zero = jnp.zeros((count, columns), jnp.bfloat16)
    stores = []
    total = None
    wide = groups * LANES
    for at, row in enumerate(order):
        fetches[at].wait()
        mask = masks_ref[row : row + 1, :]
        if AFTER <= row < ROWS - BEFORE:

            def put(g, k, value):
                turned_ref[at, g, k] = value
                z_ref[pl.ds(k * LANES, count), pl.ds(at * wide + g * LANES, LANES)] = value

            turned([rows_ref.at[at, 0], rows_ref.at[at, 1]], mask, SKEW[row], columns, put)
            store = pltpu.make_async_copy(turned_ref.at[at], mid_ref.at[row - AFTER], out_sems.at[at])
            store.start()
            stores.append(store)
        else:
            keep = jnp.broadcast_to((mask != 0).astype(jnp.float32), (count, columns)).astype(jnp.bfloat16) != 0
            for k in range(2):
                z_ref[pl.ds(k * LANES, count), pl.ds(at * wide, columns)] = jnp.where(keep, rows_ref[at, k], zero)
        if at % 2:
            z = z_ref[:, pl.ds((at - 1) * wide, 2 * wide)]
            part = lax.dot_general(z, z, NT, preferred_element_type=jnp.float32)
            total = part if total is None else total + part
    real = total[:LANES, :LANES] + total[LANES:, LANES:]
    imag = total[LANES:, :LANES] - total[:LANES, LANES:]
    i = lax.broadcasted_iota(jnp.int32, real.shape, 0)
    j = lax.broadcasted_iota(jnp.int32, real.shape, 1)
    gram_ref[...] = jnp.where(i <= j, real, imag)
    for store in stores:
        store.wait()


def middle_rows(images, valid_mask, low):
    count = images.shape[2]
    groups = low.shape[1]
    rows = ROWS - AFTER - BEFORE
    far = pl.BlockSpec(memory_space=pl.ANY)
    return pl.pallas_call(
        middle_kernel,
        in_specs=[far, far, far],
        out_specs=[far, pl.BlockSpec(memory_space=pltpu.VMEM)],
        out_shape=[rows_shape(rows, groups, count), jax.ShapeDtypeStruct((LANES, LANES), jnp.float32)],
        scratch_shapes=[
            pltpu.VMEM(images.shape, jnp.bfloat16),
            pltpu.VMEM(valid_mask.shape, jnp.int32),
            pltpu.VMEM((rows, groups, 2, count, LANES), jnp.bfloat16),
            pltpu.VMEM((2 * LANES, ROWS * groups * LANES), jnp.bfloat16),
            pltpu.SemaphoreType.DMA((ROWS + 1,)),
            pltpu.SemaphoreType.DMA((rows,)),
        ],
        compiler_params=pltpu.CompilerParams(vmem_limit_bytes=61 * 2**20),
        cost_estimate=pl.CostEstimate(flops=10**9, bytes_accessed=5 * 10**6, transcendentals=0),
        name="middle_rows",
    )(images, valid_mask, low)


def added(terms):
    if len(terms) == 4:
        return (terms[0] + terms[2]) + (terms[1] + terms[3])
    return functools.reduce(jnp.add, terms)


def slab_values(terms):
    packed = added(terms)
    flipped = packed.T
    i = lax.broadcasted_iota(jnp.int32, packed.shape, 0)
    j = lax.broadcasted_iota(jnp.int32, packed.shape, 1)
    real = jnp.where(i <= j, packed, flipped)
    imag = jnp.where(i > j, packed, jnp.where(i < j, -flipped, 0.0))
    powers = jnp.where(i == j, packed, 0.0)
    scaled = jnp.sqrt(jnp.sum(powers, axis=1, keepdims=True) * jnp.sum(powers, axis=0, keepdims=True))
    return real / scaled, imag / scaled


INNER = (1, 2, 3, 4, 5)
HALVES = (
    ((-3, -2, -1, 0), (((1, 2, 3), None), (None, (-1, 0)))),
    ((6, 7, 8, 9), ((None, (6, 7)), ((3, 4, 5), None))),
)


def looks_kernel(half, aliased, terms, slab, *refs):
    other_ref, top_ref, mid_ref, low_ref = refs[:4]
    refs = refs[4 + aliased :]
    term_refs, refs = refs[:terms], refs[terms:]
    out_ref, extra_ref, w_ref = refs
    count = top_ref.shape[3]

    @pl.when(pl.program_id(0) == 0)
    def _():
        w_ref[...] = jnp.zeros_like(w_ref)
        if slab:
            real, imag = slab_values([t[...] for t in term_refs])
            extra_ref[0] = real[:count, :count]
            extra_ref[1] = imag[:count, :count]
        elif terms:
            extra_ref[...] = added([t[...] for t in term_refs])
        else:
            extra_ref[...] = jnp.zeros_like(extra_ref)

    rows = {}
    for r in range(ROWS):
        if r < AFTER:
            rows[r] = top_ref.at[r, 0]
        elif r >= ROWS - BEFORE:
            rows[r] = low_ref.at[r - (ROWS - BEFORE), 0]
        else:
            rows[r] = mid_ref.at[r - AFTER, 0]
    for r in range(other_ref.shape[0]):
        rows[ROWS + r if half else r - BEFORE] = other_ref.at[r, 0]

    lane = lax.broadcasted_iota(jnp.int32, (1, LANES), 1)

    def lanes_of(turn):
        place = lane + (-LOOK * turn) % LANES
        place = jnp.where(place >= LANES, place - LANES, place)
        return place < LOOK

    def widened(which):
        return jnp.broadcast_to(which.astype(jnp.float32), (count, LANES)).astype(jnp.bfloat16) != 0

    single = [lanes_of(t) for t in range(2 * PER - 1)]
    wide = [widened(s) for s in single]

    def turn(l, r):
        return l + SKEW[r % ROWS]

    def gathered(l, k, which):
        out = rows[which[0]][k]
        for r in which[1:]:
            out = jnp.where(wide[turn(l, r)], rows[r][k], out)
        return out

    def kept(l, which):
        select = single[turn(l, which[0])]
        for r in which[1:]:
            select = select | single[turn(l, r)]
        return select.astype(jnp.float32)

    eight = (8, LANES)
    along = lax.broadcasted_iota(jnp.int32, eight, 1)
    on_eye = along % 8 == lax.broadcasted_iota(jnp.int32, eight, 0)
    block = along // 8

    def normalised(real, imag, w, l):
        picked = real[:8]
        for v in range(1, count // 8):
            picked = jnp.where(block == v, real[8 * v : 8 * v + 8], picked)
        power = jnp.sum(jnp.where(on_eye, picked, 0.0), axis=0, keepdims=True)
        across = lax.rsqrt(jnp.maximum(power, floor_power))
        diagonal = jnp.where(on_eye, across, 0.0)
        spread = jnp.concatenate([jnp.where(block == v, diagonal, 0.0) for v in range(count // 8)], axis=0)
        scale = jnp.sum(spread, axis=1, keepdims=True) * across
        out_ref[w, l, 0] = (real * scale).astype(jnp.bfloat16)[:, :count]
        out_ref[w, l, 1] = (imag * scale).astype(jnp.bfloat16)[:, :count]

    outer_rows, windows = HALVES[half]
    for l in range(PER):
        slot = l % 2
        for k in range(2):
            w_ref[slot, k, pl.ds(0, count), pl.ds(0, LANES)] = gathered(l, k, INNER)
            w_ref[slot, k, pl.ds(0, count), pl.ds(LANES, LANES)] = gathered(l, k, outer_rows)
        every = w_ref[slot].reshape(2 * LANES, 2 * LANES)
        nothing = jnp.zeros_like(every)
        reads = []
        for inner_rows, rest_rows in windows:
            lanes = jnp.concatenate([kept(l, inner_rows or INNER), kept(l, rest_rows or outer_rows)], axis=1)
            lanes = jnp.broadcast_to(lanes, every.shape).astype(jnp.bfloat16) != 0
            read = jnp.where(lanes, every, nothing)
            for start in range(0, LANES, TILE):
                reads.append(read[start : start + TILE])
                reads.append(read[LANES + start : LANES + start + TILE])
        gram = lax.dot_general(jnp.concatenate(reads, axis=0), every, NT, preferred_element_type=jnp.float32)
        for w in range(2):
            real, imag = [], []
            for start in range(0, LANES, TILE):
                base = 2 * (w * LANES + start)
                re, im = gram[base : base + TILE], gram[base + TILE : base + 2 * TILE]
                real.append(re[:, :LANES] + im[:, LANES:])
                imag.append(im[:, :LANES] - re[:, LANES:])
            normalised(jnp.concatenate(real, axis=0)[:count], jnp.concatenate(imag, axis=0)[:count], w, l)


def looked(half, other, top, mid, low, first, groups, looks, previous, terms, slab):
    count = other.shape[3]

    def spec(array):
        return pl.BlockSpec((array.shape[0], 1) + array.shape[2:], lambda s: (0, s + first, 0, 0, 0))

    operands = [other, top, mid, low]
    in_specs = [spec(a) for a in operands]
    aliases = {}
    if previous is not None:
        aliases = {len(operands): 0}
        operands.append(previous)
        in_specs.append(pl.BlockSpec(memory_space=pl.ANY))
    for term in terms:
        operands.append(term)
        in_specs.append(pl.BlockSpec(term.shape, lambda s: (0, 0)))
    extra = (2, count, count) if slab else (LANES, LANES)
    out_specs = [
        pl.BlockSpec((2, PER, 2, count, count), lambda s: (half, s + first, 0, 0, 0)),
        pl.BlockSpec(extra, lambda s: (0,) * len(extra)),
    ]
    out_shape = [
        jax.ShapeDtypeStruct((ROWS // 2, looks, 2, count, count), jnp.bfloat16),
        jax.ShapeDtypeStruct(extra, jnp.float32),
    ]
    return pl.pallas_call(
        functools.partial(looks_kernel, half, previous is not None, len(terms), slab),
        grid=(groups,),
        in_specs=in_specs,
        out_specs=out_specs,
        out_shape=out_shape,
        input_output_aliases=aliases,
        scratch_shapes=[
            pltpu.VMEM((2, 2, LANES, 2 * LANES), jnp.bfloat16),
        ],
        compiler_params=pltpu.CompilerParams(vmem_limit_bytes=51 * 2**20),
        cost_estimate=pl.CostEstimate(
            flops=20 * groups * PER * 2 * 512 * 256 * 256, bytes_accessed=groups * 10**6, transcendentals=0
        ),
        name="looks",
    )(*operands)


def rounds(size):
    found = []
    stride = 1
    while stride < size:
        radix = 4 if size // stride % 4 == 0 else 2
        if size // stride % radix:
            return None
        found.append((stride, radix))
        stride *= radix
    return found[::-1]


def round_terms(value, axis, stride, radix):
    size = lax.axis_size(axis)
    terms = [value]
    for shift in range(1, radix):
        pairs = []
        for i in range(size):
            place = (i // stride) % radix
            pairs.append((i, i + ((place + shift) % radix - place) * stride))
        terms.append(lax.ppermute(value, axis, pairs))
    return terms


def shards(images, valid_mask):
    looks = images.shape[3] // LOOK
    groups = -(-looks // PER)
    cut = -(-groups // 2)
    size = lax.axis_size("pix")
    forward = [(i, i + 1) for i in range(size - 1)]
    backward = [(i + 1, i) for i in range(size - 1)]
    top, low = edge_rows(images, valid_mask, groups)
    after = lax.ppermute(top, "pix", backward)
    before = lax.ppermute(low, "pix", forward)
    mid, total = middle_rows(images, valid_mask, low)
    steps = rounds(size)
    if steps is None:
        terms, steps = [lax.psum(total, "pix")], []
    else:
        terms = round_terms(total, "pix", *steps[0]) if steps else [total]
    out, total = looked(1, after, top, mid, low, 0, groups, looks, None, terms, False)
    terms = [total]
    for step in steps[1:]:
        terms = round_terms(added(terms), "pix", *step)
    out, _ = looked(0, before, top, mid, low, 0, cut, looks, out, [], False)
    out, slab = looked(0, before, top, mid, low, cut, groups - cut, looks, out, terms, True)
    return (out, slab)


def solution(mesh):
    in_specs = (P(("group", "pix"), None, None, None), P(("group", "pix"), None))
    out_specs = (P(("group", "pix"), None, None, None, None), P("group", None, None))
    return jax.shard_map(shards, mesh=mesh, in_specs=in_specs, out_specs=out_specs, check_vma=False)
```

```python
import functools
import jax
import jax.numpy as jnp
from jax import lax
from jax.experimental import pallas as pl
from jax.experimental.pallas import tpu as pltpu
from jax.sharding import PartitionSpec as P

floor_power = 30.0

LOOK = 21
LANES = 128
TILE = 16
PER = LANES // LOOK
SPAN = PER * LOOK
ROWS = 8
SKEW = (5, 0, 1, 2, 3, 4, 1, 2)
BEFORE, AFTER = 3, 2
NT = (((1,), (1,)), ((), ()))


def turned(image, mask, skew, columns, put):
    count = image[0].shape[0]
    zero = jnp.zeros((count, LANES), jnp.bfloat16)
    lane = lax.broadcasted_iota(jnp.int32, (1, LANES), 1)

    def tile(value, g):
        start, stop = g * LANES, min((g + 1) * LANES, columns)
        part = value[:, start:stop]
        if stop - start < LANES:
            rest = jnp.zeros((part.shape[0], LANES - (stop - start)), part.dtype)
            part = jnp.concatenate([part, rest], axis=1)
        return part

    def widened(which):
        return jnp.broadcast_to(which.astype(jnp.float32), (count, LANES)).astype(jnp.bfloat16) != 0

    tiles = -(-columns // LANES)
    for g in range(-(-columns // SPAN)):
        slide = (LANES - SPAN) * g
        place = (lane + slide) % LANES
        used = (place < SPAN) & (SPAN * g + place < columns)
        prior = lane >= LANES - slide
        sides = [t for t in (g - 1, g) if 0 <= t < tiles]

        def joined(value):
            parts = [tile(value, t) for t in sides]
            if len(parts) == 1:
                return parts[0]
            which = prior if value.shape[0] == 1 else widened(prior)
            return jnp.where(which, parts[0], parts[1])

        keep = widened(used & (joined(mask) != 0))
        for k in range(2):
            row = jnp.where(keep, joined(image[k]), zero)
            put(g, k, pltpu.roll(row, slide + LOOK * skew, 1))


def fetched(image_ref, mask_ref, rows_ref, masks_ref, sems, order):
    mask_copy = pltpu.make_async_copy(mask_ref, masks_ref, sems.at[len(order)])
    mask_copy.start()
    copies = [pltpu.make_async_copy(image_ref.at[row], rows_ref.at[at], sems.at[at]) for at, row in enumerate(order)]
    for copy in copies:
        copy.start()
    mask_copy.wait()
    return copies


EDGE = tuple(range(AFTER)) + tuple(range(ROWS - BEFORE, ROWS))


def edge_kernel(image_ref, mask_ref, top_ref, low_ref, _, rows_ref, masks_ref, turned_ref, in_sems, out_sems):
    fetches = fetched(image_ref, mask_ref, rows_ref, masks_ref, in_sems, EDGE)
    stores = []
    for at, row in enumerate(EDGE):
        fetches[at].wait()

        def put(g, k, value):
            turned_ref[at, g, k] = value

        turned([rows_ref.at[at, 0], rows_ref.at[at, 1]], masks_ref[row : row + 1, :], SKEW[row], masks_ref.shape[1], put)
        target = top_ref.at[row] if row < AFTER else low_ref.at[row - (ROWS - BEFORE)]
        store = pltpu.make_async_copy(turned_ref.at[at], target, out_sems.at[at])
        store.start()
        stores.append(store)
    for store in stores:
        store.wait()


def rows_shape(rows, groups, count):
    return jax.ShapeDtypeStruct((rows, groups, 2, count, LANES), jnp.bfloat16)


def edge_rows(images, valid_mask, groups):
    count = images.shape[2]
    far = pl.BlockSpec(memory_space=pl.ANY)
    return pl.pallas_call(
        edge_kernel,
        in_specs=[far, far],
        out_specs=[far] * 3,
        out_shape=[
            rows_shape(AFTER, groups, count),
            rows_shape(BEFORE, groups, count),
            jax.ShapeDtypeStruct((8, LANES), jnp.float32),
        ],
        scratch_shapes=[
            pltpu.VMEM((len(EDGE),) + images.shape[1:], jnp.bfloat16),
            pltpu.VMEM(valid_mask.shape, jnp.int32),
            pltpu.VMEM((len(EDGE), groups, 2, count, LANES), jnp.bfloat16),
            pltpu.SemaphoreType.DMA((len(EDGE) + 1,)),
            pltpu.SemaphoreType.DMA((len(EDGE),)),
        ],
        compiler_params=pltpu.CompilerParams(vmem_limit_bytes=61 * 2**20),
        cost_estimate=pl.CostEstimate(flops=10**6, bytes_accessed=4 * 10**6, transcendentals=0),
        name="edge_rows",
    )(images, valid_mask)


def middle_kernel(image_ref, mask_ref, _, mid_ref, gram_ref, rows_ref, masks_ref, turned_ref, z_ref, in_sems, out_sems):
    groups = mid_ref.shape[1]
    count, columns = image_ref.shape[2:]
    order = tuple(range(AFTER, ROWS - BEFORE)) + EDGE
    fetches = fetched(image_ref, mask_ref, rows_ref, masks_ref, in_sems, order)
    z_ref[...] = jnp.zeros_like(z_ref)
    zero = jnp.zeros((count, columns), jnp.bfloat16)
    stores = []
    total = None
    wide = groups * LANES
    for at, row in enumerate(order):
        fetches[at].wait()
        mask = masks_ref[row : row + 1, :]
        if AFTER <= row < ROWS - BEFORE:

            def put(g, k, value):
                turned_ref[at, g, k] = value
                z_ref[pl.ds(k * LANES, count), pl.ds(at * wide + g * LANES, LANES)] = value

            turned([rows_ref.at[at, 0], rows_ref.at[at, 1]], mask, SKEW[row], columns, put)
            store = pltpu.make_async_copy(turned_ref.at[at], mid_ref.at[row - AFTER], out_sems.at[at])
            store.start()
            stores.append(store)
        else:
            keep = jnp.broadcast_to((mask != 0).astype(jnp.float32), (count, columns)).astype(jnp.bfloat16) != 0
            for k in range(2):
                z_ref[pl.ds(k * LANES, count), pl.ds(at * wide, columns)] = jnp.where(keep, rows_ref[at, k], zero)
        if at % 2:
            z = z_ref[:, pl.ds((at - 1) * wide, 2 * wide)]
            part = lax.dot_general(z, z, NT, preferred_element_type=jnp.float32)
            total = part if total is None else total + part
    real = total[:LANES, :LANES] + total[LANES:, LANES:]
    imag = total[LANES:, :LANES] - total[:LANES, LANES:]
    i = lax.broadcasted_iota(jnp.int32, real.shape, 0)
    j = lax.broadcasted_iota(jnp.int32, real.shape, 1)
    gram_ref[...] = jnp.where(i <= j, real, imag)
    for store in stores:
        store.wait()


def middle_rows(images, valid_mask, groups, behind):
    count = images.shape[2]
    rows = ROWS - AFTER - BEFORE
    far = pl.BlockSpec(memory_space=pl.ANY)
    return pl.pallas_call(
        middle_kernel,
        in_specs=[far, far, far],
        out_specs=[far, pl.BlockSpec(memory_space=pltpu.VMEM)],
        out_shape=[rows_shape(rows, groups, count), jax.ShapeDtypeStruct((LANES, LANES), jnp.float32)],
        scratch_shapes=[
            pltpu.VMEM(images.shape, jnp.bfloat16),
            pltpu.VMEM(valid_mask.shape, jnp.int32),
            pltpu.VMEM((rows, groups, 2, count, LANES), jnp.bfloat16),
            pltpu.VMEM((2 * LANES, ROWS * groups * LANES), jnp.bfloat16),
            pltpu.SemaphoreType.DMA((ROWS + 1,)),
            pltpu.SemaphoreType.DMA((rows,)),
        ],
        compiler_params=pltpu.CompilerParams(vmem_limit_bytes=52 * 2**20),
        cost_estimate=pl.CostEstimate(flops=10**9, bytes_accessed=5 * 10**6, transcendentals=0),
        name="middle_rows",
    )(images, valid_mask, behind)


def added(terms):
    if len(terms) == 4:
        return (terms[0] + terms[2]) + (terms[1] + terms[3])
    return functools.reduce(jnp.add, terms)


def slab_values(terms):
    packed = added(terms)
    flipped = packed.T
    i = lax.broadcasted_iota(jnp.int32, packed.shape, 0)
    j = lax.broadcasted_iota(jnp.int32, packed.shape, 1)
    real = jnp.where(i <= j, packed, flipped)
    imag = jnp.where(i > j, packed, jnp.where(i < j, -flipped, 0.0))
    powers = jnp.where(i == j, packed, 0.0)
    scaled = jnp.sqrt(jnp.sum(powers, axis=1, keepdims=True) * jnp.sum(powers, axis=0, keepdims=True))
    return real / scaled, imag / scaled


INNER = (1, 2, 3, 4, 5)
HALVES = (
    ((-3, -2, -1, 0), (((1, 2, 3), None), (None, (-1, 0)))),
    ((6, 7, 8, 9), ((None, (6, 7)), ((3, 4, 5), None))),
)


def looks_kernel(half, aliased, terms, slab, *refs):
    other_ref, top_ref, mid_ref, low_ref = refs[:4]
    refs = refs[4 + aliased :]
    term_refs, refs = refs[:terms], refs[terms:]
    out_ref, extra_ref, w_ref = refs
    count = top_ref.shape[3]

    @pl.when(pl.program_id(0) == 0)
    def _():
        w_ref[...] = jnp.zeros_like(w_ref)
        if slab:
            real, imag = slab_values([t[...] for t in term_refs])
            extra_ref[0] = real[:count, :count]
            extra_ref[1] = imag[:count, :count]
        elif terms:
            extra_ref[...] = added([t[...] for t in term_refs])
        else:
            extra_ref[...] = jnp.zeros_like(extra_ref)

    rows = {}
    for r in range(ROWS):
        if r < AFTER:
            rows[r] = top_ref.at[r, 0]
        elif r >= ROWS - BEFORE:
            rows[r] = low_ref.at[r - (ROWS - BEFORE), 0]
        else:
            rows[r] = mid_ref.at[r - AFTER, 0]
    for r in range(other_ref.shape[0]):
        rows[ROWS + r if half else r - BEFORE] = other_ref.at[r, 0]

    lane = lax.broadcasted_iota(jnp.int32, (1, LANES), 1)

    def lanes_of(turn):
        place = lane + (-LOOK * turn) % LANES
        place = jnp.where(place >= LANES, place - LANES, place)
        return place < LOOK

    def widened(which):
        return jnp.broadcast_to(which.astype(jnp.float32), (count, LANES)).astype(jnp.bfloat16) != 0

    single = [lanes_of(t) for t in range(2 * PER - 1)]
    wide = [widened(s) for s in single]

    def turn(l, r):
        return l + SKEW[r % ROWS]

    def gathered(l, k, which):
        out = rows[which[0]][k]
        for r in which[1:]:
            out = jnp.where(wide[turn(l, r)], rows[r][k], out)
        return out

    def kept(l, which):
        select = single[turn(l, which[0])]
        for r in which[1:]:
            select = select | single[turn(l, r)]
        return select.astype(jnp.float32)

    eight = (8, LANES)
    along = lax.broadcasted_iota(jnp.int32, eight, 1)
    on_eye = along % 8 == lax.broadcasted_iota(jnp.int32, eight, 0)
    block = along // 8

    def normalised(real, imag, w, l):
        picked = real[:8]
        for v in range(1, count // 8):
            picked = jnp.where(block == v, real[8 * v : 8 * v + 8], picked)
        power = jnp.sum(jnp.where(on_eye, picked, 0.0), axis=0, keepdims=True)
        across = lax.rsqrt(jnp.maximum(power, floor_power))
        diagonal = jnp.where(on_eye, across, 0.0)
        spread = jnp.concatenate([jnp.where(block == v, diagonal, 0.0) for v in range(count // 8)], axis=0)
        scale = jnp.sum(spread, axis=1, keepdims=True) * across
        out_ref[w, l, 0] = (real * scale).astype(jnp.bfloat16)[:, :count]
        out_ref[w, l, 1] = (imag * scale).astype(jnp.bfloat16)[:, :count]

    outer_rows, windows = HALVES[half]
    for l in range(PER):
        slot = l % 2
        for k in range(2):
            w_ref[slot, k, pl.ds(0, count), pl.ds(0, LANES)] = gathered(l, k, INNER)
            w_ref[slot, k, pl.ds(0, count), pl.ds(LANES, LANES)] = gathered(l, k, outer_rows)
        every = w_ref[slot].reshape(2 * LANES, 2 * LANES)
        nothing = jnp.zeros_like(every)
        reads = []
        for inner_rows, rest_rows in windows:
            lanes = jnp.concatenate([kept(l, inner_rows or INNER), kept(l, rest_rows or outer_rows)], axis=1)
            lanes = jnp.broadcast_to(lanes, every.shape).astype(jnp.bfloat16) != 0
            read = jnp.where(lanes, every, nothing)
            for start in range(0, LANES, TILE):
                reads.append(read[start : start + TILE])
                reads.append(read[LANES + start : LANES + start + TILE])
        gram = lax.dot_general(jnp.concatenate(reads, axis=0), every, NT, preferred_element_type=jnp.float32)
        for w in range(2):
            real, imag = [], []
            for start in range(0, LANES, TILE):
                base = 2 * (w * LANES + start)
                re, im = gram[base : base + TILE], gram[base + TILE : base + 2 * TILE]
                real.append(re[:, :LANES] + im[:, LANES:])
                imag.append(im[:, :LANES] - re[:, LANES:])
            normalised(jnp.concatenate(real, axis=0)[:count], jnp.concatenate(imag, axis=0)[:count], w, l)


def looked(half, other, top, mid, low, first, groups, looks, previous, terms, slab):
    count = other.shape[3]

    def spec(array):
        return pl.BlockSpec((array.shape[0], 1) + array.shape[2:], lambda s: (0, s + first, 0, 0, 0))

    operands = [other, top, mid, low]
    in_specs = [spec(a) for a in operands]
    aliases = {}
    if previous is not None:
        aliases = {len(operands): 0}
        operands.append(previous)
        in_specs.append(pl.BlockSpec(memory_space=pl.ANY))
    for term in terms:
        operands.append(term)
        in_specs.append(pl.BlockSpec(term.shape, lambda s: (0, 0)))
    extra = (2, count, count) if slab else (LANES, LANES)
    out_specs = [
        pl.BlockSpec((2, PER, 2, count, count), lambda s: (half, s + first, 0, 0, 0)),
        pl.BlockSpec(extra, lambda s: (0,) * len(extra)),
    ]
    out_shape = [
        jax.ShapeDtypeStruct((ROWS // 2, looks, 2, count, count), jnp.bfloat16),
        jax.ShapeDtypeStruct(extra, jnp.float32),
    ]
    return pl.pallas_call(
        functools.partial(looks_kernel, half, previous is not None, len(terms), slab),
        grid=(groups,),
        in_specs=in_specs,
        out_specs=out_specs,
        out_shape=out_shape,
        input_output_aliases=aliases,
        scratch_shapes=[
            pltpu.VMEM((2, 2, LANES, 2 * LANES), jnp.bfloat16),
        ],
        compiler_params=pltpu.CompilerParams(vmem_limit_bytes=48 * 2**20),
        cost_estimate=pl.CostEstimate(
            flops=20 * groups * PER * 2 * 512 * 256 * 256, bytes_accessed=groups * 10**6, transcendentals=0
        ),
        name="looks",
    )(*operands)


def rounds(size):
    found = []
    stride = 1
    while stride < size:
        radix = 4 if size // stride % 4 == 0 else 2
        if size // stride % radix:
            return None
        found.append((stride, radix))
        stride *= radix
    return found[::-1]


def round_terms(value, axis, stride, radix):
    size = lax.axis_size(axis)
    terms = [value]
    for shift in range(1, radix):
        pairs = []
        for i in range(size):
            place = (i // stride) % radix
            pairs.append((i, i + ((place + shift) % radix - place) * stride))
        terms.append(lax.ppermute(value, axis, pairs))
    return terms


def shards(images, valid_mask):
    looks = images.shape[3] // LOOK
    groups = -(-looks // PER)
    cut = -(-groups // 2)
    size = lax.axis_size("pix")
    forward = [(i, i + 1) for i in range(size - 1)]
    backward = [(i + 1, i) for i in range(size - 1)]
    top, low, edge_done = edge_rows(images, valid_mask, groups)
    after = lax.ppermute(top, "pix", backward)
    before = lax.ppermute(low, "pix", forward)
    mid, total = middle_rows(images, valid_mask, groups, edge_done)
    steps = rounds(size)
    if steps is None:
        terms, steps = [lax.psum(total, "pix")], []
    else:
        terms = round_terms(total, "pix", *steps[0]) if steps else [total]
    out, zeros = looked(1, after, top, mid, low, 0, groups, looks, None, [], False)
    for step in steps[1:]:
        terms = round_terms(added(terms) + zeros, "pix", *step)
    out, _ = looked(0, before, top, mid, low, 0, cut, looks, out, [], False)
    out, slab = looked(0, before, top, mid, low, cut, groups - cut, looks, out, terms, True)
    return (out, slab)


def solution(mesh):
    in_specs = (P(("group", "pix"), None, None, None), P(("group", "pix"), None))
    out_specs = (P(("group", "pix"), None, None, None, None), P("group", None, None))
    return jax.shard_map(shards, mesh=mesh, in_specs=in_specs, out_specs=out_specs, check_vma=False)
```

```python
import functools
import jax
import jax.numpy as jnp
from jax import lax
from jax.experimental import pallas as pl
from jax.experimental.pallas import tpu as pltpu
from jax.sharding import PartitionSpec as P

floor_power = 30.0

LOOK = 21
LANES = 128
TILE = 16
PER = LANES // LOOK
SPAN = PER * LOOK
ROWS = 8
SKEW = (5, 0, 1, 2, 3, 4, 1, 2)
BEFORE, AFTER = 3, 2
NT = (((1,), (1,)), ((), ()))


def turned(image, mask, skew, columns, put):
    count = image[0].shape[0]
    zero = jnp.zeros((count, LANES), jnp.bfloat16)
    lane = lax.broadcasted_iota(jnp.int32, (1, LANES), 1)

    def tile(value, g):
        start, stop = g * LANES, min((g + 1) * LANES, columns)
        part = value[:, start:stop]
        if stop - start < LANES:
            rest = jnp.zeros((part.shape[0], LANES - (stop - start)), part.dtype)
            part = jnp.concatenate([part, rest], axis=1)
        return part

    def widened(which):
        return jnp.broadcast_to(which.astype(jnp.float32), (count, LANES)).astype(jnp.bfloat16) != 0

    tiles = -(-columns // LANES)
    for g in range(-(-columns // SPAN)):
        slide = (LANES - SPAN) * g
        place = (lane + slide) % LANES
        used = (place < SPAN) & (SPAN * g + place < columns)
        prior = lane >= LANES - slide
        sides = [t for t in (g - 1, g) if 0 <= t < tiles]

        def joined(value):
            parts = [tile(value, t) for t in sides]
            if len(parts) == 1:
                return parts[0]
            which = prior if value.shape[0] == 1 else widened(prior)
            return jnp.where(which, parts[0], parts[1])

        keep = widened(used & (joined(mask) != 0))
        for k in range(2):
            row = jnp.where(keep, joined(image[k]), zero)
            put(g, k, pltpu.roll(row, slide + LOOK * skew, 1))


def fetched(image_ref, mask_ref, rows_ref, masks_ref, sems, order):
    mask_copy = pltpu.make_async_copy(mask_ref, masks_ref, sems.at[len(order)])
    mask_copy.start()
    copies = [pltpu.make_async_copy(image_ref.at[row], rows_ref.at[at], sems.at[at]) for at, row in enumerate(order)]
    for copy in copies:
        copy.start()
    mask_copy.wait()
    return copies


EDGE = tuple(range(AFTER)) + tuple(range(ROWS - BEFORE, ROWS))


def edge_kernel(cut, image_ref, mask_ref, top_ref, low0_ref, low1_ref, rows_ref, masks_ref, turned_ref, in_sems, out_sems):
    fetches = fetched(image_ref, mask_ref, rows_ref, masks_ref, in_sems, EDGE)
    stores = []
    for at, row in enumerate(EDGE):
        fetches[at].wait()

        def put(g, k, value):
            turned_ref[at, g, k] = value

        turned([rows_ref.at[at, 0], rows_ref.at[at, 1]], masks_ref[row : row + 1, :], SKEW[row], masks_ref.shape[1], put)
        groups = turned_ref.shape[1]
        i = row - (ROWS - BEFORE)
        if row < AFTER:
            targets = ((top_ref.at[row], 0, groups),)
        else:
            targets = ((low0_ref.at[i], 0, cut), (low1_ref.at[i], cut, groups))
        for target, start, stop in targets:
            store = pltpu.make_async_copy(turned_ref.at[at, start:stop], target, out_sems.at[len(stores)])
            store.start()
            stores.append(store)
    for store in stores:
        store.wait()


def rows_shape(rows, groups, count):
    return jax.ShapeDtypeStruct((rows, groups, 2, count, LANES), jnp.bfloat16)


def edge_rows(images, valid_mask, groups, cut):
    count = images.shape[2]
    far = pl.BlockSpec(memory_space=pl.ANY)
    return pl.pallas_call(
        functools.partial(edge_kernel, cut),
        in_specs=[far, far],
        out_specs=[far] * 3,
        out_shape=[
            rows_shape(AFTER, groups, count),
            rows_shape(BEFORE, cut, count),
            rows_shape(BEFORE, groups - cut, count),
        ],
        scratch_shapes=[
            pltpu.VMEM((len(EDGE),) + images.shape[1:], jnp.bfloat16),
            pltpu.VMEM(valid_mask.shape, jnp.int32),
            pltpu.VMEM((len(EDGE), groups, 2, count, LANES), jnp.bfloat16),
            pltpu.SemaphoreType.DMA((len(EDGE) + 1,)),
            pltpu.SemaphoreType.DMA((AFTER + 2 * BEFORE,)),
        ],
        compiler_params=pltpu.CompilerParams(vmem_limit_bytes=61 * 2**20),
        cost_estimate=pl.CostEstimate(flops=10**6, bytes_accessed=4 * 10**6, transcendentals=0),
        name="edge_rows",
    )(images, valid_mask)


def local_kernel(image_ref, mask_ref, all_ref, gram_ref, rows_ref, masks_ref, turned_ref, z_ref, in_sems, out_sems):
    groups = all_ref.shape[1]
    count, columns = image_ref.shape[2:]
    fetches = fetched(image_ref, mask_ref, rows_ref, masks_ref, in_sems, range(ROWS))
    z_ref[...] = jnp.zeros_like(z_ref)
    stores = []
    total = None
    wide = groups * LANES
    for row in range(ROWS):
        fetches[row].wait()

        def put(g, k, value):
            turned_ref[row, g, k] = value
            z_ref[pl.ds(k * LANES, count), pl.ds(row * wide + g * LANES, LANES)] = value

        turned([rows_ref.at[row, 0], rows_ref.at[row, 1]], masks_ref[row : row + 1, :], SKEW[row], columns, put)
        store = pltpu.make_async_copy(turned_ref.at[row], all_ref.at[row], out_sems.at[row])
        store.start()
        stores.append(store)
        if row % 2:
            z = z_ref[:, pl.ds((row - 1) * wide, 2 * wide)]
            part = lax.dot_general(z, z, NT, preferred_element_type=jnp.float32)
            total = part if total is None else total + part
    real = total[:LANES, :LANES] + total[LANES:, LANES:]
    imag = total[LANES:, :LANES] - total[:LANES, LANES:]
    i = lax.broadcasted_iota(jnp.int32, real.shape, 0)
    j = lax.broadcasted_iota(jnp.int32, real.shape, 1)
    gram_ref[...] = jnp.where(i <= j, real, imag)
    for store in stores:
        store.wait()


def local_rows(images, valid_mask, groups):
    count = images.shape[2]
    far = pl.BlockSpec(memory_space=pl.ANY)
    return pl.pallas_call(
        local_kernel,
        in_specs=[far, far],
        out_specs=[far, pl.BlockSpec(memory_space=pltpu.VMEM)],
        out_shape=[rows_shape(ROWS, groups, count), jax.ShapeDtypeStruct((LANES, LANES), jnp.float32)],
        scratch_shapes=[
            pltpu.VMEM(images.shape, jnp.bfloat16),
            pltpu.VMEM(valid_mask.shape, jnp.int32),
            pltpu.VMEM((ROWS, groups, 2, count, LANES), jnp.bfloat16),
            pltpu.VMEM((2 * LANES, ROWS * groups * LANES), jnp.bfloat16),
            pltpu.SemaphoreType.DMA((ROWS + 1,)),
            pltpu.SemaphoreType.DMA((ROWS,)),
        ],
        compiler_params=pltpu.CompilerParams(vmem_limit_bytes=50 * 2**20),
        cost_estimate=pl.CostEstimate(flops=10**9, bytes_accessed=5 * 10**6, transcendentals=0),
        name="local_rows",
    )(images, valid_mask)


def added(terms):
    if len(terms) == 4:
        return (terms[0] + terms[2]) + (terms[1] + terms[3])
    return functools.reduce(jnp.add, terms)


def slab_values(terms):
    packed = added(terms)
    flipped = packed.T
    i = lax.broadcasted_iota(jnp.int32, packed.shape, 0)
    j = lax.broadcasted_iota(jnp.int32, packed.shape, 1)
    real = jnp.where(i <= j, packed, flipped)
    imag = jnp.where(i > j, packed, jnp.where(i < j, -flipped, 0.0))
    powers = jnp.where(i == j, packed, 0.0)
    scaled = jnp.sqrt(jnp.sum(powers, axis=1, keepdims=True) * jnp.sum(powers, axis=0, keepdims=True))
    return real / scaled, imag / scaled


INNER = (1, 2, 3, 4, 5)
HALVES = (
    ((-3, -2, -1, 0), (((1, 2, 3), None), (None, (-1, 0)))),
    ((6, 7, 8, 9), ((None, (6, 7)), ((3, 4, 5), None))),
)


def looks_kernel(half, aliased, terms, slab, *refs):
    other_ref, all_ref = refs[:2]
    refs = refs[2 + aliased :]
    term_refs, refs = refs[:terms], refs[terms:]
    out_ref, extra_ref, w_ref, g_ref = refs
    count = all_ref.shape[3]

    @pl.when(pl.program_id(0) == 0)
    def _():
        w_ref[...] = jnp.zeros_like(w_ref)
        if slab:
            real, imag = slab_values([t[...] for t in term_refs])
            extra_ref[0] = real[:count, :count]
            extra_ref[1] = imag[:count, :count]
        elif terms:
            extra_ref[...] = added([t[...] for t in term_refs])
        else:
            extra_ref[...] = jnp.zeros_like(extra_ref)

    rows = {r: all_ref.at[r, 0] for r in range(ROWS)}
    for r in range(other_ref.shape[0]):
        rows[ROWS + r if half else r - BEFORE] = other_ref.at[r, 0]

    lane = lax.broadcasted_iota(jnp.int32, (1, LANES), 1)

    def lanes_of(turn):
        place = lane + (-LOOK * turn) % LANES
        place = jnp.where(place >= LANES, place - LANES, place)
        return place < LOOK

    def widened(which):
        return jnp.broadcast_to(which.astype(jnp.float32), (count, LANES)).astype(jnp.bfloat16) != 0

    single = [lanes_of(t) for t in range(2 * PER - 1)]
    wide = [widened(s) for s in single]

    def turn(l, r):
        return l + SKEW[r % ROWS]

    def gathered(l, k, which):
        out = rows[which[0]][k]
        for r in which[1:]:
            out = jnp.where(wide[turn(l, r)], rows[r][k], out)
        return out

    def kept(l, which):
        select = single[turn(l, which[0])]
        for r in which[1:]:
            select = select | single[turn(l, r)]
        return select.astype(jnp.float32)

    eight = (8, LANES)
    along = lax.broadcasted_iota(jnp.int32, eight, 1)
    on_eye = along % 8 == lax.broadcasted_iota(jnp.int32, eight, 0)
    block = along // 8

    outer_rows, windows = HALVES[half]

    def products(l):
        slot = l % 2
        for k in range(2):
            w_ref[slot, k, pl.ds(0, count), pl.ds(0, LANES)] = gathered(l, k, INNER)
            w_ref[slot, k, pl.ds(0, count), pl.ds(LANES, LANES)] = gathered(l, k, outer_rows)
        every = w_ref[slot].reshape(2 * LANES, 2 * LANES)
        nothing = jnp.zeros_like(every)
        reads = []
        for inner_rows, rest_rows in windows:
            lanes = jnp.concatenate([kept(l, inner_rows or INNER), kept(l, rest_rows or outer_rows)], axis=1)
            lanes = jnp.broadcast_to(lanes, every.shape).astype(jnp.bfloat16) != 0
            read = jnp.where(lanes, every, nothing)
            for start in range(0, LANES, TILE):
                reads.append(read[start : start + TILE])
                reads.append(read[LANES + start : LANES + start + TILE])
        gram = lax.dot_general(jnp.concatenate(reads, axis=0), every, NT, preferred_element_type=jnp.float32)
        for w in range(2):
            for start in range(0, LANES, TILE):
                base = 2 * (w * LANES + start)
                re, im = gram[base : base + TILE], gram[base + TILE : base + 2 * TILE]
                g_ref[slot, w, 0, pl.ds(start, TILE)] = re[:, :LANES] + im[:, LANES:]
                g_ref[slot, w, 1, pl.ds(start, TILE)] = im[:, :LANES] - re[:, LANES:]

    def normalised(l):
        for w in range(2):
            real, imag = g_ref.at[l % 2, w, 0], g_ref.at[l % 2, w, 1]
            picked = real[0:8]
            for v in range(1, count // 8):
                picked = jnp.where(block == v, real[8 * v : 8 * v + 8], picked)
            power = jnp.sum(jnp.where(on_eye, picked, 0.0), axis=0, keepdims=True)
            across = lax.rsqrt(jnp.maximum(power, floor_power))
            diagonal = jnp.where(on_eye, across, 0.0)
            spread = jnp.concatenate([jnp.where(block == v, diagonal, 0.0) for v in range(count // 8)], axis=0)
            scale = jnp.sum(spread, axis=1, keepdims=True) * across
            out_ref[w, l, 0] = (real[0:count] * scale).astype(jnp.bfloat16)[:, :count]
            out_ref[w, l, 1] = (imag[0:count] * scale).astype(jnp.bfloat16)[:, :count]

    products(0)
    for l in range(PER):
        if l + 1 < PER:
            products(l + 1)
        normalised(l)


def looked(half, other, rows, first, groups, looks, previous, terms, slab):
    count = other.shape[3]

    def spec(array):
        offset = 0 if array is other else first
        return pl.BlockSpec((array.shape[0], 1) + array.shape[2:], lambda s: (0, s + offset, 0, 0, 0))

    operands = [other, rows]
    in_specs = [spec(a) for a in operands]
    aliases = {}
    if previous is not None:
        aliases = {len(operands): 0}
        operands.append(previous)
        in_specs.append(pl.BlockSpec(memory_space=pl.ANY))
    for term in terms:
        operands.append(term)
        in_specs.append(pl.BlockSpec(term.shape, lambda s: (0, 0)))
    extra = (2, count, count) if slab else (LANES, LANES)
    out_specs = [
        pl.BlockSpec((2, PER, 2, count, count), lambda s: (half, s + first, 0, 0, 0)),
        pl.BlockSpec(extra, lambda s: (0,) * len(extra)),
    ]
    out_shape = [
        jax.ShapeDtypeStruct((ROWS // 2, looks, 2, count, count), jnp.bfloat16),
        jax.ShapeDtypeStruct(extra, jnp.float32),
    ]
    return pl.pallas_call(
        functools.partial(looks_kernel, half, previous is not None, len(terms), slab),
        grid=(groups,),
        in_specs=in_specs,
        out_specs=out_specs,
        out_shape=out_shape,
        input_output_aliases=aliases,
        scratch_shapes=[
            pltpu.VMEM((2, 2, LANES, 2 * LANES), jnp.bfloat16),
            pltpu.VMEM((2, 2, 2, LANES, LANES), jnp.float32),
        ],
        compiler_params=pltpu.CompilerParams(vmem_limit_bytes=49 * 2**20),
        cost_estimate=pl.CostEstimate(
            flops=1 * groups * PER * 2 * 512 * 256 * 256, bytes_accessed=groups * 10**6, transcendentals=0
        ),
        name="looks",
    )(*operands)


def rounds(size):
    found = []
    stride = 1
    while stride < size:
        radix = 4 if size // stride % 4 == 0 else 2
        if size // stride % radix:
            return None
        found.append((stride, radix))
        stride *= radix
    return found[::-1]


def round_terms(value, axis, stride, radix):
    size = lax.axis_size(axis)
    terms = [value]
    for shift in range(1, radix):
        pairs = []
        for i in range(size):
            place = (i // stride) % radix
            pairs.append((i, i + ((place + shift) % radix - place) * stride))
        terms.append(lax.ppermute(value, axis, pairs))
    return terms


def shards(images, valid_mask):
    looks = images.shape[3] // LOOK
    groups = -(-looks // PER)
    cut = -(-groups // 2)
    size = lax.axis_size("pix")
    forward = [(i, i + 1) for i in range(size - 1)]
    backward = [(i + 1, i) for i in range(size - 1)]
    top, low0, low1 = edge_rows(images, valid_mask, groups, cut)
    after = lax.ppermute(top, "pix", backward)
    before0 = lax.ppermute(low0, "pix", forward)
    before1 = lax.ppermute(low1, "pix", forward)
    rows, total = local_rows(images, valid_mask, groups)
    steps = rounds(size)
    if steps is None:
        terms, steps = [lax.psum(total, "pix")], []
    else:
        terms = round_terms(total, "pix", *steps[0]) if steps else [total]
    out, zeros = looked(1, after, rows, 0, groups, looks, None, [], False)
    for step in steps[1:]:
        terms = round_terms(added(terms) + zeros, "pix", *step)
    out, _ = looked(0, before0, rows, 0, cut, looks, out, [], False)
    out, slab = looked(0, before1, rows, cut, groups - cut, looks, out, terms, True)
    return (out, slab)


def solution(mesh):
    in_specs = (P(("group", "pix"), None, None, None), P(("group", "pix"), None))
    out_specs = (P(("group", "pix"), None, None, None, None), P("group", None, None))
    return jax.shard_map(shards, mesh=mesh, in_specs=in_specs, out_specs=out_specs, check_vma=False)
```

```python
import functools
import jax
import jax.numpy as jnp
from jax import lax
from jax.experimental import pallas as pl
from jax.experimental.pallas import tpu as pltpu
from jax.sharding import PartitionSpec as P

floor_power = 30.0

LOOK = 21
LANES = 128
TILE = 16
PER = LANES // LOOK
SPAN = PER * LOOK
ROWS = 8
SKEW = (5, 0, 1, 2, 3, 4, 1, 2)
BEFORE, AFTER = 3, 2


def turned(image, mask, skew, columns, put):
    count = image[0].shape[0]
    zero = jnp.zeros((count, LANES), jnp.bfloat16)
    lane = lax.broadcasted_iota(jnp.int32, (1, LANES), 1)

    def tile(value, g):
        start, stop = g * LANES, min((g + 1) * LANES, columns)
        part = value[:, start:stop]
        if stop - start < LANES:
            rest = jnp.zeros((part.shape[0], LANES - (stop - start)), part.dtype)
            part = jnp.concatenate([part, rest], axis=1)
        return part

    def widened(which):
        return jnp.broadcast_to(which.astype(jnp.float32), (count, LANES)).astype(jnp.bfloat16) != 0

    tiles = -(-columns // LANES)
    for g in range(-(-columns // SPAN)):
        slide = (LANES - SPAN) * g
        place = (lane + slide) % LANES
        used = (place < SPAN) & (SPAN * g + place < columns)
        prior = lane >= LANES - slide
        sides = [t for t in (g - 1, g) if 0 <= t < tiles]

        def joined(value):
            parts = [tile(value, t) for t in sides]
            if len(parts) == 1:
                return parts[0]
            which = prior if value.shape[0] == 1 else widened(prior)
            return jnp.where(which, parts[0], parts[1])

        keep = widened(used & (joined(mask) != 0))
        for k in range(2):
            row = jnp.where(keep, joined(image[k]), zero)
            put(g, k, pltpu.roll(row, slide + LOOK * skew, 1))


def fetched(image_ref, mask_ref, rows_ref, masks_ref, sems, order):
    mask_copy = pltpu.make_async_copy(mask_ref, masks_ref, sems.at[len(order)])
    mask_copy.start()
    copies = [pltpu.make_async_copy(image_ref.at[row], rows_ref.at[at], sems.at[at]) for at, row in enumerate(order)]
    for copy in copies:
        copy.start()
    mask_copy.wait()
    return copies


EDGE = tuple(range(AFTER)) + tuple(range(ROWS - BEFORE, ROWS))


def edge_kernel(cut, image_ref, mask_ref, top_ref, low0_ref, low1_ref, rows_ref, masks_ref, turned_ref, in_sems, out_sems):
    fetches = fetched(image_ref, mask_ref, rows_ref, masks_ref, in_sems, EDGE)
    stores = []
    for at, row in enumerate(EDGE):
        fetches[at].wait()

        def put(g, k, value):
            turned_ref[at, g, k] = value

        turned([rows_ref.at[at, 0], rows_ref.at[at, 1]], masks_ref[row : row + 1, :], SKEW[row], masks_ref.shape[1], put)
        groups = turned_ref.shape[1]
        i = row - (ROWS - BEFORE)
        if row < AFTER:
            targets = ((top_ref.at[row], 0, groups),)
        else:
            targets = ((low0_ref.at[i], 0, cut), (low1_ref.at[i], cut, groups))
        for target, start, stop in targets:
            store = pltpu.make_async_copy(turned_ref.at[at, start:stop], target, out_sems.at[len(stores)])
            store.start()
            stores.append(store)
    for store in stores:
        store.wait()


def rows_shape(rows, groups, count):
    return jax.ShapeDtypeStruct((rows, groups, 2, count, LANES), jnp.bfloat16)


def edge_rows(images, valid_mask, groups, cut):
    count = images.shape[2]
    far = pl.BlockSpec(memory_space=pl.ANY)
    return pl.pallas_call(
        functools.partial(edge_kernel, cut),
        in_specs=[far, far],
        out_specs=[far] * 3,
        out_shape=[
            rows_shape(AFTER, groups, count),
            rows_shape(BEFORE, cut, count),
            rows_shape(BEFORE, groups - cut, count),
        ],
        scratch_shapes=[
            pltpu.VMEM((len(EDGE),) + images.shape[1:], jnp.bfloat16),
            pltpu.VMEM(valid_mask.shape, jnp.int32),
            pltpu.VMEM((len(EDGE), groups, 2, count, LANES), jnp.bfloat16),
            pltpu.SemaphoreType.DMA((len(EDGE) + 1,)),
            pltpu.SemaphoreType.DMA((AFTER + 2 * BEFORE,)),
        ],
        compiler_params=pltpu.CompilerParams(vmem_limit_bytes=61 * 2**20),
        cost_estimate=pl.CostEstimate(flops=10**6, bytes_accessed=4 * 10**6, transcendentals=0),
        name="edge_rows",
    )(images, valid_mask)


def local_kernel(image_ref, mask_ref, all_ref, gram_ref, rows_ref, masks_ref, y_ref, in_sems, out_sems):
    groups = all_ref.shape[1]
    count, columns = image_ref.shape[2:]
    fetches = fetched(image_ref, mask_ref, rows_ref, masks_ref, in_sems, range(ROWS))
    rest = LANES - count
    y_ref[:, :, 0:2, pl.ds(count, rest), :] = jnp.zeros((ROWS, groups, 2, rest, LANES), jnp.bfloat16)
    stores = []
    total = None
    for row in range(ROWS):
        fetches[row].wait()

        def put(g, k, value):
            y_ref[row, g, k, pl.ds(0, count), :] = value

        turned([rows_ref.at[row, 0], rows_ref.at[row, 1]], masks_ref[row : row + 1, :], SKEW[row], columns, put)
        for g in range(groups):
            for k in range(2):
                y_ref[row, g, 2 + k] = y_ref[row, g, k].T
        store = pltpu.make_async_copy(y_ref.at[row], all_ref.at[row], out_sems.at[row])
        store.start()
        stores.append(store)
        left = [y_ref[row, g, 0:2].reshape(2 * LANES, LANES) for g in range(groups)]
        right = [jnp.concatenate([y_ref[row, g, 2], y_ref[row, g, 3]], axis=1) for g in range(groups)]
        left, right = jnp.concatenate(left, axis=1), jnp.concatenate(right, axis=0)
        part = jnp.dot(left, right, preferred_element_type=jnp.float32)
        total = part if total is None else total + part
    real = total[:LANES, :LANES] + total[LANES:, LANES:]
    imag = total[LANES:, :LANES] - total[:LANES, LANES:]
    i = lax.broadcasted_iota(jnp.int32, real.shape, 0)
    j = lax.broadcasted_iota(jnp.int32, real.shape, 1)
    gram_ref[...] = jnp.where(i <= j, real, imag)
    for copy in stores:
        copy.wait()


def local_rows(images, valid_mask, groups):
    far = pl.BlockSpec(memory_space=pl.ANY)
    shape = (ROWS, groups, 4, LANES, LANES)
    return pl.pallas_call(
        local_kernel,
        in_specs=[far, far],
        out_specs=[far, pl.BlockSpec(memory_space=pltpu.VMEM)],
        out_shape=[jax.ShapeDtypeStruct(shape, jnp.bfloat16), jax.ShapeDtypeStruct((LANES, LANES), jnp.float32)],
        scratch_shapes=[
            pltpu.VMEM(images.shape, jnp.bfloat16),
            pltpu.VMEM(valid_mask.shape, jnp.int32),
            pltpu.VMEM(shape, jnp.bfloat16),
            pltpu.SemaphoreType.DMA((ROWS + 1,)),
            pltpu.SemaphoreType.DMA((ROWS,)),
        ],
        compiler_params=pltpu.CompilerParams(vmem_limit_bytes=40 * 2**20),
        cost_estimate=pl.CostEstimate(flops=10**9, bytes_accessed=5 * 10**6, transcendentals=0),
        name="local_rows",
    )(images, valid_mask)


def added(terms):
    if len(terms) == 4:
        return (terms[0] + terms[2]) + (terms[1] + terms[3])
    return functools.reduce(jnp.add, terms)


def slab_values(terms):
    packed = added(terms)
    flipped = packed.T
    i = lax.broadcasted_iota(jnp.int32, packed.shape, 0)
    j = lax.broadcasted_iota(jnp.int32, packed.shape, 1)
    real = jnp.where(i <= j, packed, flipped)
    imag = jnp.where(i > j, packed, jnp.where(i < j, -flipped, 0.0))
    powers = jnp.where(i == j, packed, 0.0)
    scaled = jnp.sqrt(jnp.sum(powers, axis=1, keepdims=True) * jnp.sum(powers, axis=0, keepdims=True))
    return real / scaled, imag / scaled


INNER = (1, 2, 3, 4, 5)
HALVES = (
    ((-3, -2, -1, 0), (((1, 2, 3), None), (None, (-1, 0)))),
    ((6, 7, 8, 9), ((None, (6, 7)), ((3, 4, 5), None))),
)


def looks_kernel(half, aliased, terms, slab, *refs):
    other_ref, all_ref = refs[:2]
    refs = refs[2 + aliased :]
    term_refs, refs = refs[:terms], refs[terms:]
    out_ref, extra_ref, w_ref, g_ref, h_ref = refs
    count = other_ref.shape[3]

    @pl.when(pl.program_id(0) == 0)
    def _():
        h_ref[...] = jnp.zeros_like(h_ref)
        if slab:
            real, imag = slab_values([t[...] for t in term_refs])
            extra_ref[0] = real[:count, :count]
            extra_ref[1] = imag[:count, :count]
        elif terms:
            extra_ref[...] = added([t[...] for t in term_refs])
        else:
            extra_ref[...] = jnp.zeros_like(extra_ref)

    rows = {r: all_ref.at[r, 0] for r in range(ROWS)}
    for r in range(other_ref.shape[0]):
        for k in range(2):
            h_ref[r, k, pl.ds(0, count), :] = other_ref[r, 0, k]
            h_ref[r, 2 + k] = h_ref[r, k].T
        rows[ROWS + r if half else r - BEFORE] = h_ref.at[r]

    lane = lax.broadcasted_iota(jnp.int32, (1, LANES), 1)

    def lanes_of(turn):
        place = lane + (-LOOK * turn) % LANES
        place = jnp.where(place >= LANES, place - LANES, place)
        return place < LOOK

    def widened(which):
        return jnp.broadcast_to(which.astype(jnp.float32), (LANES, LANES)).astype(jnp.bfloat16) != 0

    single = [lanes_of(t) for t in range(2 * PER - 1)]
    wide = [widened(s) for s in single]

    def turn(l, r):
        return l + SKEW[r % ROWS]

    def gathered(l, k, which):
        out = rows[which[0]][k]
        for r in which[1:]:
            out = jnp.where(wide[turn(l, r)], rows[r][k], out)
        return out

    def kept(l, which):
        select = single[turn(l, which[0])]
        for r in which[1:]:
            select = select | single[turn(l, r)]
        return select.astype(jnp.float32)

    across_tile = lax.broadcasted_iota(jnp.int32, (TILE, 2 * LANES), 0).astype(jnp.float32).astype(jnp.bfloat16)

    def tall(r, start):
        return jnp.concatenate([rows[r][2, start : start + TILE], rows[r][3, start : start + TILE]], axis=1)

    def stacked(l, which):
        owners = [None] * LANES
        for r in which:
            for q in range(LOOK):
                owners[(LOOK * turn(l, r) + q) % LANES] = r
        tiles = []
        for start in range(0, LANES, TILE):
            here = owners[start : start + TILE]
            found = [r for r in dict.fromkeys(here) if r is not None] or [which[0]]
            value = tall(found[0], start)
            for r in found[1:]:
                value = jnp.where(across_tile < here.index(r), value, tall(r, start))
            tiles.append(value)
        return tiles

    eight = (8, LANES)
    along = lax.broadcasted_iota(jnp.int32, eight, 1)
    on_eye = along % 8 == lax.broadcasted_iota(jnp.int32, eight, 0)
    block = along // 8

    outer_rows, windows = HALVES[half]

    def products(l):
        slot = l % 2
        for k in range(2):
            w_ref[slot, k, :, pl.ds(0, LANES)] = gathered(l, k, INNER)
            w_ref[slot, k, :, pl.ds(LANES, LANES)] = gathered(l, k, outer_rows)
        every = w_ref[slot].reshape(2 * LANES, 2 * LANES)
        nothing = jnp.zeros_like(every)
        reads = []
        for inner_rows, rest_rows in windows:
            lanes = jnp.concatenate([kept(l, inner_rows or INNER), kept(l, rest_rows or outer_rows)], axis=1)
            lanes = jnp.broadcast_to(lanes, every.shape).astype(jnp.bfloat16) != 0
            read = jnp.where(lanes, every, nothing)
            for start in range(0, LANES, TILE):
                reads.append(read[start : start + TILE])
                reads.append(read[LANES + start : LANES + start + TILE])
        right = jnp.concatenate(stacked(l, INNER) + stacked(l, outer_rows), axis=0)
        gram = jnp.dot(jnp.concatenate(reads, axis=0), right, preferred_element_type=jnp.float32)
        for w in range(2):
            for start in range(0, LANES, TILE):
                base = 2 * (w * LANES + start)
                re, im = gram[base : base + TILE], gram[base + TILE : base + 2 * TILE]
                g_ref[slot, w, 0, pl.ds(start, TILE)] = re[:, :LANES] + im[:, LANES:]
                g_ref[slot, w, 1, pl.ds(start, TILE)] = im[:, :LANES] - re[:, LANES:]

    def normalised(l):
        for w in range(2):
            real, imag = g_ref.at[l % 2, w, 0], g_ref.at[l % 2, w, 1]
            picked = real[0:8]
            for v in range(1, count // 8):
                picked = jnp.where(block == v, real[8 * v : 8 * v + 8], picked)
            power = jnp.sum(jnp.where(on_eye, picked, 0.0), axis=0, keepdims=True)
            across = lax.rsqrt(jnp.maximum(power, floor_power))
            diagonal = jnp.where(on_eye, across, 0.0)
            spread = jnp.concatenate([jnp.where(block == v, diagonal, 0.0) for v in range(count // 8)], axis=0)
            scale = jnp.sum(spread, axis=1, keepdims=True) * across
            out_ref[w, l, 0] = (real[0:count] * scale).astype(jnp.bfloat16)[:, :count]
            out_ref[w, l, 1] = (imag[0:count] * scale).astype(jnp.bfloat16)[:, :count]

    products(0)
    for l in range(PER):
        if l + 1 < PER:
            products(l + 1)
        normalised(l)


def looked(half, other, rows, first, groups, looks, previous, terms, slab):
    count = other.shape[3]

    def spec(array):
        offset = 0 if array is other else first
        rest = array.shape[2:]
        return pl.BlockSpec((array.shape[0], 1) + rest, lambda s: (0, s + offset) + (0,) * len(rest))

    operands = [other, rows]
    in_specs = [spec(a) for a in operands]
    aliases = {}
    if previous is not None:
        aliases = {len(operands): 0}
        operands.append(previous)
        in_specs.append(pl.BlockSpec(memory_space=pl.ANY))
    for term in terms:
        operands.append(term)
        in_specs.append(pl.BlockSpec(term.shape, lambda s: (0, 0)))
    extra = (2, count, count) if slab else (LANES, LANES)
    out_specs = [
        pl.BlockSpec((2, PER, 2, count, count), lambda s: (half, s + first, 0, 0, 0)),
        pl.BlockSpec(extra, lambda s: (0,) * len(extra)),
    ]
    out_shape = [
        jax.ShapeDtypeStruct((ROWS // 2, looks, 2, count, count), jnp.bfloat16),
        jax.ShapeDtypeStruct(extra, jnp.float32),
    ]
    return pl.pallas_call(
        functools.partial(looks_kernel, half, previous is not None, len(terms), slab),
        grid=(groups,),
        in_specs=in_specs,
        out_specs=out_specs,
        out_shape=out_shape,
        input_output_aliases=aliases,
        scratch_shapes=[
            pltpu.VMEM((2, 2, LANES, 2 * LANES), jnp.bfloat16),
            pltpu.VMEM((2, 2, 2, LANES, LANES), jnp.float32),
            pltpu.VMEM((other.shape[0], 4, LANES, LANES), jnp.bfloat16),
        ],
        compiler_params=pltpu.CompilerParams(vmem_limit_bytes=44 * 2**20),
        cost_estimate=pl.CostEstimate(
            flops=1 * groups * PER * 2 * 512 * 256 * 256, bytes_accessed=groups * 10**6, transcendentals=0
        ),
        name="looks",
    )(*operands)


def rounds(size):
    found = []
    stride = 1
    while stride < size:
        radix = 4 if size // stride % 4 == 0 else 2
        if size // stride % radix:
            return None
        found.append((stride, radix))
        stride *= radix
    return found[::-1]


def round_terms(value, axis, stride, radix):
    size = lax.axis_size(axis)
    terms = [value]
    for shift in range(1, radix):
        pairs = []
        for i in range(size):
            place = (i // stride) % radix
            pairs.append((i, i + ((place + shift) % radix - place) * stride))
        terms.append(lax.ppermute(value, axis, pairs))
    return terms


def shards(images, valid_mask):
    looks = images.shape[3] // LOOK
    groups = -(-looks // PER)
    cut = -(-groups // 2)
    size = lax.axis_size("pix")
    forward = [(i, i + 1) for i in range(size - 1)]
    backward = [(i + 1, i) for i in range(size - 1)]
    top, low0, low1 = edge_rows(images, valid_mask, groups, cut)
    after = lax.ppermute(top, "pix", backward)
    before0 = lax.ppermute(low0, "pix", forward)
    before1 = lax.ppermute(low1, "pix", forward)
    rows, total = local_rows(images, valid_mask, groups)
    steps = rounds(size)
    if steps is None:
        terms, steps = [lax.psum(total, "pix")], []
    else:
        terms = round_terms(total, "pix", *steps[0]) if steps else [total]
    out, zeros = looked(1, after, rows, 0, groups, looks, None, [], False)
    for step in steps[1:]:
        terms = round_terms(added(terms) + zeros, "pix", *step)
    out, _ = looked(0, before0, rows, 0, cut, looks, out, [], False)
    out, slab = looked(0, before1, rows, cut, groups - cut, looks, out, terms, True)
    return (out, slab)


def solution(mesh):
    in_specs = (P(("group", "pix"), None, None, None), P(("group", "pix"), None))
    out_specs = (P(("group", "pix"), None, None, None, None), P("group", None, None))
    return jax.shard_map(shards, mesh=mesh, in_specs=in_specs, out_specs=out_specs, check_vma=False)
```

```python
import functools
import jax
import jax.numpy as jnp
from jax import lax
from jax.experimental import pallas as pl
from jax.experimental.pallas import tpu as pltpu
from jax.sharding import PartitionSpec as P

floor_power = 30.0

LOOK = 21
LANES = 128
TILE = 16
PER = LANES // LOOK
SPAN = PER * LOOK
ROWS = 8
SKEW = (5, 0, 1, 2, 3, 4, 1, 2)
BEFORE, AFTER = 3, 2
NT = (((1,), (1,)), ((), ()))


def turned(image, mask, skew, columns, put):
    count = image[0].shape[0]
    zero = jnp.zeros((count, LANES), jnp.bfloat16)
    lane = lax.broadcasted_iota(jnp.int32, (1, LANES), 1)

    def tile(value, g):
        start, stop = g * LANES, min((g + 1) * LANES, columns)
        part = value[:, start:stop]
        if stop - start < LANES:
            rest = jnp.zeros((part.shape[0], LANES - (stop - start)), part.dtype)
            part = jnp.concatenate([part, rest], axis=1)
        return part

    def widened(which):
        return jnp.broadcast_to(which.astype(jnp.float32), (count, LANES)).astype(jnp.bfloat16) != 0

    tiles = -(-columns // LANES)
    for g in range(-(-columns // SPAN)):
        slide = (LANES - SPAN) * g
        place = (lane + slide) % LANES
        used = (place < SPAN) & (SPAN * g + place < columns)
        prior = lane >= LANES - slide
        sides = [t for t in (g - 1, g) if 0 <= t < tiles]

        def joined(value):
            parts = [tile(value, t) for t in sides]
            if len(parts) == 1:
                return parts[0]
            which = prior if value.shape[0] == 1 else widened(prior)
            return jnp.where(which, parts[0], parts[1])

        keep = widened(used & (joined(mask) != 0))
        for k in range(2):
            row = jnp.where(keep, joined(image[k]), zero)
            put(g, k, pltpu.roll(row, slide + LOOK * skew, 1))


def fetched(image_ref, mask_ref, rows_ref, masks_ref, sems, order):
    mask_copy = pltpu.make_async_copy(mask_ref, masks_ref, sems.at[len(order)])
    mask_copy.start()
    copies = [pltpu.make_async_copy(image_ref.at[row], rows_ref.at[at], sems.at[at]) for at, row in enumerate(order)]
    for copy in copies:
        copy.start()
    mask_copy.wait()
    return copies


EDGE = tuple(range(AFTER)) + tuple(range(ROWS - BEFORE, ROWS))


def edge_kernel(cut, image_ref, mask_ref, top_ref, low0_ref, low1_ref, rows_ref, masks_ref, turned_ref, in_sems, out_sems):
    fetches = fetched(image_ref, mask_ref, rows_ref, masks_ref, in_sems, EDGE)
    stores = []
    for at, row in enumerate(EDGE):
        fetches[at].wait()

        def put(g, k, value):
            turned_ref[at, g, k] = value

        turned([rows_ref.at[at, 0], rows_ref.at[at, 1]], masks_ref[row : row + 1, :], SKEW[row], masks_ref.shape[1], put)
        groups = turned_ref.shape[1]
        i = row - (ROWS - BEFORE)
        if row < AFTER:
            targets = ((top_ref.at[row], 0, groups),)
        else:
            targets = ((low0_ref.at[i], 0, cut), (low1_ref.at[i], cut, groups))
        for target, start, stop in targets:
            store = pltpu.make_async_copy(turned_ref.at[at, start:stop], target, out_sems.at[len(stores)])
            store.start()
            stores.append(store)
    for store in stores:
        store.wait()


def rows_shape(rows, groups, count):
    return jax.ShapeDtypeStruct((rows, groups, 2, count, LANES), jnp.bfloat16)


def edge_rows(images, valid_mask, groups, cut):
    count = images.shape[2]
    far = pl.BlockSpec(memory_space=pl.ANY)
    return pl.pallas_call(
        functools.partial(edge_kernel, cut),
        in_specs=[far, far],
        out_specs=[far] * 3,
        out_shape=[
            rows_shape(AFTER, groups, count),
            rows_shape(BEFORE, cut, count),
            rows_shape(BEFORE, groups - cut, count),
        ],
        scratch_shapes=[
            pltpu.VMEM((len(EDGE),) + images.shape[1:], jnp.bfloat16),
            pltpu.VMEM(valid_mask.shape, jnp.int32),
            pltpu.VMEM((len(EDGE), groups, 2, count, LANES), jnp.bfloat16),
            pltpu.SemaphoreType.DMA((len(EDGE) + 1,)),
            pltpu.SemaphoreType.DMA((AFTER + 2 * BEFORE,)),
        ],
        compiler_params=pltpu.CompilerParams(vmem_limit_bytes=61 * 2**20),
        cost_estimate=pl.CostEstimate(flops=10**6, bytes_accessed=4 * 10**6, transcendentals=0),
        name="edge_rows",
    )(images, valid_mask)


def local_kernel(image_ref, mask_ref, all_ref, gram_ref, rows_ref, masks_ref, turned_ref, z_ref, in_sems, out_sems):
    groups = all_ref.shape[1]
    count, columns = image_ref.shape[2:]
    fetches = fetched(image_ref, mask_ref, rows_ref, masks_ref, in_sems, range(ROWS))
    z_ref[...] = jnp.zeros_like(z_ref)
    stores = []
    total = None
    wide = groups * LANES
    for row in range(ROWS):
        fetches[row].wait()

        def put(g, k, value):
            turned_ref[row, g, k] = value
            z_ref[pl.ds(k * LANES, count), pl.ds(row * wide + g * LANES, LANES)] = value

        turned([rows_ref.at[row, 0], rows_ref.at[row, 1]], masks_ref[row : row + 1, :], SKEW[row], columns, put)
        store = pltpu.make_async_copy(turned_ref.at[row], all_ref.at[row], out_sems.at[row])
        store.start()
        stores.append(store)
        if row % 2:
            z = z_ref[:, pl.ds((row - 1) * wide, 2 * wide)]
            part = lax.dot_general(z, z, NT, preferred_element_type=jnp.float32)
            total = part if total is None else total + part
    real = total[:LANES, :LANES] + total[LANES:, LANES:]
    imag = total[LANES:, :LANES] - total[:LANES, LANES:]
    i = lax.broadcasted_iota(jnp.int32, real.shape, 0)
    j = lax.broadcasted_iota(jnp.int32, real.shape, 1)
    gram_ref[...] = jnp.where(i <= j, real, imag)
    for store in stores:
        store.wait()


def local_rows(images, valid_mask, groups):
    count = images.shape[2]
    far = pl.BlockSpec(memory_space=pl.ANY)
    return pl.pallas_call(
        local_kernel,
        in_specs=[far, far],
        out_specs=[far, pl.BlockSpec(memory_space=pltpu.VMEM)],
        out_shape=[rows_shape(ROWS, groups, count), jax.ShapeDtypeStruct((LANES, LANES), jnp.float32)],
        scratch_shapes=[
            pltpu.VMEM(images.shape, jnp.bfloat16),
            pltpu.VMEM(valid_mask.shape, jnp.int32),
            pltpu.VMEM((ROWS, groups, 2, count, LANES), jnp.bfloat16),
            pltpu.VMEM((2 * LANES, ROWS * groups * LANES), jnp.bfloat16),
            pltpu.SemaphoreType.DMA((ROWS + 1,)),
            pltpu.SemaphoreType.DMA((ROWS,)),
        ],
        compiler_params=pltpu.CompilerParams(vmem_limit_bytes=50 * 2**20),
        cost_estimate=pl.CostEstimate(flops=10**9, bytes_accessed=5 * 10**6, transcendentals=0),
        name="local_rows",
    )(images, valid_mask)


def added(terms):
    if len(terms) == 4:
        return (terms[0] + terms[2]) + (terms[1] + terms[3])
    return functools.reduce(jnp.add, terms)


def slab_values(terms):
    packed = added(terms)
    flipped = packed.T
    i = lax.broadcasted_iota(jnp.int32, packed.shape, 0)
    j = lax.broadcasted_iota(jnp.int32, packed.shape, 1)
    real = jnp.where(i <= j, packed, flipped)
    imag = jnp.where(i > j, packed, jnp.where(i < j, -flipped, 0.0))
    powers = jnp.where(i == j, packed, 0.0)
    scaled = jnp.sqrt(jnp.sum(powers, axis=1, keepdims=True) * jnp.sum(powers, axis=0, keepdims=True))
    return real / scaled, imag / scaled


INNER = (1, 2, 3, 4, 5)
HALVES = (
    ((-3, -2, -1, 0), (((1, 2, 3), None), (None, (-1, 0)))),
    ((6, 7, 8, 9), ((None, (6, 7)), ((3, 4, 5), None))),
)


def looks_kernel(half, aliased, terms, slab, *refs):
    other_ref, all_ref = refs[:2]
    refs = refs[2 + aliased :]
    term_refs, refs = refs[:terms], refs[terms:]
    out_ref, extra_ref, w_ref, g_ref = refs
    count = all_ref.shape[3]

    @pl.when(pl.program_id(0) == 0)
    def _():
        w_ref[...] = jnp.zeros_like(w_ref)
        if slab:
            real, imag = slab_values([t[...] for t in term_refs])
            extra_ref[0] = real[:count, :count]
            extra_ref[1] = imag[:count, :count]
        elif terms:
            extra_ref[...] = added([t[...] for t in term_refs])
        else:
            extra_ref[...] = jnp.zeros_like(extra_ref)

    rows = {r: all_ref.at[r, 0] for r in range(ROWS)}
    for r in range(other_ref.shape[0]):
        rows[ROWS + r if half else r - BEFORE] = other_ref.at[r, 0]

    lane = lax.broadcasted_iota(jnp.int32, (1, LANES), 1)

    def lanes_of(turn):
        place = lane + (-LOOK * turn) % LANES
        place = jnp.where(place >= LANES, place - LANES, place)
        return place < LOOK

    def widened(which):
        return jnp.broadcast_to(which.astype(jnp.float32), (count, LANES)).astype(jnp.bfloat16) != 0

    single = [lanes_of(t) for t in range(2 * PER - 1)]
    wide = [widened(s) for s in single]

    def turn(l, r):
        return l + SKEW[r % ROWS]

    def gathered(l, k, which):
        out = rows[which[0]][k]
        for r in which[1:]:
            out = jnp.where(wide[turn(l, r)], rows[r][k], out)
        return out

    def kept(l, which):
        select = single[turn(l, which[0])]
        for r in which[1:]:
            select = select | single[turn(l, r)]
        return select.astype(jnp.float32)

    eight = (8, LANES)
    along = lax.broadcasted_iota(jnp.int32, eight, 1)
    on_eye = along % 8 == lax.broadcasted_iota(jnp.int32, eight, 0)
    block = along // 8

    outer_rows, windows = HALVES[half]

    def products(l):
        slot = l % 2
        for k in range(2):
            w_ref[slot, k, pl.ds(0, count), pl.ds(0, LANES)] = gathered(l, k, INNER)
            w_ref[slot, k, pl.ds(0, count), pl.ds(LANES, LANES)] = gathered(l, k, outer_rows)
        every = w_ref[slot].reshape(2 * LANES, 2 * LANES)
        nothing = jnp.zeros_like(every)
        reads = []
        for inner_rows, rest_rows in windows:
            lanes = jnp.concatenate([kept(l, inner_rows or INNER), kept(l, rest_rows or outer_rows)], axis=1)
            lanes = jnp.broadcast_to(lanes, every.shape).astype(jnp.bfloat16) != 0
            read = jnp.where(lanes, every, nothing)
            for start in range(0, LANES, TILE):
                reads.append(read[start : start + TILE])
                reads.append(read[LANES + start : LANES + start + TILE])
        gram = lax.dot_general(jnp.concatenate(reads, axis=0), every, NT, preferred_element_type=jnp.float32)
        for w in range(2):
            for start in range(0, LANES, TILE):
                base = 2 * (w * LANES + start)
                re, im = gram[base : base + TILE], gram[base + TILE : base + 2 * TILE]
                g_ref[slot, w, 0, pl.ds(start, TILE)] = re[:, :LANES] + im[:, LANES:]
                g_ref[slot, w, 1, pl.ds(start, TILE)] = im[:, :LANES] - re[:, LANES:]

    def normalised(l):
        for w in range(2):
            real, imag = g_ref.at[l % 2, w, 0], g_ref.at[l % 2, w, 1]
            picked = real[0:8]
            for v in range(1, count // 8):
                picked = jnp.where(block == v, real[8 * v : 8 * v + 8], picked)
            power = jnp.sum(jnp.where(on_eye, picked, 0.0), axis=0, keepdims=True)
            across = lax.rsqrt(jnp.maximum(power, floor_power))
            run = jnp.where(on_eye, across, 0.0)
            for shift in (1, 2, 4):
                run = run + pltpu.roll(run, shift, 1)
            scale = jnp.concatenate([run[:, 8 * v + 7 : 8 * v + 8] * across for v in range(count // 8)], axis=0)
            out_ref[w, l, 0] = (real[0:count] * scale).astype(jnp.bfloat16)[:, :count]
            out_ref[w, l, 1] = (imag[0:count] * scale).astype(jnp.bfloat16)[:, :count]

    products(0)
    for l in range(PER):
        if l + 1 < PER:
            products(l + 1)
        normalised(l)


def looked(half, other, rows, first, groups, looks, previous, terms, slab):
    count = other.shape[3]

    def spec(array):
        offset = 0 if array is other else first
        return pl.BlockSpec((array.shape[0], 1) + array.shape[2:], lambda s: (0, s + offset, 0, 0, 0))

    operands = [other, rows]
    in_specs = [spec(a) for a in operands]
    aliases = {}
    if previous is not None:
        aliases = {len(operands): 0}
        operands.append(previous)
        in_specs.append(pl.BlockSpec(memory_space=pl.ANY))
    for term in terms:
        operands.append(term)
        in_specs.append(pl.BlockSpec(term.shape, lambda s: (0, 0)))
    extra = (2, count, count) if slab else (LANES, LANES)
    out_specs = [
        pl.BlockSpec((2, PER, 2, count, count), lambda s: (half, s + first, 0, 0, 0)),
        pl.BlockSpec(extra, lambda s: (0,) * len(extra)),
    ]
    out_shape = [
        jax.ShapeDtypeStruct((ROWS // 2, looks, 2, count, count), jnp.bfloat16),
        jax.ShapeDtypeStruct(extra, jnp.float32),
    ]
    return pl.pallas_call(
        functools.partial(looks_kernel, half, previous is not None, len(terms), slab),
        grid=(groups,),
        in_specs=in_specs,
        out_specs=out_specs,
        out_shape=out_shape,
        input_output_aliases=aliases,
        scratch_shapes=[
            pltpu.VMEM((2, 2, LANES, 2 * LANES), jnp.bfloat16),
            pltpu.VMEM((2, 2, 2, LANES, LANES), jnp.float32),
        ],
        compiler_params=pltpu.CompilerParams(vmem_limit_bytes=49 * 2**20),
        cost_estimate=pl.CostEstimate(
            flops=1 * groups * PER * 2 * 512 * 256 * 256, bytes_accessed=groups * 10**6, transcendentals=0
        ),
        name="looks",
    )(*operands)


def rounds(size):
    found = []
    stride = 1
    while stride < size:
        radix = 4 if size // stride % 4 == 0 else 2
        if size // stride % radix:
            return None
        found.append((stride, radix))
        stride *= radix
    return found[::-1]


def round_terms(value, axis, stride, radix):
    size = lax.axis_size(axis)
    terms = [value]
    for shift in range(1, radix):
        pairs = []
        for i in range(size):
            place = (i // stride) % radix
            pairs.append((i, i + ((place + shift) % radix - place) * stride))
        terms.append(lax.ppermute(value, axis, pairs))
    return terms


def shards(images, valid_mask):
    looks = images.shape[3] // LOOK
    groups = -(-looks // PER)
    cut = -(-groups // 2)
    size = lax.axis_size("pix")
    forward = [(i, i + 1) for i in range(size - 1)]
    backward = [(i + 1, i) for i in range(size - 1)]
    top, low0, low1 = edge_rows(images, valid_mask, groups, cut)
    after = lax.ppermute(top, "pix", backward)
    before0 = lax.ppermute(low0, "pix", forward)
    before1 = lax.ppermute(low1, "pix", forward)
    rows, total = local_rows(images, valid_mask, groups)
    steps = rounds(size)
    if steps is None:
        terms, steps = [lax.psum(total, "pix")], []
    else:
        terms = round_terms(total, "pix", *steps[0]) if steps else [total]
    out, zeros = looked(1, after, rows, 0, groups, looks, None, [], False)
    for step in steps[1:]:
        terms = round_terms(added(terms) + zeros, "pix", *step)
    out, _ = looked(0, before0, rows, 0, cut, looks, out, [], False)
    out, slab = looked(0, before1, rows, cut, groups - cut, looks, out, terms, True)
    return (out, slab)


def solution(mesh):
    in_specs = (P(("group", "pix"), None, None, None), P(("group", "pix"), None))
    out_specs = (P(("group", "pix"), None, None, None, None), P("group", None, None))
    return jax.shard_map(shards, mesh=mesh, in_specs=in_specs, out_specs=out_specs, check_vma=False)
```

```python
import functools
import jax
import jax.numpy as jnp
from jax import lax
from jax.experimental import pallas as pl
from jax.experimental.pallas import tpu as pltpu
from jax.sharding import PartitionSpec as P

floor_power = 30.0

LOOK = 21
LANES = 128
TILE = 16
PER = LANES // LOOK
SPAN = PER * LOOK
ROWS = 8
SKEW = (5, 0, 1, 2, 3, 4, 1, 2)
BEFORE, AFTER = 3, 2
NT = (((1,), (1,)), ((), ()))


def turned(image, mask, skew, columns, put):
    count = image[0].shape[0]
    zero = jnp.zeros((count, LANES), jnp.bfloat16)
    lane = lax.broadcasted_iota(jnp.int32, (1, LANES), 1)

    def tile(value, g):
        start, stop = g * LANES, min((g + 1) * LANES, columns)
        part = value[:, start:stop]
        if stop - start < LANES:
            rest = jnp.zeros((part.shape[0], LANES - (stop - start)), part.dtype)
            part = jnp.concatenate([part, rest], axis=1)
        return part

    def widened(which):
        return jnp.broadcast_to(which.astype(jnp.float32), (count, LANES)).astype(jnp.bfloat16) != 0

    tiles = -(-columns // LANES)
    for g in range(-(-columns // SPAN)):
        slide = (LANES - SPAN) * g
        place = (lane + slide) % LANES
        used = (place < SPAN) & (SPAN * g + place < columns)
        prior = lane >= LANES - slide
        sides = [t for t in (g - 1, g) if 0 <= t < tiles]

        def joined(value):
            parts = [tile(value, t) for t in sides]
            if len(parts) == 1:
                return parts[0]
            which = prior if value.shape[0] == 1 else widened(prior)
            return jnp.where(which, parts[0], parts[1])

        keep = widened(used & (joined(mask) != 0))
        for k in range(2):
            row = jnp.where(keep, joined(image[k]), zero)
            put(g, k, pltpu.roll(row, slide + LOOK * skew, 1))


def fetched(image_ref, mask_ref, rows_ref, masks_ref, sems, order):
    mask_copy = pltpu.make_async_copy(mask_ref, masks_ref, sems.at[len(order)])
    mask_copy.start()
    copies = [pltpu.make_async_copy(image_ref.at[row], rows_ref.at[at], sems.at[at]) for at, row in enumerate(order)]
    for copy in copies:
        copy.start()
    mask_copy.wait()
    return copies


EDGE = tuple(range(AFTER)) + tuple(range(ROWS - BEFORE, ROWS))


def edge_kernel(cut, image_ref, mask_ref, top_ref, low0_ref, low1_ref, rows_ref, masks_ref, turned_ref, in_sems, out_sems):
    fetches = fetched(image_ref, mask_ref, rows_ref, masks_ref, in_sems, EDGE)
    stores = []
    for at, row in enumerate(EDGE):
        fetches[at].wait()

        def put(g, k, value):
            turned_ref[at, g, k] = value

        turned([rows_ref.at[at, 0], rows_ref.at[at, 1]], masks_ref[row : row + 1, :], SKEW[row], masks_ref.shape[1], put)
        groups = turned_ref.shape[1]
        i = row - (ROWS - BEFORE)
        if row < AFTER:
            targets = ((top_ref.at[row], 0, groups),)
        else:
            targets = ((low0_ref.at[i], 0, cut), (low1_ref.at[i], cut, groups))
        for target, start, stop in targets:
            store = pltpu.make_async_copy(turned_ref.at[at, start:stop], target, out_sems.at[len(stores)])
            store.start()
            stores.append(store)
    for store in stores:
        store.wait()


def rows_shape(rows, groups, count):
    return jax.ShapeDtypeStruct((rows, groups, 2, count, LANES), jnp.bfloat16)


def edge_rows(images, valid_mask, groups, cut):
    count = images.shape[2]
    far = pl.BlockSpec(memory_space=pl.ANY)
    return pl.pallas_call(
        functools.partial(edge_kernel, cut),
        in_specs=[far, far],
        out_specs=[far] * 3,
        out_shape=[
            rows_shape(AFTER, groups, count),
            rows_shape(BEFORE, cut, count),
            rows_shape(BEFORE, groups - cut, count),
        ],
        scratch_shapes=[
            pltpu.VMEM((len(EDGE),) + images.shape[1:], jnp.bfloat16),
            pltpu.VMEM(valid_mask.shape, jnp.int32),
            pltpu.VMEM((len(EDGE), groups, 2, count, LANES), jnp.bfloat16),
            pltpu.SemaphoreType.DMA((len(EDGE) + 1,)),
            pltpu.SemaphoreType.DMA((AFTER + 2 * BEFORE,)),
        ],
        compiler_params=pltpu.CompilerParams(vmem_limit_bytes=61 * 2**20),
        cost_estimate=pl.CostEstimate(flops=10**6, bytes_accessed=4 * 10**6, transcendentals=0),
        name="edge_rows",
    )(images, valid_mask)


def local_kernel(image_ref, mask_ref, all_ref, gram_ref, rows_ref, masks_ref, turned_ref, z_ref, in_sems, out_sems):
    groups = all_ref.shape[1]
    count, columns = image_ref.shape[2:]
    fetches = fetched(image_ref, mask_ref, rows_ref, masks_ref, in_sems, range(ROWS))
    z_ref[...] = jnp.zeros_like(z_ref)
    stores = []
    total = None
    wide = groups * LANES
    for row in range(ROWS):
        fetches[row].wait()

        def put(g, k, value):
            turned_ref[row, g, k] = value
            z_ref[pl.ds(k * LANES, count), pl.ds(row * wide + g * LANES, LANES)] = value

        turned([rows_ref.at[row, 0], rows_ref.at[row, 1]], masks_ref[row : row + 1, :], SKEW[row], columns, put)
        store = pltpu.make_async_copy(turned_ref.at[row], all_ref.at[row], out_sems.at[row])
        store.start()
        stores.append(store)
        if row % 2:
            z = z_ref[:, pl.ds((row - 1) * wide, 2 * wide)]
            part = lax.dot_general(z, z, NT, preferred_element_type=jnp.float32)
            total = part if total is None else total + part
    real = total[:LANES, :LANES] + total[LANES:, LANES:]
    imag = total[LANES:, :LANES] - total[:LANES, LANES:]
    i = lax.broadcasted_iota(jnp.int32, real.shape, 0)
    j = lax.broadcasted_iota(jnp.int32, real.shape, 1)
    gram_ref[...] = jnp.where(i <= j, real, imag)
    for store in stores:
        store.wait()


def local_rows(images, valid_mask, groups):
    count = images.shape[2]
    far = pl.BlockSpec(memory_space=pl.ANY)
    return pl.pallas_call(
        local_kernel,
        in_specs=[far, far],
        out_specs=[far, pl.BlockSpec(memory_space=pltpu.VMEM)],
        out_shape=[rows_shape(ROWS, groups, count), jax.ShapeDtypeStruct((LANES, LANES), jnp.float32)],
        scratch_shapes=[
            pltpu.VMEM(images.shape, jnp.bfloat16),
            pltpu.VMEM(valid_mask.shape, jnp.int32),
            pltpu.VMEM((ROWS, groups, 2, count, LANES), jnp.bfloat16),
            pltpu.VMEM((2 * LANES, ROWS * groups * LANES), jnp.bfloat16),
            pltpu.SemaphoreType.DMA((ROWS + 1,)),
            pltpu.SemaphoreType.DMA((ROWS,)),
        ],
        compiler_params=pltpu.CompilerParams(vmem_limit_bytes=50 * 2**20),
        cost_estimate=pl.CostEstimate(flops=10**9, bytes_accessed=5 * 10**6, transcendentals=0),
        name="local_rows",
    )(images, valid_mask)


def added(terms):
    if len(terms) == 4:
        return (terms[0] + terms[2]) + (terms[1] + terms[3])
    return functools.reduce(jnp.add, terms)


def slab_values(terms):
    packed = added(terms)
    flipped = packed.T
    i = lax.broadcasted_iota(jnp.int32, packed.shape, 0)
    j = lax.broadcasted_iota(jnp.int32, packed.shape, 1)
    real = jnp.where(i <= j, packed, flipped)
    imag = jnp.where(i > j, packed, jnp.where(i < j, -flipped, 0.0))
    powers = jnp.where(i == j, packed, 0.0)
    scaled = jnp.sqrt(jnp.sum(powers, axis=1, keepdims=True) * jnp.sum(powers, axis=0, keepdims=True))
    return real / scaled, imag / scaled


INNER = (1, 2, 3, 4, 5)
HALVES = (
    ((-3, -2, -1, 0), (((1, 2, 3), None), (None, (-1, 0)))),
    ((6, 7, 8, 9), ((None, (6, 7)), ((3, 4, 5), None))),
)


def looks_kernel(half, aliased, terms, slab, *refs):
    other_ref, all_ref = refs[:2]
    refs = refs[2 + aliased :]
    term_refs, refs = refs[:terms], refs[terms:]
    out_ref, extra_ref, w_ref, g_ref, eye_ref = refs
    count = all_ref.shape[3]

    @pl.when(pl.program_id(0) == 0)
    def _():
        w_ref[...] = jnp.zeros_like(w_ref)
        i = lax.broadcasted_iota(jnp.int32, eye_ref.shape, 0)
        j = lax.broadcasted_iota(jnp.int32, eye_ref.shape, 1)
        eye_ref[...] = jnp.where(i == j % LANES, 1.0, 0.0).astype(jnp.bfloat16)
        if slab:
            real, imag = slab_values([t[...] for t in term_refs])
            extra_ref[0] = real[:count, :count]
            extra_ref[1] = imag[:count, :count]
        elif terms:
            extra_ref[...] = added([t[...] for t in term_refs])
        else:
            extra_ref[...] = jnp.zeros_like(extra_ref)

    rows = {r: all_ref.at[r, 0] for r in range(ROWS)}
    for r in range(other_ref.shape[0]):
        rows[ROWS + r if half else r - BEFORE] = other_ref.at[r, 0]

    lane = lax.broadcasted_iota(jnp.int32, (1, LANES), 1)

    def lanes_of(turn):
        place = lane + (-LOOK * turn) % LANES
        place = jnp.where(place >= LANES, place - LANES, place)
        return place < LOOK

    def widened(which):
        return jnp.broadcast_to(which.astype(jnp.float32), (count, LANES)).astype(jnp.bfloat16) != 0

    single = [lanes_of(t) for t in range(2 * PER - 1)]
    wide = [widened(s) for s in single]

    def turn(l, r):
        return l + SKEW[r % ROWS]

    def gathered(l, k, which):
        out = rows[which[0]][k]
        for r in which[1:]:
            out = jnp.where(wide[turn(l, r)], rows[r][k], out)
        return out

    def kept(l, which):
        select = single[turn(l, which[0])]
        for r in which[1:]:
            select = select | single[turn(l, r)]
        return select.astype(jnp.float32)

    eight = (8, LANES)
    along = lax.broadcasted_iota(jnp.int32, eight, 1)
    on_eye = along % 8 == lax.broadcasted_iota(jnp.int32, eight, 0)
    block = along // 8

    outer_rows, windows = HALVES[half]

    def products(l):
        slot = l % 2
        for k in range(2):
            w_ref[slot, k, pl.ds(0, count), pl.ds(0, LANES)] = gathered(l, k, INNER)
            w_ref[slot, k, pl.ds(0, count), pl.ds(LANES, LANES)] = gathered(l, k, outer_rows)
        every = w_ref[slot].reshape(2 * LANES, 2 * LANES)
        nothing = jnp.zeros_like(every)
        reads = []
        for inner_rows, rest_rows in windows:
            lanes = jnp.concatenate([kept(l, inner_rows or INNER), kept(l, rest_rows or outer_rows)], axis=1)
            lanes = jnp.broadcast_to(lanes, every.shape).astype(jnp.bfloat16) != 0
            read = jnp.where(lanes, every, nothing)
            for start in range(0, LANES, TILE):
                reads.append(read[start : start + TILE])
                reads.append(read[LANES + start : LANES + start + TILE])
        gram = lax.dot_general(jnp.concatenate(reads, axis=0), every, NT, preferred_element_type=jnp.float32)
        for w in range(2):
            for start in range(0, LANES, TILE):
                base = 2 * (w * LANES + start)
                re, im = gram[base : base + TILE], gram[base + TILE : base + 2 * TILE]
                g_ref[slot, w, 0, pl.ds(start, TILE)] = re[:, :LANES] + im[:, LANES:]
                g_ref[slot, w, 1, pl.ds(start, TILE)] = im[:, :LANES] - re[:, LANES:]

    def normalised(l):
        acrosses, terms_of = [], []
        for w in range(2):
            real = g_ref.at[l % 2, w, 0]
            picked = real[0:8]
            for v in range(1, count // 8):
                picked = jnp.where(block == v, real[8 * v : 8 * v + 8], picked)
            power = jnp.sum(jnp.where(on_eye, picked, 0.0), axis=0, keepdims=True)
            across = lax.rsqrt(jnp.maximum(power, floor_power))
            acrosses.append(across)
            tile = jnp.broadcast_to(across, (TILE, LANES))
            high = tile.astype(jnp.bfloat16)
            rest = (tile - high.astype(jnp.float32)).astype(jnp.bfloat16)
            terms_of += [jnp.concatenate([high, rest], axis=1)] * (LANES // TILE)
        down = lax.dot_general(eye_ref[...], jnp.concatenate(terms_of, axis=0), NT, preferred_element_type=jnp.float32)
        for w in range(2):
            real, imag = g_ref.at[l % 2, w, 0], g_ref.at[l % 2, w, 1]
            scale = down[0:count, w * LANES : (w + 1) * LANES] * acrosses[w]
            out_ref[w, l, 0] = (real[0:count] * scale).astype(jnp.bfloat16)[:, :count]
            out_ref[w, l, 1] = (imag[0:count] * scale).astype(jnp.bfloat16)[:, :count]

    products(0)
    for l in range(PER):
        if l + 1 < PER:
            products(l + 1)
        normalised(l)


def looked(half, other, rows, first, groups, looks, previous, terms, slab):
    count = other.shape[3]

    def spec(array):
        offset = 0 if array is other else first
        return pl.BlockSpec((array.shape[0], 1) + array.shape[2:], lambda s: (0, s + offset, 0, 0, 0))

    operands = [other, rows]
    in_specs = [spec(a) for a in operands]
    aliases = {}
    if previous is not None:
        aliases = {len(operands): 0}
        operands.append(previous)
        in_specs.append(pl.BlockSpec(memory_space=pl.ANY))
    for term in terms:
        operands.append(term)
        in_specs.append(pl.BlockSpec(term.shape, lambda s: (0, 0)))
    extra = (2, count, count) if slab else (LANES, LANES)
    out_specs = [
        pl.BlockSpec((2, PER, 2, count, count), lambda s: (half, s + first, 0, 0, 0)),
        pl.BlockSpec(extra, lambda s: (0,) * len(extra)),
    ]
    out_shape = [
        jax.ShapeDtypeStruct((ROWS // 2, looks, 2, count, count), jnp.bfloat16),
        jax.ShapeDtypeStruct(extra, jnp.float32),
    ]
    return pl.pallas_call(
        functools.partial(looks_kernel, half, previous is not None, len(terms), slab),
        grid=(groups,),
        in_specs=in_specs,
        out_specs=out_specs,
        out_shape=out_shape,
        input_output_aliases=aliases,
        scratch_shapes=[
            pltpu.VMEM((2, 2, LANES, 2 * LANES), jnp.bfloat16),
            pltpu.VMEM((2, 2, 2, LANES, LANES), jnp.float32),
            pltpu.VMEM((LANES, 2 * LANES), jnp.bfloat16),
        ],
        compiler_params=pltpu.CompilerParams(vmem_limit_bytes=49 * 2**20),
        cost_estimate=pl.CostEstimate(
            flops=1 * groups * PER * 2 * 512 * 256 * 256, bytes_accessed=groups * 10**6, transcendentals=0
        ),
        name="looks",
    )(*operands)


def rounds(size):
    found = []
    stride = 1
    while stride < size:
        radix = 4 if size // stride % 4 == 0 else 2
        if size // stride % radix:
            return None
        found.append((stride, radix))
        stride *= radix
    return found[::-1]


def round_terms(value, axis, stride, radix):
    size = lax.axis_size(axis)
    terms = [value]
    for shift in range(1, radix):
        pairs = []
        for i in range(size):
            place = (i // stride) % radix
            pairs.append((i, i + ((place + shift) % radix - place) * stride))
        terms.append(lax.ppermute(value, axis, pairs))
    return terms


def shards(images, valid_mask):
    looks = images.shape[3] // LOOK
    groups = -(-looks // PER)
    cut = -(-groups // 2)
    size = lax.axis_size("pix")
    forward = [(i, i + 1) for i in range(size - 1)]
    backward = [(i + 1, i) for i in range(size - 1)]
    top, low0, low1 = edge_rows(images, valid_mask, groups, cut)
    after = lax.ppermute(top, "pix", backward)
    before0 = lax.ppermute(low0, "pix", forward)
    before1 = lax.ppermute(low1, "pix", forward)
    rows, total = local_rows(images, valid_mask, groups)
    steps = rounds(size)
    if steps is None:
        terms, steps = [lax.psum(total, "pix")], []
    else:
        terms = round_terms(total, "pix", *steps[0]) if steps else [total]
    out, zeros = looked(1, after, rows, 0, groups, looks, None, [], False)
    for step in steps[1:]:
        terms = round_terms(added(terms) + zeros, "pix", *step)
    out, _ = looked(0, before0, rows, 0, cut, looks, out, [], False)
    out, slab = looked(0, before1, rows, cut, groups - cut, looks, out, terms, True)
    return (out, slab)


def solution(mesh):
    in_specs = (P(("group", "pix"), None, None, None), P(("group", "pix"), None))
    out_specs = (P(("group", "pix"), None, None, None, None), P("group", None, None))
    return jax.shard_map(shards, mesh=mesh, in_specs=in_specs, out_specs=out_specs, check_vma=False)
```

```python
import functools
import jax
import jax.numpy as jnp
from jax import lax
from jax.experimental import pallas as pl
from jax.experimental.pallas import tpu as pltpu
from jax.sharding import PartitionSpec as P

floor_power = 30.0

LOOK = 21
LANES = 128
TILE = 16
PER = LANES // LOOK
SPAN = PER * LOOK
ROWS = 8
SKEW = (3, 4, 5, 4, 5, 0, 1, 2)
BEFORE, AFTER = 3, 2
NT = (((1,), (1,)), ((), ()))


def turned(image, mask, skew, columns, put):
    count = image[0].shape[0]
    zero = jnp.zeros((count, LANES), jnp.bfloat16)
    lane = lax.broadcasted_iota(jnp.int32, (1, LANES), 1)

    def tile(value, g):
        start, stop = g * LANES, min((g + 1) * LANES, columns)
        part = value[:, start:stop]
        if stop - start < LANES:
            rest = jnp.zeros((part.shape[0], LANES - (stop - start)), part.dtype)
            part = jnp.concatenate([part, rest], axis=1)
        return part

    def widened(which):
        return jnp.broadcast_to(which.astype(jnp.float32), (count, LANES)).astype(jnp.bfloat16) != 0

    tiles = -(-columns // LANES)
    for g in range(-(-columns // SPAN)):
        slide = (LANES - SPAN) * g
        place = (lane + slide) % LANES
        used = (place < SPAN) & (SPAN * g + place < columns)
        prior = lane >= LANES - slide
        sides = [t for t in (g - 1, g) if 0 <= t < tiles]

        def joined(value):
            parts = [tile(value, t) for t in sides]
            if len(parts) == 1:
                return parts[0]
            which = prior if value.shape[0] == 1 else widened(prior)
            return jnp.where(which, parts[0], parts[1])

        keep = widened(used & (joined(mask) != 0))
        for k in range(2):
            row = jnp.where(keep, joined(image[k]), zero)
            put(g, k, pltpu.roll(row, slide + LOOK * skew, 1))


def fetched(image_ref, mask_ref, rows_ref, masks_ref, sems, order):
    mask_copy = pltpu.make_async_copy(mask_ref, masks_ref, sems.at[len(order)])
    mask_copy.start()
    copies = [pltpu.make_async_copy(image_ref.at[row], rows_ref.at[at], sems.at[at]) for at, row in enumerate(order)]
    for copy in copies:
        copy.start()
    mask_copy.wait()
    return copies


EDGE = tuple(range(AFTER)) + tuple(range(ROWS - BEFORE, ROWS))


def edge_kernel(cut, image_ref, mask_ref, top_ref, low0_ref, low1_ref, rows_ref, masks_ref, turned_ref, in_sems, out_sems):
    fetches = fetched(image_ref, mask_ref, rows_ref, masks_ref, in_sems, EDGE)
    stores = []
    for at, row in enumerate(EDGE):
        fetches[at].wait()

        def put(g, k, value):
            turned_ref[at, g, k] = value

        turned([rows_ref.at[at, 0], rows_ref.at[at, 1]], masks_ref[row : row + 1, :], SKEW[row], masks_ref.shape[1], put)
        groups = turned_ref.shape[1]
        i = row - (ROWS - BEFORE)
        if row < AFTER:
            targets = ((top_ref.at[row], 0, groups),)
        else:
            targets = ((low0_ref.at[i], 0, cut), (low1_ref.at[i], cut, groups))
        for target, start, stop in targets:
            store = pltpu.make_async_copy(turned_ref.at[at, start:stop], target, out_sems.at[len(stores)])
            store.start()
            stores.append(store)
    for store in stores:
        store.wait()


def rows_shape(rows, groups, count):
    return jax.ShapeDtypeStruct((rows, groups, 2, count, LANES), jnp.bfloat16)


def edge_rows(images, valid_mask, groups, cut):
    count = images.shape[2]
    far = pl.BlockSpec(memory_space=pl.ANY)
    return pl.pallas_call(
        functools.partial(edge_kernel, cut),
        in_specs=[far, far],
        out_specs=[far] * 3,
        out_shape=[
            rows_shape(AFTER, groups, count),
            rows_shape(BEFORE, cut, count),
            rows_shape(BEFORE, groups - cut, count),
        ],
        scratch_shapes=[
            pltpu.VMEM((len(EDGE),) + images.shape[1:], jnp.bfloat16),
            pltpu.VMEM(valid_mask.shape, jnp.int32),
            pltpu.VMEM((len(EDGE), groups, 2, count, LANES), jnp.bfloat16),
            pltpu.SemaphoreType.DMA((len(EDGE) + 1,)),
            pltpu.SemaphoreType.DMA((AFTER + 2 * BEFORE,)),
        ],
        compiler_params=pltpu.CompilerParams(vmem_limit_bytes=61 * 2**20),
        cost_estimate=pl.CostEstimate(flops=10**6, bytes_accessed=4 * 10**6, transcendentals=0),
        name="edge_rows",
    )(images, valid_mask)


def local_kernel(image_ref, mask_ref, all_ref, gram_ref, rows_ref, masks_ref, turned_ref, z_ref, in_sems, out_sems):
    groups = all_ref.shape[1]
    count, columns = image_ref.shape[2:]
    fetches = fetched(image_ref, mask_ref, rows_ref, masks_ref, in_sems, range(ROWS))
    z_ref[...] = jnp.zeros_like(z_ref)
    stores = []
    total = None
    wide = groups * LANES
    for row in range(ROWS):
        fetches[row].wait()

        def put(g, k, value):
            turned_ref[row, g, k] = value
            z_ref[pl.ds(k * LANES, count), pl.ds(row * wide + g * LANES, LANES)] = value

        turned([rows_ref.at[row, 0], rows_ref.at[row, 1]], masks_ref[row : row + 1, :], SKEW[row], columns, put)
        store = pltpu.make_async_copy(turned_ref.at[row], all_ref.at[row], out_sems.at[row])
        store.start()
        stores.append(store)
        if row % 2:
            z = z_ref[:, pl.ds((row - 1) * wide, 2 * wide)]
            part = lax.dot_general(z, z, NT, preferred_element_type=jnp.float32)
            total = part if total is None else total + part
    real = total[:LANES, :LANES] + total[LANES:, LANES:]
    imag = total[LANES:, :LANES] - total[:LANES, LANES:]
    i = lax.broadcasted_iota(jnp.int32, real.shape, 0)
    j = lax.broadcasted_iota(jnp.int32, real.shape, 1)
    gram_ref[...] = jnp.where(i <= j, real, imag)
    for store in stores:
        store.wait()


def local_rows(images, valid_mask, groups):
    count = images.shape[2]
    far = pl.BlockSpec(memory_space=pl.ANY)
    return pl.pallas_call(
        local_kernel,
        in_specs=[far, far],
        out_specs=[far, pl.BlockSpec(memory_space=pltpu.VMEM)],
        out_shape=[rows_shape(ROWS, groups, count), jax.ShapeDtypeStruct((LANES, LANES), jnp.float32)],
        scratch_shapes=[
            pltpu.VMEM(images.shape, jnp.bfloat16),
            pltpu.VMEM(valid_mask.shape, jnp.int32),
            pltpu.VMEM((ROWS, groups, 2, count, LANES), jnp.bfloat16),
            pltpu.VMEM((2 * LANES, ROWS * groups * LANES), jnp.bfloat16),
            pltpu.SemaphoreType.DMA((ROWS + 1,)),
            pltpu.SemaphoreType.DMA((ROWS,)),
        ],
        compiler_params=pltpu.CompilerParams(vmem_limit_bytes=50 * 2**20),
        cost_estimate=pl.CostEstimate(flops=10**9, bytes_accessed=5 * 10**6, transcendentals=0),
        name="local_rows",
    )(images, valid_mask)


def added(terms):
    if len(terms) == 4:
        return (terms[0] + terms[2]) + (terms[1] + terms[3])
    return functools.reduce(jnp.add, terms)


def slab_values(terms):
    packed = added(terms)
    flipped = packed.T
    i = lax.broadcasted_iota(jnp.int32, packed.shape, 0)
    j = lax.broadcasted_iota(jnp.int32, packed.shape, 1)
    real = jnp.where(i <= j, packed, flipped)
    imag = jnp.where(i > j, packed, jnp.where(i < j, -flipped, 0.0))
    powers = jnp.where(i == j, packed, 0.0)
    scaled = jnp.sqrt(jnp.sum(powers, axis=1, keepdims=True) * jnp.sum(powers, axis=0, keepdims=True))
    return real / scaled, imag / scaled


TILES = ((-3, -2, -1, 0, 1, 2), (3, 4, 5, 6, 7, 8))
LAST = ROWS + AFTER - 1
WINDOWS = tuple(tuple(range(2 * w - 3, 2 * w + 4)) for w in range(ROWS // 2))


def looks_kernel(aliased, terms, *refs):
    before_ref, all_ref, after_ref = refs[:3]
    refs = refs[3 + aliased :]
    term_refs, refs = refs[:terms], refs[terms:]
    if terms:
        out_ref, slab_ref, w_ref, g_ref, last_ref, e_ref = refs
    else:
        out_ref, w_ref, g_ref, last_ref, e_ref = refs
    count = all_ref.shape[3]

    @pl.when(pl.program_id(0) == 0)
    def _():
        w_ref[...] = jnp.zeros_like(w_ref)
        last_ref[...] = jnp.zeros_like(last_ref)
        if terms:
            real, imag = slab_values([t[...] for t in term_refs])
            slab_ref[0] = real[:count, :count]
            slab_ref[1] = imag[:count, :count]

    rows = {r: all_ref.at[r, 0] for r in range(ROWS)}
    for r in range(BEFORE):
        rows[r - BEFORE] = before_ref.at[r, 0]
    for r in range(AFTER):
        rows[ROWS + r] = after_ref.at[r, 0]

    lane = lax.broadcasted_iota(jnp.int32, (1, LANES), 1)

    def lanes_of(turn):
        place = lane + (-LOOK * turn) % LANES
        place = jnp.where(place >= LANES, place - LANES, place)
        return place < LOOK

    def widened(which):
        return jnp.broadcast_to(which.astype(jnp.float32), (count, LANES)).astype(jnp.bfloat16) != 0

    single = [lanes_of(t) for t in range(2 * PER - 1)]
    wide = [widened(s) for s in single]

    def turn(l, r):
        return l + SKEW[r % ROWS]

    def gathered(l, k, which):
        out = rows[which[0]][k]
        for r in which[1:]:
            out = jnp.where(wide[turn(l, r)], rows[r][k], out)
        return out

    def kept(l, which):
        select = jnp.zeros((1, LANES), jnp.bool_)
        for r in which:
            select = select | single[turn(l, r)]
        return select.astype(jnp.float32)

    def masked(value, lanes):
        lanes = jnp.broadcast_to(lanes, value.shape).astype(jnp.bfloat16) != 0
        value = jnp.where(lanes, value, jnp.zeros_like(value))
        parts = []
        for start in range(0, LANES, TILE):
            parts += [value[start : start + TILE], value[LANES + start : LANES + start + TILE]]
        return parts

    def combined(gram, base, put):
        for start in range(0, LANES, TILE):
            at = base + 2 * start
            re, im = gram[at : at + TILE], gram[at + TILE : at + 2 * TILE]
            put(start, re[:, :LANES] + im[:, LANES:], im[:, :LANES] - re[:, LANES:])

    for k in range(2):
        last_ref[k, pl.ds(0, count), :] = rows[LAST][k]
    last = last_ref[...].reshape(2 * LANES, LANES)
    reads = []
    for l in range(PER):
        reads += masked(last, kept(l, (LAST,)))
    last_gram = lax.dot_general(jnp.concatenate(reads, axis=0), last, NT, preferred_element_type=jnp.float32)
    for l in range(PER):

        def put_last(start, real, imag):
            e_ref[l, 0, pl.ds(start, TILE)] = real
            e_ref[l, 1, pl.ds(start, TILE)] = imag

        combined(last_gram, 2 * LANES * l, put_last)

    eight = (8, LANES)
    along = lax.broadcasted_iota(jnp.int32, eight, 1)
    on_eye = along % 8 == lax.broadcasted_iota(jnp.int32, eight, 0)
    block = along // 8

    def products(l):
        slot = l % 2
        for k in range(2):
            for t, which in enumerate(TILES):
                w_ref[slot, k, pl.ds(0, count), pl.ds(t * LANES, LANES)] = gathered(l, k, which)
        every = w_ref[slot].reshape(2 * LANES, 2 * LANES)
        reads = []
        for window in WINDOWS:
            lanes = [kept(l, [r for r in which if r in window]) for which in TILES]
            reads += masked(every, jnp.concatenate(lanes, axis=1))
        gram = lax.dot_general(jnp.concatenate(reads, axis=0), every, NT, preferred_element_type=jnp.float32)
        for w, window in enumerate(WINDOWS):

            def put(start, real, imag):
                if LAST in window:
                    real = real + e_ref[l, 0, pl.ds(start, TILE)]
                    imag = imag + e_ref[l, 1, pl.ds(start, TILE)]
                g_ref[slot, w, 0, pl.ds(start, TILE)] = real
                g_ref[slot, w, 1, pl.ds(start, TILE)] = imag

            combined(gram, 2 * LANES * w, put)

    def normalised(l):
        for w in range(len(WINDOWS)):
            real, imag = g_ref.at[l % 2, w, 0], g_ref.at[l % 2, w, 1]
            picked = real[0:8]
            for v in range(1, count // 8):
                picked = jnp.where(block == v, real[8 * v : 8 * v + 8], picked)
            power = jnp.sum(jnp.where(on_eye, picked, 0.0), axis=0, keepdims=True)
            across = lax.rsqrt(jnp.maximum(power, floor_power))
            diagonal = jnp.where(on_eye, across, 0.0)
            spread = jnp.concatenate([jnp.where(block == v, diagonal, 0.0) for v in range(count // 8)], axis=0)
            scale = jnp.sum(spread, axis=1, keepdims=True) * across
            out_ref[w, l, 0] = (real[0:count] * scale).astype(jnp.bfloat16)[:, :count]
            out_ref[w, l, 1] = (imag[0:count] * scale).astype(jnp.bfloat16)[:, :count]

    products(0)
    for l in range(PER):
        if l + 1 < PER:
            products(l + 1)
        normalised(l)


def looked(before, rows, after, first, groups, looks, previous, terms):
    count = rows.shape[3]

    def spec(array, offset):
        return pl.BlockSpec((array.shape[0], 1) + array.shape[2:], lambda s: (0, s + offset, 0, 0, 0))

    operands = [before, rows, after]
    in_specs = [spec(before, 0), spec(rows, first), spec(after, first)]
    aliases = {}
    if previous is not None:
        aliases = {len(operands): 0}
        operands.append(previous)
        in_specs.append(pl.BlockSpec(memory_space=pl.ANY))
    for term in terms:
        operands.append(term)
        in_specs.append(pl.BlockSpec(term.shape, lambda s: (0, 0)))
    out_specs = [pl.BlockSpec((ROWS // 2, PER, 2, count, count), lambda s: (0, s + first, 0, 0, 0))]
    out_shape = [jax.ShapeDtypeStruct((ROWS // 2, looks, 2, count, count), jnp.bfloat16)]
    if terms:
        out_specs.append(pl.BlockSpec((2, count, count), lambda s: (0, 0, 0)))
        out_shape.append(jax.ShapeDtypeStruct((2, count, count), jnp.float32))
    return pl.pallas_call(
        functools.partial(looks_kernel, previous is not None, len(terms)),
        grid=(groups,),
        in_specs=in_specs,
        out_specs=out_specs,
        out_shape=out_shape,
        input_output_aliases=aliases,
        scratch_shapes=[
            pltpu.VMEM((2, 2, LANES, 2 * LANES), jnp.bfloat16),
            pltpu.VMEM((2, ROWS // 2, 2, LANES, LANES), jnp.float32),
            pltpu.VMEM((2, LANES, LANES), jnp.bfloat16),
            pltpu.VMEM((PER, 2, LANES, LANES), jnp.float32),
        ],
        compiler_params=pltpu.CompilerParams(vmem_limit_bytes=49 * 2**20),
        cost_estimate=pl.CostEstimate(
            flops=1 * groups * PER * 2 * 1024 * 256 * 256, bytes_accessed=2 * groups * 10**6, transcendentals=0
        ),
        name="looks",
    )(*operands)


def rounds(size):
    found = []
    stride = 1
    while stride < size:
        radix = 4 if size // stride % 4 == 0 else 2
        if size // stride % radix:
            return None
        found.append((stride, radix))
        stride *= radix
    return found[::-1]


def round_terms(value, axis, stride, radix):
    size = lax.axis_size(axis)
    terms = [value]
    for shift in range(1, radix):
        pairs = []
        for i in range(size):
            place = (i // stride) % radix
            pairs.append((i, i + ((place + shift) % radix - place) * stride))
        terms.append(lax.ppermute(value, axis, pairs))
    return terms


def shards(images, valid_mask):
    looks = images.shape[3] // LOOK
    groups = -(-looks // PER)
    cut = -(-groups // 2)
    size = lax.axis_size("pix")
    forward = [(i, i + 1) for i in range(size - 1)]
    backward = [(i + 1, i) for i in range(size - 1)]
    top, low0, low1 = edge_rows(images, valid_mask, groups, cut)
    after = lax.ppermute(top, "pix", backward)
    before0 = lax.ppermute(low0, "pix", forward)
    before1 = lax.ppermute(low1, "pix", forward)
    rows, total = local_rows(images, valid_mask, groups)
    terms = [total]
    steps = rounds(size)
    if steps is None:
        terms, steps = [lax.psum(total, "pix")], []
    for step in steps:
        terms = round_terms(added(terms), "pix", *step)
    (out,) = looked(before0, rows, after, 0, cut, looks, None, [])
    out, slab = looked(before1, rows, after, cut, groups - cut, looks, out, terms)
    return (out, slab)


def solution(mesh):
    in_specs = (P(("group", "pix"), None, None, None), P(("group", "pix"), None))
    out_specs = (P(("group", "pix"), None, None, None, None), P("group", None, None))
    return jax.shard_map(shards, mesh=mesh, in_specs=in_specs, out_specs=out_specs, check_vma=False)
```

```python
import functools
import jax
import jax.numpy as jnp
from jax import lax
from jax.experimental import pallas as pl
from jax.experimental.pallas import tpu as pltpu
from jax.sharding import PartitionSpec as P

floor_power = 30.0

LOOK = 21
LANES = 128
TILE = 16
PER = LANES // LOOK
SPAN = PER * LOOK
ROWS = 8
SKEW = (5, 0, 1, 2, 3, 4, 1, 2)
BEFORE, AFTER = 3, 2
NT = (((1,), (1,)), ((), ()))


def turned(image, mask, skew, columns, put):
    count = image[0].shape[0]
    zero = jnp.zeros((count, LANES), jnp.bfloat16)
    lane = lax.broadcasted_iota(jnp.int32, (1, LANES), 1)

    def tile(value, g):
        start, stop = g * LANES, min((g + 1) * LANES, columns)
        part = value[:, start:stop]
        if stop - start < LANES:
            rest = jnp.zeros((part.shape[0], LANES - (stop - start)), part.dtype)
            part = jnp.concatenate([part, rest], axis=1)
        return part

    def widened(which):
        return jnp.broadcast_to(which.astype(jnp.float32), (count, LANES)).astype(jnp.bfloat16) != 0

    tiles = -(-columns // LANES)
    for g in range(-(-columns // SPAN)):
        slide = (LANES - SPAN) * g
        place = (lane + slide) % LANES
        used = (place < SPAN) & (SPAN * g + place < columns)
        prior = lane >= LANES - slide
        sides = [t for t in (g - 1, g) if 0 <= t < tiles]

        def joined(value):
            parts = [tile(value, t) for t in sides]
            if len(parts) == 1:
                return parts[0]
            which = prior if value.shape[0] == 1 else widened(prior)
            return jnp.where(which, parts[0], parts[1])

        keep = widened(used & (joined(mask) != 0))
        for k in range(2):
            row = jnp.where(keep, joined(image[k]), zero)
            put(g, k, pltpu.roll(row, slide + LOOK * skew, 1))


def fetched(image_ref, mask_ref, rows_ref, masks_ref, sems, order):
    mask_copy = pltpu.make_async_copy(mask_ref, masks_ref, sems.at[len(order)])
    mask_copy.start()
    copies = [pltpu.make_async_copy(image_ref.at[row], rows_ref.at[at], sems.at[at]) for at, row in enumerate(order)]
    for copy in copies:
        copy.start()
    mask_copy.wait()
    return copies


EDGE = tuple(range(AFTER)) + tuple(range(ROWS - BEFORE, ROWS))


def edge_kernel(image_ref, mask_ref, top_ref, low_ref, rows_ref, masks_ref, turned_ref, in_sems, out_sems):
    fetches = fetched(image_ref, mask_ref, rows_ref, masks_ref, in_sems, EDGE)
    stores = []
    for at, row in enumerate(EDGE):
        fetches[at].wait()

        def put(g, k, value):
            turned_ref[at, g, k] = value

        turned([rows_ref.at[at, 0], rows_ref.at[at, 1]], masks_ref[row : row + 1, :], SKEW[row], masks_ref.shape[1], put)
        target = top_ref.at[row] if row < AFTER else low_ref.at[row - (ROWS - BEFORE)]
        store = pltpu.make_async_copy(turned_ref.at[at], target, out_sems.at[at])
        store.start()
        stores.append(store)
    for store in stores:
        store.wait()


def rows_shape(rows, groups, count):
    return jax.ShapeDtypeStruct((rows, groups, 2, count, LANES), jnp.bfloat16)


def edge_rows(images, valid_mask, groups):
    count = images.shape[2]
    far = pl.BlockSpec(memory_space=pl.ANY)
    return pl.pallas_call(
        edge_kernel,
        in_specs=[far, far],
        out_specs=[far] * 2,
        out_shape=[
            rows_shape(AFTER, groups, count),
            rows_shape(BEFORE, groups, count),
        ],
        scratch_shapes=[
            pltpu.VMEM((len(EDGE),) + images.shape[1:], jnp.bfloat16),
            pltpu.VMEM(valid_mask.shape, jnp.int32),
            pltpu.VMEM((len(EDGE), groups, 2, count, LANES), jnp.bfloat16),
            pltpu.SemaphoreType.DMA((len(EDGE) + 1,)),
            pltpu.SemaphoreType.DMA((len(EDGE),)),
        ],
        compiler_params=pltpu.CompilerParams(vmem_limit_bytes=61 * 2**20),
        cost_estimate=pl.CostEstimate(flops=10**6, bytes_accessed=4 * 10**6, transcendentals=0),
        name="edge_rows",
    )(images, valid_mask)


def local_kernel(image_ref, mask_ref, all_ref, gram_ref, rows_ref, masks_ref, turned_ref, z_ref, in_sems, out_sems):
    groups = all_ref.shape[1]
    count, columns = image_ref.shape[2:]
    fetches = fetched(image_ref, mask_ref, rows_ref, masks_ref, in_sems, range(ROWS))
    z_ref[...] = jnp.zeros_like(z_ref)
    stores = []
    total = None
    wide = groups * LANES
    for row in range(ROWS):
        fetches[row].wait()

        def put(g, k, value):
            turned_ref[row, g, k] = value
            z_ref[pl.ds(k * LANES, count), pl.ds(row * wide + g * LANES, LANES)] = value

        turned([rows_ref.at[row, 0], rows_ref.at[row, 1]], masks_ref[row : row + 1, :], SKEW[row], columns, put)
        store = pltpu.make_async_copy(turned_ref.at[row], all_ref.at[row], out_sems.at[row])
        store.start()
        stores.append(store)
        if row % 2:
            z = z_ref[:, pl.ds((row - 1) * wide, 2 * wide)]
            part = lax.dot_general(z, z, NT, preferred_element_type=jnp.float32)
            total = part if total is None else total + part
    real = total[:LANES, :LANES] + total[LANES:, LANES:]
    imag = total[LANES:, :LANES] - total[:LANES, LANES:]
    i = lax.broadcasted_iota(jnp.int32, real.shape, 0)
    j = lax.broadcasted_iota(jnp.int32, real.shape, 1)
    gram_ref[...] = jnp.where(i <= j, real, imag)
    for store in stores:
        store.wait()


def local_rows(images, valid_mask, groups):
    count = images.shape[2]
    far = pl.BlockSpec(memory_space=pl.ANY)
    return pl.pallas_call(
        local_kernel,
        in_specs=[far, far],
        out_specs=[far, pl.BlockSpec(memory_space=pltpu.VMEM)],
        out_shape=[rows_shape(ROWS, groups, count), jax.ShapeDtypeStruct((LANES, LANES), jnp.float32)],
        scratch_shapes=[
            pltpu.VMEM(images.shape, jnp.bfloat16),
            pltpu.VMEM(valid_mask.shape, jnp.int32),
            pltpu.VMEM((ROWS, groups, 2, count, LANES), jnp.bfloat16),
            pltpu.VMEM((2 * LANES, ROWS * groups * LANES), jnp.bfloat16),
            pltpu.SemaphoreType.DMA((ROWS + 1,)),
            pltpu.SemaphoreType.DMA((ROWS,)),
        ],
        compiler_params=pltpu.CompilerParams(vmem_limit_bytes=50 * 2**20),
        cost_estimate=pl.CostEstimate(flops=10**9, bytes_accessed=5 * 10**6, transcendentals=0),
        name="local_rows",
    )(images, valid_mask)


def added(terms):
    if len(terms) == 4:
        return (terms[0] + terms[2]) + (terms[1] + terms[3])
    return functools.reduce(jnp.add, terms)


def slab_values(terms):
    packed = added(terms)
    flipped = packed.T
    i = lax.broadcasted_iota(jnp.int32, packed.shape, 0)
    j = lax.broadcasted_iota(jnp.int32, packed.shape, 1)
    real = jnp.where(i <= j, packed, flipped)
    imag = jnp.where(i > j, packed, jnp.where(i < j, -flipped, 0.0))
    powers = jnp.where(i == j, packed, 0.0)
    scaled = jnp.sqrt(jnp.sum(powers, axis=1, keepdims=True) * jnp.sum(powers, axis=0, keepdims=True))
    return real / scaled, imag / scaled


INNER = (1, 2, 3, 4, 5)
HALVES = (
    ((-3, -2, -1, 0), (((1, 2, 3), None), (None, (-1, 0)))),
    ((6, 7, 8, 9), ((None, (6, 7)), ((3, 4, 5), None))),
)


def looks_kernel(half, aliased, terms, slab, *refs):
    other_ref, all_ref = refs[:2]
    refs = refs[2 + aliased :]
    term_refs, refs = refs[:terms], refs[terms:]
    out_ref, extra_ref, w_ref, g_ref = refs
    count = all_ref.shape[3]

    @pl.when(pl.program_id(0) == 0)
    def _():
        w_ref[...] = jnp.zeros_like(w_ref)
        if slab:
            real, imag = slab_values([t[...] for t in term_refs])
            extra_ref[0] = real[:count, :count]
            extra_ref[1] = imag[:count, :count]
        elif terms:
            extra_ref[...] = added([t[...] for t in term_refs])
        else:
            extra_ref[...] = jnp.zeros_like(extra_ref)

    rows = {r: all_ref.at[r, 0] for r in range(ROWS)}
    for r in range(other_ref.shape[0]):
        rows[ROWS + r if half else r - BEFORE] = other_ref.at[r, 0]

    lane = lax.broadcasted_iota(jnp.int32, (1, LANES), 1)

    def lanes_of(turn):
        place = lane + (-LOOK * turn) % LANES
        place = jnp.where(place >= LANES, place - LANES, place)
        return place < LOOK

    def widened(which):
        return jnp.broadcast_to(which.astype(jnp.float32), (count, LANES)).astype(jnp.bfloat16) != 0

    single = [lanes_of(t) for t in range(2 * PER - 1)]
    wide = [widened(s) for s in single]

    def turn(l, r):
        return l + SKEW[r % ROWS]

    def gathered(l, k, which):
        out = rows[which[0]][k]
        for r in which[1:]:
            out = jnp.where(wide[turn(l, r)], rows[r][k], out)
        return out

    def kept(l, which):
        select = single[turn(l, which[0])]
        for r in which[1:]:
            select = select | single[turn(l, r)]
        return select.astype(jnp.float32)

    eight = (8, LANES)
    along = lax.broadcasted_iota(jnp.int32, eight, 1)
    on_eye = along % 8 == lax.broadcasted_iota(jnp.int32, eight, 0)
    block = along // 8

    outer_rows, windows = HALVES[half]

    def products(l):
        slot = l % 2
        for k in range(2):
            w_ref[slot, k, pl.ds(0, count), pl.ds(0, LANES)] = gathered(l, k, INNER)
            w_ref[slot, k, pl.ds(0, count), pl.ds(LANES, LANES)] = gathered(l, k, outer_rows)
        every = w_ref[slot].reshape(2 * LANES, 2 * LANES)
        nothing = jnp.zeros_like(every)
        for w, (inner_rows, rest_rows) in enumerate(windows):
            lanes = jnp.concatenate([kept(l, inner_rows or INNER), kept(l, rest_rows or outer_rows)], axis=1)
            lanes = jnp.broadcast_to(lanes, every.shape).astype(jnp.bfloat16) != 0
            read = jnp.where(lanes, every, nothing)
            reads = []
            for start in range(0, LANES, TILE):
                reads.append(read[start : start + TILE])
                reads.append(read[LANES + start : LANES + start + TILE])
            gram = lax.dot_general(jnp.concatenate(reads, axis=0), every, NT, preferred_element_type=jnp.float32)
            for start in range(0, LANES, TILE):
                re, im = gram[2 * start : 2 * start + TILE], gram[2 * start + TILE : 2 * start + 2 * TILE]
                g_ref[slot, w, 0, pl.ds(start, TILE)] = re[:, :LANES] + im[:, LANES:]
                g_ref[slot, w, 1, pl.ds(start, TILE)] = im[:, :LANES] - re[:, LANES:]

    def normalised(l):
        for w in range(2):
            real, imag = g_ref.at[l % 2, w, 0], g_ref.at[l % 2, w, 1]
            picked = real[0:8]
            for v in range(1, count // 8):
                picked = jnp.where(block == v, real[8 * v : 8 * v + 8], picked)
            power = jnp.sum(jnp.where(on_eye, picked, 0.0), axis=0, keepdims=True)
            across = lax.rsqrt(jnp.maximum(power, floor_power))
            diagonal = jnp.where(on_eye, across, 0.0)
            spread = jnp.concatenate([jnp.where(block == v, diagonal, 0.0) for v in range(count // 8)], axis=0)
            scale = jnp.sum(spread, axis=1, keepdims=True) * across
            out_ref[w, l, 0] = (real[0:count] * scale).astype(jnp.bfloat16)[:, :count]
            out_ref[w, l, 1] = (imag[0:count] * scale).astype(jnp.bfloat16)[:, :count]

    products(0)
    for l in range(PER):
        if l + 1 < PER:
            products(l + 1)
        normalised(l)


def looked(half, other, rows, first, groups, looks, previous, terms, slab):
    count = other.shape[3]

    def spec(array):
        return pl.BlockSpec((array.shape[0], 1) + array.shape[2:], lambda s: (0, s + first, 0, 0, 0))

    operands = [other, rows]
    in_specs = [spec(a) for a in operands]
    aliases = {}
    if previous is not None:
        aliases = {len(operands): 0}
        operands.append(previous)
        in_specs.append(pl.BlockSpec(memory_space=pl.ANY))
    for term in terms:
        operands.append(term)
        in_specs.append(pl.BlockSpec(term.shape, lambda s: (0, 0)))
    extra = (2, count, count) if slab else (LANES, LANES)
    out_specs = [
        pl.BlockSpec((2, PER, 2, count, count), lambda s: (half, s + first, 0, 0, 0)),
        pl.BlockSpec(extra, lambda s: (0,) * len(extra)),
    ]
    out_shape = [
        jax.ShapeDtypeStruct((ROWS // 2, looks, 2, count, count), jnp.bfloat16),
        jax.ShapeDtypeStruct(extra, jnp.float32),
    ]
    return pl.pallas_call(
        functools.partial(looks_kernel, half, previous is not None, len(terms), slab),
        grid=(groups,),
        in_specs=in_specs,
        out_specs=out_specs,
        out_shape=out_shape,
        input_output_aliases=aliases,
        scratch_shapes=[
            pltpu.VMEM((2, 2, LANES, 2 * LANES), jnp.bfloat16),
            pltpu.VMEM((2, 2, 2, LANES, LANES), jnp.float32),
        ],
        compiler_params=pltpu.CompilerParams(vmem_limit_bytes=49 * 2**20),
        cost_estimate=pl.CostEstimate(
            flops=1 * groups * PER * 2 * 512 * 256 * 256, bytes_accessed=groups * 10**6, transcendentals=0
        ),
        name="looks",
    )(*operands)


def rounds(size):
    found = []
    stride = 1
    while stride < size:
        radix = 4 if size // stride % 4 == 0 else 2
        if size // stride % radix:
            return None
        found.append((stride, radix))
        stride *= radix
    return found[::-1]


def round_terms(value, axis, stride, radix):
    size = lax.axis_size(axis)
    terms = [value]
    for shift in range(1, radix):
        pairs = []
        for i in range(size):
            place = (i // stride) % radix
            pairs.append((i, i + ((place + shift) % radix - place) * stride))
        terms.append(lax.ppermute(value, axis, pairs))
    return terms


def shards(images, valid_mask):
    looks = images.shape[3] // LOOK
    groups = -(-looks // PER)
    cut = -(-groups // 2)
    size = lax.axis_size("pix")
    forward = [(i, i + 1) for i in range(size - 1)]
    backward = [(i + 1, i) for i in range(size - 1)]
    top, low = edge_rows(images, valid_mask, groups)
    after = lax.ppermute(top, "pix", backward)
    before = lax.ppermute(low, "pix", forward)
    rows, total = local_rows(images, valid_mask, groups)
    steps = rounds(size)
    if steps is None:
        terms, steps = [lax.psum(total, "pix")], []
    else:
        terms = round_terms(total, "pix", *steps[0]) if steps else [total]
    out, zeros = looked(1, after, rows, 0, groups, looks, None, [], False)
    for step in steps[1:]:
        terms = round_terms(added(terms) + zeros, "pix", *step)
    out, _ = looked(0, before, rows, 0, cut, looks, out, [], False)
    out, slab = looked(0, before, rows, cut, groups - cut, looks, out, terms, True)
    return (out, slab)


def solution(mesh):
    in_specs = (P(("group", "pix"), None, None, None), P(("group", "pix"), None))
    out_specs = (P(("group", "pix"), None, None, None, None), P("group", None, None))
    return jax.shard_map(shards, mesh=mesh, in_specs=in_specs, out_specs=out_specs, check_vma=False)
```

```python
import functools
import jax
import jax.numpy as jnp
from jax import lax
from jax.experimental import pallas as pl
from jax.experimental.pallas import tpu as pltpu
from jax.sharding import PartitionSpec as P

floor_power = 30.0

LOOK = 21
LANES = 128
TILE = 16
PER = LANES // LOOK
SPAN = PER * LOOK
ROWS = 8
SKEW = (5, 0, 1, 2, 3, 4, 1, 2)
BEFORE, AFTER = 3, 2
NT = (((1,), (1,)), ((), ()))


def turned(image, mask, skew, columns, put):
    count = image[0].shape[0]
    zero = jnp.zeros((count, LANES), jnp.bfloat16)
    lane = lax.broadcasted_iota(jnp.int32, (1, LANES), 1)

    def tile(value, g):
        start, stop = g * LANES, min((g + 1) * LANES, columns)
        part = value[:, start:stop]
        if stop - start < LANES:
            rest = jnp.zeros((part.shape[0], LANES - (stop - start)), part.dtype)
            part = jnp.concatenate([part, rest], axis=1)
        return part

    def widened(which):
        return jnp.broadcast_to(which.astype(jnp.float32), (count, LANES)).astype(jnp.bfloat16) != 0

    tiles = -(-columns // LANES)
    for g in range(-(-columns // SPAN)):
        slide = (LANES - SPAN) * g
        place = (lane + slide) % LANES
        used = (place < SPAN) & (SPAN * g + place < columns)
        prior = lane >= LANES - slide
        sides = [t for t in (g - 1, g) if 0 <= t < tiles]

        def joined(value):
            parts = [tile(value, t) for t in sides]
            if len(parts) == 1:
                return parts[0]
            which = prior if value.shape[0] == 1 else widened(prior)
            return jnp.where(which, parts[0], parts[1])

        keep = widened(used & (joined(mask) != 0))
        for k in range(2):
            row = jnp.where(keep, joined(image[k]), zero)
            put(g, k, pltpu.roll(row, slide + LOOK * skew, 1))


def fetched(image_ref, mask_ref, rows_ref, masks_ref, sems, order):
    mask_copy = pltpu.make_async_copy(mask_ref, masks_ref, sems.at[len(order)])
    mask_copy.start()
    copies = [pltpu.make_async_copy(image_ref.at[row], rows_ref.at[at], sems.at[at]) for at, row in enumerate(order)]
    for copy in copies:
        copy.start()
    mask_copy.wait()
    return copies


EDGE = tuple(range(AFTER)) + tuple(range(ROWS - BEFORE, ROWS))


def edge_kernel(image_ref, mask_ref, top_ref, low_ref, rows_ref, masks_ref, turned_ref, in_sems, out_sems):
    fetches = fetched(image_ref, mask_ref, rows_ref, masks_ref, in_sems, EDGE)
    stores = []
    for at, row in enumerate(EDGE):
        fetches[at].wait()

        def put(g, k, value):
            turned_ref[at, g, k] = value

        turned([rows_ref.at[at, 0], rows_ref.at[at, 1]], masks_ref[row : row + 1, :], SKEW[row], masks_ref.shape[1], put)
        target = top_ref.at[row] if row < AFTER else low_ref.at[row - (ROWS - BEFORE)]
        store = pltpu.make_async_copy(turned_ref.at[at], target, out_sems.at[at])
        store.start()
        stores.append(store)
    for store in stores:
        store.wait()


def rows_shape(rows, groups, count):
    return jax.ShapeDtypeStruct((rows, groups, 2, count, LANES), jnp.bfloat16)


def edge_rows(images, valid_mask, groups):
    count = images.shape[2]
    far = pl.BlockSpec(memory_space=pl.ANY)
    return pl.pallas_call(
        edge_kernel,
        in_specs=[far, far],
        out_specs=[far] * 2,
        out_shape=[
            rows_shape(AFTER, groups, count),
            rows_shape(BEFORE, groups, count),
        ],
        scratch_shapes=[
            pltpu.VMEM((len(EDGE),) + images.shape[1:], jnp.bfloat16),
            pltpu.VMEM(valid_mask.shape, jnp.int32),
            pltpu.VMEM((len(EDGE), groups, 2, count, LANES), jnp.bfloat16),
            pltpu.SemaphoreType.DMA((len(EDGE) + 1,)),
            pltpu.SemaphoreType.DMA((len(EDGE),)),
        ],
        compiler_params=pltpu.CompilerParams(vmem_limit_bytes=61 * 2**20),
        cost_estimate=pl.CostEstimate(flops=10**6, bytes_accessed=4 * 10**6, transcendentals=0),
        name="edge_rows",
    )(images, valid_mask)


def middle_kernel(image_ref, mask_ref, low_ref, mid_ref, gram_ref, again_ref, *scratch):
    rows_ref, masks_ref, turned_ref, z_ref, in_sems, out_sems = scratch
    groups = mid_ref.shape[1]
    count, columns = image_ref.shape[2:]
    order = tuple(range(AFTER, ROWS - BEFORE)) + EDGE
    fetches = fetched(image_ref, mask_ref, rows_ref, masks_ref, in_sems, order)
    stores = [pltpu.make_async_copy(low_ref, again_ref, out_sems.at[ROWS - AFTER - BEFORE])]
    stores[0].start()
    z_ref[...] = jnp.zeros_like(z_ref)
    zero = jnp.zeros((count, columns), jnp.bfloat16)
    total = None
    wide = groups * LANES
    for at, row in enumerate(order):
        fetches[at].wait()
        mask = masks_ref[row : row + 1, :]
        if AFTER <= row < ROWS - BEFORE:

            def put(g, k, value):
                turned_ref[at, g, k] = value
                z_ref[pl.ds(k * LANES, count), pl.ds(at * wide + g * LANES, LANES)] = value

            turned([rows_ref.at[at, 0], rows_ref.at[at, 1]], mask, SKEW[row], columns, put)
            store = pltpu.make_async_copy(turned_ref.at[at], mid_ref.at[row - AFTER], out_sems.at[at])
            store.start()
            stores.append(store)
        else:
            keep = jnp.broadcast_to((mask != 0).astype(jnp.float32), (count, columns)).astype(jnp.bfloat16) != 0
            for k in range(2):
                z_ref[pl.ds(k * LANES, count), pl.ds(at * wide, columns)] = jnp.where(keep, rows_ref[at, k], zero)
        if at % 2:
            z = z_ref[:, pl.ds((at - 1) * wide, 2 * wide)]
            part = lax.dot_general(z, z, NT, preferred_element_type=jnp.float32)
            total = part if total is None else total + part
    real = total[:LANES, :LANES] + total[LANES:, LANES:]
    imag = total[LANES:, :LANES] - total[:LANES, LANES:]
    i = lax.broadcasted_iota(jnp.int32, real.shape, 0)
    j = lax.broadcasted_iota(jnp.int32, real.shape, 1)
    gram_ref[...] = jnp.where(i <= j, real, imag)
    for store in stores:
        store.wait()


def middle_rows(images, valid_mask, low):
    count = images.shape[2]
    groups = low.shape[1]
    rows = ROWS - AFTER - BEFORE
    far = pl.BlockSpec(memory_space=pl.ANY)
    return pl.pallas_call(
        middle_kernel,
        in_specs=[far, far, far],
        out_specs=[far, pl.BlockSpec(memory_space=pltpu.VMEM), far],
        out_shape=[
            rows_shape(rows, groups, count),
            jax.ShapeDtypeStruct((LANES, LANES), jnp.float32),
            jax.ShapeDtypeStruct(low.shape, low.dtype),
        ],
        scratch_shapes=[
            pltpu.VMEM(images.shape, jnp.bfloat16),
            pltpu.VMEM(valid_mask.shape, jnp.int32),
            pltpu.VMEM((rows, groups, 2, count, LANES), jnp.bfloat16),
            pltpu.VMEM((2 * LANES, ROWS * groups * LANES), jnp.bfloat16),
            pltpu.SemaphoreType.DMA((ROWS + 1,)),
            pltpu.SemaphoreType.DMA((rows + 1,)),
        ],
        compiler_params=pltpu.CompilerParams(vmem_limit_bytes=51 * 2**20),
        cost_estimate=pl.CostEstimate(flops=10**9, bytes_accessed=5 * 10**6, transcendentals=0),
        name="middle_rows",
    )(images, valid_mask, low)


def added(terms):
    if len(terms) == 4:
        return (terms[0] + terms[2]) + (terms[1] + terms[3])
    return functools.reduce(jnp.add, terms)


def slab_values(terms):
    packed = added(terms)
    flipped = packed.T
    i = lax.broadcasted_iota(jnp.int32, packed.shape, 0)
    j = lax.broadcasted_iota(jnp.int32, packed.shape, 1)
    real = jnp.where(i <= j, packed, flipped)
    imag = jnp.where(i > j, packed, jnp.where(i < j, -flipped, 0.0))
    powers = jnp.where(i == j, packed, 0.0)
    scaled = jnp.sqrt(jnp.sum(powers, axis=1, keepdims=True) * jnp.sum(powers, axis=0, keepdims=True))
    return real / scaled, imag / scaled


INNER = (1, 2, 3, 4, 5)
HALVES = (
    ((-3, -2, -1, 0), (((1, 2, 3), None), (None, (-1, 0)))),
    ((6, 7, 8, 9), ((None, (6, 7)), ((3, 4, 5), None))),
)


def looks_kernel(half, aliased, terms, slab, *refs):
    other_ref, top_ref, mid_ref, low_ref = refs[:4]
    refs = refs[4 + aliased :]
    term_refs, refs = refs[:terms], refs[terms:]
    out_ref, extra_ref, w_ref = refs
    count = top_ref.shape[3]

    @pl.when(pl.program_id(0) == 0)
    def _():
        w_ref[...] = jnp.zeros_like(w_ref)
        if slab:
            real, imag = slab_values([t[...] for t in term_refs])
            extra_ref[0] = real[:count, :count]
            extra_ref[1] = imag[:count, :count]
        elif terms:
            extra_ref[...] = added([t[...] for t in term_refs])
        else:
            extra_ref[...] = jnp.zeros_like(extra_ref)

    rows = {}
    for r in range(ROWS):
        if r < AFTER:
            rows[r] = top_ref.at[r, 0]
        elif r >= ROWS - BEFORE:
            rows[r] = low_ref.at[r - (ROWS - BEFORE), 0]
        else:
            rows[r] = mid_ref.at[r - AFTER, 0]
    for r in range(other_ref.shape[0]):
        rows[ROWS + r if half else r - BEFORE] = other_ref.at[r, 0]

    lane = lax.broadcasted_iota(jnp.int32, (1, LANES), 1)

    def lanes_of(turn):
        place = lane + (-LOOK * turn) % LANES
        place = jnp.where(place >= LANES, place - LANES, place)
        return place < LOOK

    def widened(which):
        return jnp.broadcast_to(which.astype(jnp.float32), (count, LANES)).astype(jnp.bfloat16) != 0

    single = [lanes_of(t) for t in range(2 * PER - 1)]
    wide = [widened(s) for s in single]

    def turn(l, r):
        return l + SKEW[r % ROWS]

    def gathered(l, k, which):
        out = rows[which[0]][k]
        for r in which[1:]:
            out = jnp.where(wide[turn(l, r)], rows[r][k], out)
        return out

    def kept(l, which):
        select = single[turn(l, which[0])]
        for r in which[1:]:
            select = select | single[turn(l, r)]
        return select.astype(jnp.float32)

    eight = (8, LANES)
    along = lax.broadcasted_iota(jnp.int32, eight, 1)
    on_eye = along % 8 == lax.broadcasted_iota(jnp.int32, eight, 0)
    block = along // 8

    def normalised(real, imag, w, l):
        picked = real[:8]
        for v in range(1, count // 8):
            picked = jnp.where(block == v, real[8 * v : 8 * v + 8], picked)
        power = jnp.sum(jnp.where(on_eye, picked, 0.0), axis=0, keepdims=True)
        across = lax.rsqrt(jnp.maximum(power, floor_power))
        diagonal = jnp.where(on_eye, across, 0.0)
        spread = jnp.concatenate([jnp.where(block == v, diagonal, 0.0) for v in range(count // 8)], axis=0)
        scale = jnp.sum(spread, axis=1, keepdims=True) * across
        out_ref[w, l, 0] = (real * scale).astype(jnp.bfloat16)[:, :count]
        out_ref[w, l, 1] = (imag * scale).astype(jnp.bfloat16)[:, :count]

    outer_rows, windows = HALVES[half]
    for l in range(PER):
        slot = l % 2
        for k in range(2):
            w_ref[slot, k, pl.ds(0, count), pl.ds(0, LANES)] = gathered(l, k, INNER)
            w_ref[slot, k, pl.ds(0, count), pl.ds(LANES, LANES)] = gathered(l, k, outer_rows)
        every = w_ref[slot].reshape(2 * LANES, 2 * LANES)
        nothing = jnp.zeros_like(every)
        reads = []
        for inner_rows, rest_rows in windows:
            lanes = jnp.concatenate([kept(l, inner_rows or INNER), kept(l, rest_rows or outer_rows)], axis=1)
            lanes = jnp.broadcast_to(lanes, every.shape).astype(jnp.bfloat16) != 0
            read = jnp.where(lanes, every, nothing)
            for start in range(0, LANES, TILE):
                reads.append(read[start : start + TILE])
                reads.append(read[LANES + start : LANES + start + TILE])
        gram = lax.dot_general(jnp.concatenate(reads, axis=0), every, NT, preferred_element_type=jnp.float32)
        for w in range(2):
            real, imag = [], []
            for start in range(0, LANES, TILE):
                base = 2 * (w * LANES + start)
                re, im = gram[base : base + TILE], gram[base + TILE : base + 2 * TILE]
                real.append(re[:, :LANES] + im[:, LANES:])
                imag.append(im[:, :LANES] - re[:, LANES:])
            normalised(jnp.concatenate(real, axis=0)[:count], jnp.concatenate(imag, axis=0)[:count], w, l)


def looked(half, other, top, mid, low, first, groups, looks, previous, terms, slab):
    count = other.shape[3]

    def spec(array):
        return pl.BlockSpec((array.shape[0], 1) + array.shape[2:], lambda s: (0, s + first, 0, 0, 0))

    operands = [other, top, mid, low]
    in_specs = [spec(a) for a in operands]
    aliases = {}
    if previous is not None:
        aliases = {len(operands): 0}
        operands.append(previous)
        in_specs.append(pl.BlockSpec(memory_space=pl.ANY))
    for term in terms:
        operands.append(term)
        in_specs.append(pl.BlockSpec(term.shape, lambda s: (0, 0)))
    extra = (2, count, count) if slab else (LANES, LANES)
    out_specs = [
        pl.BlockSpec((2, PER, 2, count, count), lambda s: (half, s + first, 0, 0, 0)),
        pl.BlockSpec(extra, lambda s: (0,) * len(extra)),
    ]
    out_shape = [
        jax.ShapeDtypeStruct((ROWS // 2, looks, 2, count, count), jnp.bfloat16),
        jax.ShapeDtypeStruct(extra, jnp.float32),
    ]
    return pl.pallas_call(
        functools.partial(looks_kernel, half, previous is not None, len(terms), slab),
        grid=(groups,),
        in_specs=in_specs,
        out_specs=out_specs,
        out_shape=out_shape,
        input_output_aliases=aliases,
        scratch_shapes=[
            pltpu.VMEM((2, 2, LANES, 2 * LANES), jnp.bfloat16),
        ],
        compiler_params=pltpu.CompilerParams(vmem_limit_bytes=48 * 2**20),
        cost_estimate=pl.CostEstimate(
            flops=2 * groups * PER * 2 * 512 * 256 * 256, bytes_accessed=groups * 10**6, transcendentals=0
        ),
        name="looks",
    )(*operands)


def rounds(size):
    found = []
    stride = 1
    while stride < size:
        radix = 4 if size // stride % 4 == 0 else 2
        if size // stride % radix:
            return None
        found.append((stride, radix))
        stride *= radix
    return found[::-1]


def round_terms(value, axis, stride, radix):
    size = lax.axis_size(axis)
    terms = [value]
    for shift in range(1, radix):
        pairs = []
        for i in range(size):
            place = (i // stride) % radix
            pairs.append((i, i + ((place + shift) % radix - place) * stride))
        terms.append(lax.ppermute(value, axis, pairs))
    return terms


def shards(images, valid_mask):
    looks = images.shape[3] // LOOK
    groups = -(-looks // PER)
    cut = -(-groups // 2)
    size = lax.axis_size("pix")
    forward = [(i, i + 1) for i in range(size - 1)]
    backward = [(i + 1, i) for i in range(size - 1)]
    top, low = edge_rows(images, valid_mask, groups)
    after = lax.ppermute(top, "pix", backward)
    mid, total, low = middle_rows(images, valid_mask, low)
    before = lax.ppermute(low, "pix", forward)
    steps = rounds(size)
    if steps is None:
        terms, steps = [lax.psum(total, "pix")], []
    else:
        terms = round_terms(total, "pix", *steps[0]) if steps else [total]
    out, zeros = looked(1, after, top, mid, low, 0, groups, looks, None, [], False)
    for step in steps[1:]:
        terms = round_terms(added(terms) + zeros, "pix", *step)
    out, _ = looked(0, before, top, mid, low, 0, cut, looks, out, [], False)
    out, slab = looked(0, before, top, mid, low, cut, groups - cut, looks, out, terms, True)
    return (out, slab)


def solution(mesh):
    in_specs = (P(("group", "pix"), None, None, None), P(("group", "pix"), None))
    out_specs = (P(("group", "pix"), None, None, None, None), P("group", None, None))
    return jax.shard_map(shards, mesh=mesh, in_specs=in_specs, out_specs=out_specs, check_vma=False)
```

```python
import functools
import jax
import jax.numpy as jnp
from jax import lax
from jax.experimental import pallas as pl
from jax.experimental.pallas import tpu as pltpu
from jax.sharding import PartitionSpec as P

floor_power = 30.0

LOOK = 21
LANES = 128
TILE = 16
PER = LANES // LOOK
SPAN = PER * LOOK
ROWS = 8
SKEW = (5, 0, 1, 2, 3, 4, 1, 2)
BEFORE, AFTER = 3, 2
NT = (((1,), (1,)), ((), ()))


def turned(image, mask, skew, columns, put):
    count = image[0].shape[0]
    zero = jnp.zeros((count, LANES), jnp.bfloat16)
    lane = lax.broadcasted_iota(jnp.int32, (1, LANES), 1)

    def tile(value, g):
        start, stop = g * LANES, min((g + 1) * LANES, columns)
        part = value[:, start:stop]
        if stop - start < LANES:
            rest = jnp.zeros((part.shape[0], LANES - (stop - start)), part.dtype)
            part = jnp.concatenate([part, rest], axis=1)
        return part

    def widened(which):
        return jnp.broadcast_to(which.astype(jnp.float32), (count, LANES)).astype(jnp.bfloat16) != 0

    tiles = -(-columns // LANES)
    for g in range(-(-columns // SPAN)):
        slide = (LANES - SPAN) * g
        place = (lane + slide) % LANES
        used = (place < SPAN) & (SPAN * g + place < columns)
        prior = lane >= LANES - slide
        sides = [t for t in (g - 1, g) if 0 <= t < tiles]

        def joined(value):
            parts = [tile(value, t) for t in sides]
            if len(parts) == 1:
                return parts[0]
            which = prior if value.shape[0] == 1 else widened(prior)
            return jnp.where(which, parts[0], parts[1])

        keep = widened(used & (joined(mask) != 0))
        for k in range(2):
            row = jnp.where(keep, joined(image[k]), zero)
            put(g, k, pltpu.roll(row, slide + LOOK * skew, 1))


def fetched(image_ref, mask_ref, rows_ref, masks_ref, sems, order):
    mask_copy = pltpu.make_async_copy(mask_ref, masks_ref, sems.at[len(order)])
    mask_copy.start()
    copies = [pltpu.make_async_copy(image_ref.at[row], rows_ref.at[at], sems.at[at]) for at, row in enumerate(order)]
    for copy in copies:
        copy.start()
    mask_copy.wait()
    return copies


EDGE = tuple(range(AFTER)) + tuple(range(ROWS - BEFORE, ROWS))


def edge_kernel(image_ref, mask_ref, top_ref, low_ref, rows_ref, masks_ref, turned_ref, in_sems, out_sems):
    fetches = fetched(image_ref, mask_ref, rows_ref, masks_ref, in_sems, EDGE)
    stores = []
    for at, row in enumerate(EDGE):
        fetches[at].wait()

        def put(g, k, value):
            turned_ref[at, g, k] = value

        turned([rows_ref.at[at, 0], rows_ref.at[at, 1]], masks_ref[row : row + 1, :], SKEW[row], masks_ref.shape[1], put)
        target = top_ref.at[row] if row < AFTER else low_ref.at[row - (ROWS - BEFORE)]
        store = pltpu.make_async_copy(turned_ref.at[at], target, out_sems.at[at])
        store.start()
        stores.append(store)
    for store in stores:
        store.wait()


def rows_shape(rows, groups, count):
    return jax.ShapeDtypeStruct((rows, groups, 2, count, LANES), jnp.bfloat16)


def edge_rows(images, valid_mask, groups):
    count = images.shape[2]
    far = pl.BlockSpec(memory_space=pl.ANY)
    return pl.pallas_call(
        edge_kernel,
        in_specs=[far, far],
        out_specs=[far] * 2,
        out_shape=[
            rows_shape(AFTER, groups, count),
            rows_shape(BEFORE, groups, count),
        ],
        scratch_shapes=[
            pltpu.VMEM((len(EDGE),) + images.shape[1:], jnp.bfloat16),
            pltpu.VMEM(valid_mask.shape, jnp.int32),
            pltpu.VMEM((len(EDGE), groups, 2, count, LANES), jnp.bfloat16),
            pltpu.SemaphoreType.DMA((len(EDGE) + 1,)),
            pltpu.SemaphoreType.DMA((len(EDGE),)),
        ],
        compiler_params=pltpu.CompilerParams(vmem_limit_bytes=61 * 2**20),
        cost_estimate=pl.CostEstimate(flops=10**6, bytes_accessed=4 * 10**6, transcendentals=0),
        name="edge_rows",
    )(images, valid_mask)


def middle_kernel(cut, image_ref, mask_ref, low_ref, mid_ref, gram_ref, again_ref, first_ref, second_ref, *scratch):
    rows_ref, masks_ref, turned_ref, z_ref, in_sems, out_sems = scratch
    groups = mid_ref.shape[1]
    count, columns = image_ref.shape[2:]
    order = tuple(range(AFTER, ROWS - BEFORE)) + EDGE
    fetches = fetched(image_ref, mask_ref, rows_ref, masks_ref, in_sems, order)
    stores = []
    for target, start, stop in ((first_ref, 0, cut), (second_ref, cut, groups), (again_ref, 0, groups)):
        sem = out_sems.at[ROWS - AFTER - BEFORE + len(stores)]
        stores.append(pltpu.make_async_copy(low_ref.at[:, start:stop], target, sem))
        stores[-1].start()
    z_ref[...] = jnp.zeros_like(z_ref)
    zero = jnp.zeros((count, columns), jnp.bfloat16)
    total = None
    wide = groups * LANES
    for at, row in enumerate(order):
        fetches[at].wait()
        mask = masks_ref[row : row + 1, :]
        if AFTER <= row < ROWS - BEFORE:

            def put(g, k, value):
                turned_ref[at, g, k] = value
                z_ref[pl.ds(k * LANES, count), pl.ds(at * wide + g * LANES, LANES)] = value

            turned([rows_ref.at[at, 0], rows_ref.at[at, 1]], mask, SKEW[row], columns, put)
            store = pltpu.make_async_copy(turned_ref.at[at], mid_ref.at[row - AFTER], out_sems.at[at])
            store.start()
            stores.append(store)
        else:
            keep = jnp.broadcast_to((mask != 0).astype(jnp.float32), (count, columns)).astype(jnp.bfloat16) != 0
            for k in range(2):
                z_ref[pl.ds(k * LANES, count), pl.ds(at * wide, columns)] = jnp.where(keep, rows_ref[at, k], zero)
        if at % 2:
            z = z_ref[:, pl.ds((at - 1) * wide, 2 * wide)]
            part = lax.dot_general(z, z, NT, preferred_element_type=jnp.float32)
            total = part if total is None else total + part
    real = total[:LANES, :LANES] + total[LANES:, LANES:]
    imag = total[LANES:, :LANES] - total[:LANES, LANES:]
    i = lax.broadcasted_iota(jnp.int32, real.shape, 0)
    j = lax.broadcasted_iota(jnp.int32, real.shape, 1)
    gram_ref[...] = jnp.where(i <= j, real, imag)
    for store in stores:
        store.wait()


def middle_rows(images, valid_mask, low, cut):
    count = images.shape[2]
    groups = low.shape[1]
    rows = ROWS - AFTER - BEFORE
    far = pl.BlockSpec(memory_space=pl.ANY)
    return pl.pallas_call(
        functools.partial(middle_kernel, cut),
        in_specs=[far, far, far],
        out_specs=[far, pl.BlockSpec(memory_space=pltpu.VMEM), far, far, far],
        out_shape=[
            rows_shape(rows, groups, count),
            jax.ShapeDtypeStruct((LANES, LANES), jnp.float32),
            jax.ShapeDtypeStruct(low.shape, low.dtype),
            rows_shape(BEFORE, cut, count),
            rows_shape(BEFORE, groups - cut, count),
        ],
        scratch_shapes=[
            pltpu.VMEM(images.shape, jnp.bfloat16),
            pltpu.VMEM(valid_mask.shape, jnp.int32),
            pltpu.VMEM((rows, groups, 2, count, LANES), jnp.bfloat16),
            pltpu.VMEM((2 * LANES, ROWS * groups * LANES), jnp.bfloat16),
            pltpu.SemaphoreType.DMA((ROWS + 1,)),
            pltpu.SemaphoreType.DMA((rows + 3,)),
        ],
        compiler_params=pltpu.CompilerParams(vmem_limit_bytes=49 * 2**20),
        cost_estimate=pl.CostEstimate(flops=10**9, bytes_accessed=5 * 10**6, transcendentals=0),
        name="middle_rows",
    )(images, valid_mask, low)


def added(terms):
    if len(terms) == 4:
        return (terms[0] + terms[2]) + (terms[1] + terms[3])
    return functools.reduce(jnp.add, terms)


def slab_values(terms):
    packed = added(terms)
    flipped = packed.T
    i = lax.broadcasted_iota(jnp.int32, packed.shape, 0)
    j = lax.broadcasted_iota(jnp.int32, packed.shape, 1)
    real = jnp.where(i <= j, packed, flipped)
    imag = jnp.where(i > j, packed, jnp.where(i < j, -flipped, 0.0))
    powers = jnp.where(i == j, packed, 0.0)
    scaled = jnp.sqrt(jnp.sum(powers, axis=1, keepdims=True) * jnp.sum(powers, axis=0, keepdims=True))
    return real / scaled, imag / scaled


INNER = (1, 2, 3, 4, 5)
HALVES = (
    ((-3, -2, -1, 0), (((1, 2, 3), None), (None, (-1, 0)))),
    ((6, 7, 8, 9), ((None, (6, 7)), ((3, 4, 5), None))),
)


def looks_kernel(half, aliased, terms, slab, *refs):
    other_ref, top_ref, mid_ref, low_ref = refs[:4]
    refs = refs[4 + aliased :]
    term_refs, refs = refs[:terms], refs[terms:]
    out_ref, extra_ref, w_ref = refs
    count = top_ref.shape[3]

    @pl.when(pl.program_id(0) == 0)
    def _():
        w_ref[...] = jnp.zeros_like(w_ref)
        if slab:
            real, imag = slab_values([t[...] for t in term_refs])
            extra_ref[0] = real[:count, :count]
            extra_ref[1] = imag[:count, :count]
        elif terms:
            extra_ref[...] = added([t[...] for t in term_refs])
        else:
            extra_ref[...] = jnp.zeros_like(extra_ref)

    rows = {}
    for r in range(ROWS):
        if r < AFTER:
            rows[r] = top_ref.at[r, 0]
        elif r >= ROWS - BEFORE:
            rows[r] = low_ref.at[r - (ROWS - BEFORE), 0]
        else:
            rows[r] = mid_ref.at[r - AFTER, 0]
    for r in range(other_ref.shape[0]):
        rows[ROWS + r if half else r - BEFORE] = other_ref.at[r, 0]

    lane = lax.broadcasted_iota(jnp.int32, (1, LANES), 1)

    def lanes_of(turn):
        place = lane + (-LOOK * turn) % LANES
        place = jnp.where(place >= LANES, place - LANES, place)
        return place < LOOK

    def widened(which):
        return jnp.broadcast_to(which.astype(jnp.float32), (count, LANES)).astype(jnp.bfloat16) != 0

    single = [lanes_of(t) for t in range(2 * PER - 1)]
    wide = [widened(s) for s in single]

    def turn(l, r):
        return l + SKEW[r % ROWS]

    def gathered(l, k, which):
        out = rows[which[0]][k]
        for r in which[1:]:
            out = jnp.where(wide[turn(l, r)], rows[r][k], out)
        return out

    def kept(l, which):
        select = single[turn(l, which[0])]
        for r in which[1:]:
            select = select | single[turn(l, r)]
        return select.astype(jnp.float32)

    eight = (8, LANES)
    along = lax.broadcasted_iota(jnp.int32, eight, 1)
    on_eye = along % 8 == lax.broadcasted_iota(jnp.int32, eight, 0)
    block = along // 8

    def normalised(real, imag, w, l):
        picked = real[:8]
        for v in range(1, count // 8):
            picked = jnp.where(block == v, real[8 * v : 8 * v + 8], picked)
        power = jnp.sum(jnp.where(on_eye, picked, 0.0), axis=0, keepdims=True)
        across = lax.rsqrt(jnp.maximum(power, floor_power))
        diagonal = jnp.where(on_eye, across, 0.0)
        spread = jnp.concatenate([jnp.where(block == v, diagonal, 0.0) for v in range(count // 8)], axis=0)
        scale = jnp.sum(spread, axis=1, keepdims=True) * across
        out_ref[w, l, 0] = (real * scale).astype(jnp.bfloat16)[:, :count]
        out_ref[w, l, 1] = (imag * scale).astype(jnp.bfloat16)[:, :count]

    outer_rows, windows = HALVES[half]
    for l in range(PER):
        slot = l % 2
        for k in range(2):
            w_ref[slot, k, pl.ds(0, count), pl.ds(0, LANES)] = gathered(l, k, INNER)
            w_ref[slot, k, pl.ds(0, count), pl.ds(LANES, LANES)] = gathered(l, k, outer_rows)
        every = w_ref[slot].reshape(2 * LANES, 2 * LANES)
        nothing = jnp.zeros_like(every)
        reads = []
        for inner_rows, rest_rows in windows:
            lanes = jnp.concatenate([kept(l, inner_rows or INNER), kept(l, rest_rows or outer_rows)], axis=1)
            lanes = jnp.broadcast_to(lanes, every.shape).astype(jnp.bfloat16) != 0
            read = jnp.where(lanes, every, nothing)
            for start in range(0, LANES, TILE):
                reads.append(read[start : start + TILE])
                reads.append(read[LANES + start : LANES + start + TILE])
        gram = lax.dot_general(jnp.concatenate(reads, axis=0), every, NT, preferred_element_type=jnp.float32)
        for w in range(2):
            real, imag = [], []
            for start in range(0, LANES, TILE):
                base = 2 * (w * LANES + start)
                re, im = gram[base : base + TILE], gram[base + TILE : base + 2 * TILE]
                real.append(re[:, :LANES] + im[:, LANES:])
                imag.append(im[:, :LANES] - re[:, LANES:])
            normalised(jnp.concatenate(real, axis=0)[:count], jnp.concatenate(imag, axis=0)[:count], w, l)


def looked(half, other, top, mid, low, first, groups, looks, previous, terms, slab):
    count = other.shape[3]

    def spec(array):
        offset = 0 if array is other else first
        return pl.BlockSpec((array.shape[0], 1) + array.shape[2:], lambda s: (0, s + offset, 0, 0, 0))

    operands = [other, top, mid, low]
    in_specs = [spec(a) for a in operands]
    aliases = {}
    if previous is not None:
        aliases = {len(operands): 0}
        operands.append(previous)
        in_specs.append(pl.BlockSpec(memory_space=pl.ANY))
    for term in terms:
        operands.append(term)
        in_specs.append(pl.BlockSpec(term.shape, lambda s: (0, 0)))
    extra = (2, count, count) if slab else (LANES, LANES)
    out_specs = [
        pl.BlockSpec((2, PER, 2, count, count), lambda s: (half, s + first, 0, 0, 0)),
        pl.BlockSpec(extra, lambda s: (0,) * len(extra)),
    ]
    out_shape = [
        jax.ShapeDtypeStruct((ROWS // 2, looks, 2, count, count), jnp.bfloat16),
        jax.ShapeDtypeStruct(extra, jnp.float32),
    ]
    return pl.pallas_call(
        functools.partial(looks_kernel, half, previous is not None, len(terms), slab),
        grid=(groups,),
        in_specs=in_specs,
        out_specs=out_specs,
        out_shape=out_shape,
        input_output_aliases=aliases,
        scratch_shapes=[
            pltpu.VMEM((2, 2, LANES, 2 * LANES), jnp.bfloat16),
        ],
        compiler_params=pltpu.CompilerParams(vmem_limit_bytes=48 * 2**20),
        cost_estimate=pl.CostEstimate(
            flops=2 * groups * PER * 2 * 512 * 256 * 256, bytes_accessed=groups * 10**6, transcendentals=0
        ),
        name="looks",
    )(*operands)


def rounds(size):
    found = []
    stride = 1
    while stride < size:
        radix = 4 if size // stride % 4 == 0 else 2
        if size // stride % radix:
            return None
        found.append((stride, radix))
        stride *= radix
    return found[::-1]


def round_terms(value, axis, stride, radix):
    size = lax.axis_size(axis)
    terms = [value]
    for shift in range(1, radix):
        pairs = []
        for i in range(size):
            place = (i // stride) % radix
            pairs.append((i, i + ((place + shift) % radix - place) * stride))
        terms.append(lax.ppermute(value, axis, pairs))
    return terms


def shards(images, valid_mask):
    looks = images.shape[3] // LOOK
    groups = -(-looks // PER)
    cut = -(-groups // 2)
    size = lax.axis_size("pix")
    forward = [(i, i + 1) for i in range(size - 1)]
    backward = [(i + 1, i) for i in range(size - 1)]
    top, low = edge_rows(images, valid_mask, groups)
    after = lax.ppermute(top, "pix", backward)
    mid, total, low, low0, low1 = middle_rows(images, valid_mask, low, cut)
    before0 = lax.ppermute(low0, "pix", forward)
    before1 = lax.ppermute(low1, "pix", forward)
    steps = rounds(size)
    if steps is None:
        terms, steps = [lax.psum(total, "pix")], []
    else:
        terms = round_terms(total, "pix", *steps[0]) if steps else [total]
    out, _ = looked(1, after, top, mid, low, 0, groups, looks, None, [], False)
    out, zeros = looked(0, before0, top, mid, low, 0, cut, looks, out, [], False)
    for step in steps[1:]:
        terms = round_terms(added(terms) + zeros, "pix", *step)
    out, slab = looked(0, before1, top, mid, low, cut, groups - cut, looks, out, terms, True)
    return (out, slab)


def solution(mesh):
    in_specs = (P(("group", "pix"), None, None, None), P(("group", "pix"), None))
    out_specs = (P(("group", "pix"), None, None, None, None), P("group", None, None))
    return jax.shard_map(shards, mesh=mesh, in_specs=in_specs, out_specs=out_specs, check_vma=False)
```

```python
import functools
import jax
import jax.numpy as jnp
from jax import lax
from jax.experimental import pallas as pl
from jax.experimental.pallas import tpu as pltpu
from jax.sharding import PartitionSpec as P

floor_power = 30.0

LOOK = 21
LANES = 128
TILE = 16
PER = LANES // LOOK
SPAN = PER * LOOK
ROWS = 8
SKEW = (5, 0, 1, 2, 3, 4, 1, 2)
BEFORE, AFTER = 3, 2
NT = (((1,), (1,)), ((), ()))


def turned(image, mask, skew, columns, put):
    count = image[0].shape[0]
    zero = jnp.zeros((count, LANES), jnp.bfloat16)
    lane = lax.broadcasted_iota(jnp.int32, (1, LANES), 1)

    def tile(value, g):
        start, stop = g * LANES, min((g + 1) * LANES, columns)
        part = value[:, start:stop]
        if stop - start < LANES:
            rest = jnp.zeros((part.shape[0], LANES - (stop - start)), part.dtype)
            part = jnp.concatenate([part, rest], axis=1)
        return part

    def widened(which):
        return jnp.broadcast_to(which.astype(jnp.float32), (count, LANES)).astype(jnp.bfloat16) != 0

    tiles = -(-columns // LANES)
    for g in range(-(-columns // SPAN)):
        slide = (LANES - SPAN) * g
        place = (lane + slide) % LANES
        used = (place < SPAN) & (SPAN * g + place < columns)
        prior = lane >= LANES - slide
        sides = [t for t in (g - 1, g) if 0 <= t < tiles]

        def joined(value):
            parts = [tile(value, t) for t in sides]
            if len(parts) == 1:
                return parts[0]
            which = prior if value.shape[0] == 1 else widened(prior)
            return jnp.where(which, parts[0], parts[1])

        keep = widened(used & (joined(mask) != 0))
        for k in range(2):
            row = jnp.where(keep, joined(image[k]), zero)
            put(g, k, pltpu.roll(row, slide + LOOK * skew, 1))


def fetched(image_ref, mask_ref, rows_ref, masks_ref, sems, order):
    mask_copy = pltpu.make_async_copy(mask_ref, masks_ref, sems.at[len(order)])
    mask_copy.start()
    copies = [pltpu.make_async_copy(image_ref.at[row], rows_ref.at[at], sems.at[at]) for at, row in enumerate(order)]
    for copy in copies:
        copy.start()
    mask_copy.wait()
    return copies


EDGE = tuple(range(AFTER)) + tuple(range(ROWS - BEFORE, ROWS))


def edge_kernel(image_ref, mask_ref, top_ref, low_ref, rows_ref, masks_ref, turned_ref, in_sems, out_sems):
    fetches = fetched(image_ref, mask_ref, rows_ref, masks_ref, in_sems, EDGE)
    stores = []
    for at, row in enumerate(EDGE):
        fetches[at].wait()

        def put(g, k, value):
            turned_ref[at, g, k] = value

        turned([rows_ref.at[at, 0], rows_ref.at[at, 1]], masks_ref[row : row + 1, :], SKEW[row], masks_ref.shape[1], put)
        target = top_ref.at[row] if row < AFTER else low_ref.at[row - (ROWS - BEFORE)]
        store = pltpu.make_async_copy(turned_ref.at[at], target, out_sems.at[at])
        store.start()
        stores.append(store)
    for store in stores:
        store.wait()


def rows_shape(rows, groups, count):
    return jax.ShapeDtypeStruct((rows, groups, 2, count, LANES), jnp.bfloat16)


def edge_rows(images, valid_mask, groups):
    count = images.shape[2]
    far = pl.BlockSpec(memory_space=pl.ANY)
    return pl.pallas_call(
        edge_kernel,
        in_specs=[far, far],
        out_specs=[far] * 2,
        out_shape=[
            rows_shape(AFTER, groups, count),
            rows_shape(BEFORE, groups, count),
        ],
        scratch_shapes=[
            pltpu.VMEM((len(EDGE),) + images.shape[1:], jnp.bfloat16),
            pltpu.VMEM(valid_mask.shape, jnp.int32),
            pltpu.VMEM((len(EDGE), groups, 2, count, LANES), jnp.bfloat16),
            pltpu.SemaphoreType.DMA((len(EDGE) + 1,)),
            pltpu.SemaphoreType.DMA((len(EDGE),)),
        ],
        compiler_params=pltpu.CompilerParams(vmem_limit_bytes=61 * 2**20),
        cost_estimate=pl.CostEstimate(flops=10**6, bytes_accessed=4 * 10**6, transcendentals=0),
        name="edge_rows",
    )(images, valid_mask)


def middle_kernel(cut, image_ref, mask_ref, low_ref, mid_ref, gram_ref, again_ref, first_ref, second_ref, *scratch):
    rows_ref, masks_ref, turned_ref, z_ref, in_sems, out_sems = scratch
    groups = mid_ref.shape[1]
    count, columns = image_ref.shape[2:]
    order = tuple(range(AFTER, ROWS - BEFORE)) + EDGE
    fetches = fetched(image_ref, mask_ref, rows_ref, masks_ref, in_sems, order)
    stores = []
    for target, start, stop in ((first_ref, 0, cut), (second_ref, cut, groups), (again_ref, 0, groups)):
        sem = out_sems.at[ROWS - AFTER - BEFORE + len(stores)]
        stores.append(pltpu.make_async_copy(low_ref.at[:, start:stop], target, sem))
        stores[-1].start()
    z_ref[...] = jnp.zeros_like(z_ref)
    zero = jnp.zeros((count, columns), jnp.bfloat16)
    total = None
    wide = groups * LANES
    for at, row in enumerate(order):
        fetches[at].wait()
        mask = masks_ref[row : row + 1, :]
        if AFTER <= row < ROWS - BEFORE:

            def put(g, k, value):
                turned_ref[at, g, k] = value
                z_ref[pl.ds(k * LANES, count), pl.ds(at * wide + g * LANES, LANES)] = value

            turned([rows_ref.at[at, 0], rows_ref.at[at, 1]], mask, SKEW[row], columns, put)
            store = pltpu.make_async_copy(turned_ref.at[at], mid_ref.at[row - AFTER], out_sems.at[at])
            store.start()
            stores.append(store)
        else:
            keep = jnp.broadcast_to((mask != 0).astype(jnp.float32), (count, columns)).astype(jnp.bfloat16) != 0
            for k in range(2):
                z_ref[pl.ds(k * LANES, count), pl.ds(at * wide, columns)] = jnp.where(keep, rows_ref[at, k], zero)
        if at % 2:
            z = z_ref[:, pl.ds((at - 1) * wide, 2 * wide)]
            part = lax.dot_general(z, z, NT, preferred_element_type=jnp.float32)
            total = part if total is None else total + part
    real = total[:LANES, :LANES] + total[LANES:, LANES:]
    imag = total[LANES:, :LANES] - total[:LANES, LANES:]
    i = lax.broadcasted_iota(jnp.int32, real.shape, 0)
    j = lax.broadcasted_iota(jnp.int32, real.shape, 1)
    gram_ref[...] = jnp.where(i <= j, real, imag)
    for store in stores:
        store.wait()


def middle_rows(images, valid_mask, low, cut):
    count = images.shape[2]
    groups = low.shape[1]
    rows = ROWS - AFTER - BEFORE
    far = pl.BlockSpec(memory_space=pl.ANY)
    return pl.pallas_call(
        functools.partial(middle_kernel, cut),
        in_specs=[far, far, far],
        out_specs=[far, pl.BlockSpec(memory_space=pltpu.VMEM), far, far, far],
        out_shape=[
            rows_shape(rows, groups, count),
            jax.ShapeDtypeStruct((LANES, LANES), jnp.float32),
            jax.ShapeDtypeStruct(low.shape, low.dtype),
            rows_shape(BEFORE, cut, count),
            rows_shape(BEFORE, groups - cut, count),
        ],
        scratch_shapes=[
            pltpu.VMEM(images.shape, jnp.bfloat16),
            pltpu.VMEM(valid_mask.shape, jnp.int32),
            pltpu.VMEM((rows, groups, 2, count, LANES), jnp.bfloat16),
            pltpu.VMEM((2 * LANES, ROWS * groups * LANES), jnp.bfloat16),
            pltpu.SemaphoreType.DMA((ROWS + 1,)),
            pltpu.SemaphoreType.DMA((rows + 3,)),
        ],
        compiler_params=pltpu.CompilerParams(vmem_limit_bytes=49 * 2**20),
        cost_estimate=pl.CostEstimate(flops=10**9, bytes_accessed=5 * 10**6, transcendentals=0),
        name="middle_rows",
    )(images, valid_mask, low)


def added(terms):
    if len(terms) == 4:
        return (terms[0] + terms[2]) + (terms[1] + terms[3])
    return functools.reduce(jnp.add, terms)


def slab_values(terms):
    packed = added(terms)
    flipped = packed.T
    i = lax.broadcasted_iota(jnp.int32, packed.shape, 0)
    j = lax.broadcasted_iota(jnp.int32, packed.shape, 1)
    real = jnp.where(i <= j, packed, flipped)
    imag = jnp.where(i > j, packed, jnp.where(i < j, -flipped, 0.0))
    powers = jnp.where(i == j, packed, 0.0)
    scaled = jnp.sqrt(jnp.sum(powers, axis=1, keepdims=True) * jnp.sum(powers, axis=0, keepdims=True))
    return real / scaled, imag / scaled


INNER = (1, 2, 3, 4, 5)
HALVES = (
    ((-3, -2, -1, 0), (((1, 2, 3), None), (None, (-1, 0)))),
    ((6, 7, 8, 9), ((None, (6, 7)), ((3, 4, 5), None))),
)


def looks_kernel(half, aliased, terms, slab, *refs):
    other_ref, top_ref, mid_ref, low_ref = refs[:4]
    refs = refs[4 + aliased :]
    term_refs, refs = refs[:terms], refs[terms:]
    out_ref, extra_ref, w_ref = refs
    count = top_ref.shape[3]

    @pl.when(pl.program_id(0) == 0)
    def _():
        w_ref[...] = jnp.zeros_like(w_ref)
        if slab:
            real, imag = slab_values([t[...] for t in term_refs])
            extra_ref[0] = real[:count, :count]
            extra_ref[1] = imag[:count, :count]
        elif terms:
            extra_ref[...] = added([t[...] for t in term_refs])
        else:
            extra_ref[...] = jnp.zeros_like(extra_ref)

    rows = {}
    for r in range(ROWS):
        if r < AFTER:
            rows[r] = top_ref.at[r, 0]
        elif r >= ROWS - BEFORE:
            rows[r] = low_ref.at[r - (ROWS - BEFORE), 0]
        else:
            rows[r] = mid_ref.at[r - AFTER, 0]
    for r in range(other_ref.shape[0]):
        rows[ROWS + r if half else r - BEFORE] = other_ref.at[r, 0]

    lane = lax.broadcasted_iota(jnp.int32, (1, LANES), 1)

    def lanes_of(turn):
        place = lane + (-LOOK * turn) % LANES
        place = jnp.where(place >= LANES, place - LANES, place)
        return place < LOOK

    def widened(which):
        return jnp.broadcast_to(which.astype(jnp.float32), (count, LANES)).astype(jnp.bfloat16) != 0

    single = [lanes_of(t) for t in range(2 * PER - 1)]
    wide = [widened(s) for s in single]

    def turn(l, r):
        return l + SKEW[r % ROWS]

    def gathered(l, k, which):
        out = rows[which[0]][k]
        for r in which[1:]:
            out = jnp.where(wide[turn(l, r)], rows[r][k], out)
        return out

    def kept(l, which):
        select = single[turn(l, which[0])]
        for r in which[1:]:
            select = select | single[turn(l, r)]
        return select.astype(jnp.float32)

    eight = (8, LANES)
    along = lax.broadcasted_iota(jnp.int32, eight, 1)
    on_eye = along % 8 == lax.broadcasted_iota(jnp.int32, eight, 0)
    block = along // 8

    def normalised(real, imag, w, l):
        picked = real[:8]
        for v in range(1, count // 8):
            picked = jnp.where(block == v, real[8 * v : 8 * v + 8], picked)
        power = jnp.sum(jnp.where(on_eye, picked, 0.0), axis=0, keepdims=True)
        across = lax.rsqrt(jnp.maximum(power, floor_power))
        diagonal = jnp.where(on_eye, across, 0.0)
        spread = jnp.concatenate([jnp.where(block == v, diagonal, 0.0) for v in range(count // 8)], axis=0)
        scale = jnp.sum(spread, axis=1, keepdims=True) * across
        out_ref[w, l, 0] = (real * scale).astype(jnp.bfloat16)[:, :count]
        out_ref[w, l, 1] = (imag * scale).astype(jnp.bfloat16)[:, :count]

    outer_rows, windows = HALVES[half]
    for l in range(PER):
        slot = l % 2
        for k in range(2):
            w_ref[slot, k, pl.ds(0, count), pl.ds(0, LANES)] = gathered(l, k, INNER)
            w_ref[slot, k, pl.ds(0, count), pl.ds(LANES, LANES)] = gathered(l, k, outer_rows)
        every = w_ref[slot].reshape(2 * LANES, 2 * LANES)
        nothing = jnp.zeros_like(every)
        reads = []
        for inner_rows, rest_rows in windows:
            lanes = jnp.concatenate([kept(l, inner_rows or INNER), kept(l, rest_rows or outer_rows)], axis=1)
            lanes = jnp.broadcast_to(lanes, every.shape).astype(jnp.bfloat16) != 0
            read = jnp.where(lanes, every, nothing)
            for start in range(0, LANES, TILE):
                reads.append(read[start : start + TILE])
                reads.append(read[LANES + start : LANES + start + TILE])
        gram = lax.dot_general(jnp.concatenate(reads, axis=0), every, NT, preferred_element_type=jnp.float32)
        for w in range(2):
            real, imag = [], []
            for start in range(0, LANES, TILE):
                base = 2 * (w * LANES + start)
                re, im = gram[base : base + TILE], gram[base + TILE : base + 2 * TILE]
                real.append(re[:, :LANES] + im[:, LANES:])
                imag.append(im[:, :LANES] - re[:, LANES:])
            normalised(jnp.concatenate(real, axis=0)[:count], jnp.concatenate(imag, axis=0)[:count], w, l)


def looked(half, other, top, mid, low, first, groups, looks, previous, terms, slab):
    count = other.shape[3]

    def spec(array):
        offset = 0 if array is other else first
        return pl.BlockSpec((array.shape[0], 1) + array.shape[2:], lambda s: (0, s + offset, 0, 0, 0))

    operands = [other, top, mid, low]
    in_specs = [spec(a) for a in operands]
    aliases = {}
    if previous is not None:
        aliases = {len(operands): 0}
        operands.append(previous)
        in_specs.append(pl.BlockSpec(memory_space=pl.ANY))
    for term in terms:
        operands.append(term)
        in_specs.append(pl.BlockSpec(term.shape, lambda s: (0, 0)))
    extra = (2, count, count) if slab else (LANES, LANES)
    out_specs = [
        pl.BlockSpec((2, PER, 2, count, count), lambda s: (half, s + first, 0, 0, 0)),
        pl.BlockSpec(extra, lambda s: (0,) * len(extra)),
    ]
    out_shape = [
        jax.ShapeDtypeStruct((ROWS // 2, looks, 2, count, count), jnp.bfloat16),
        jax.ShapeDtypeStruct(extra, jnp.float32),
    ]
    return pl.pallas_call(
        functools.partial(looks_kernel, half, previous is not None, len(terms), slab),
        grid=(groups,),
        in_specs=in_specs,
        out_specs=out_specs,
        out_shape=out_shape,
        input_output_aliases=aliases,
        scratch_shapes=[
            pltpu.VMEM((2, 2, LANES, 2 * LANES), jnp.bfloat16),
        ],
        compiler_params=pltpu.CompilerParams(vmem_limit_bytes=48 * 2**20),
        cost_estimate=pl.CostEstimate(
            flops=groups * PER * 2 * 512 * 256 * 256, bytes_accessed=groups * 10**6, transcendentals=0
        ),
        name="looks",
    )(*operands)


def rounds(size):
    found = []
    stride = 1
    while stride < size:
        radix = 4 if size // stride % 4 == 0 else 2
        if size // stride % radix:
            return None
        found.append((stride, radix))
        stride *= radix
    return found[::-1]


def round_terms(value, axis, stride, radix):
    size = lax.axis_size(axis)
    terms = [value]
    for shift in range(1, radix):
        pairs = []
        for i in range(size):
            place = (i // stride) % radix
            pairs.append((i, i + ((place + shift) % radix - place) * stride))
        terms.append(lax.ppermute(value, axis, pairs))
    return terms


def shards(images, valid_mask):
    looks = images.shape[3] // LOOK
    groups = -(-looks // PER)
    cut = -(-groups // 2)
    size = lax.axis_size("pix")
    forward = [(i, i + 1) for i in range(size - 1)]
    backward = [(i + 1, i) for i in range(size - 1)]
    top, low = edge_rows(images, valid_mask, groups)
    after = lax.ppermute(top, "pix", backward)
    mid, total, low, low0, low1 = middle_rows(images, valid_mask, low, cut)
    before0 = lax.ppermute(low0, "pix", forward)
    before1 = lax.ppermute(low1, "pix", forward)
    steps = rounds(size)
    if steps is None:
        terms, steps = [lax.psum(total, "pix")], []
    else:
        terms = round_terms(total, "pix", *steps[0]) if steps else [total]
    out, zeros = looked(1, after, top, mid, low, 0, groups, looks, None, [], False)
    for step in steps[1:]:
        terms = round_terms(added(terms) + zeros, "pix", *step)
    out, _ = looked(0, before0, top, mid, low, 0, cut, looks, out, [], False)
    out, slab = looked(0, before1, top, mid, low, cut, groups - cut, looks, out, terms, True)
    return (out, slab)


def solution(mesh):
    in_specs = (P(("group", "pix"), None, None, None), P(("group", "pix"), None))
    out_specs = (P(("group", "pix"), None, None, None, None), P("group", None, None))
    return jax.shard_map(shards, mesh=mesh, in_specs=in_specs, out_specs=out_specs, check_vma=False)
```

```python
import functools
import jax
import jax.numpy as jnp
from jax import lax
from jax.experimental import pallas as pl
from jax.experimental.pallas import tpu as pltpu
from jax.sharding import PartitionSpec as P

floor_power = 30.0

LOOK = 21
LANES = 128
TILE = 16
PER = LANES // LOOK
SPAN = PER * LOOK
ROWS = 8
SKEW = (5, 0, 1, 2, 3, 4, 1, 2)
BEFORE, AFTER = 3, 2
NT = (((1,), (1,)), ((), ()))


def turned(image, mask, skew, columns, put):
    count = image[0].shape[0]
    zero = jnp.zeros((count, LANES), jnp.bfloat16)
    lane = lax.broadcasted_iota(jnp.int32, (1, LANES), 1)

    def tile(value, g):
        start, stop = g * LANES, min((g + 1) * LANES, columns)
        part = value[:, start:stop]
        if stop - start < LANES:
            rest = jnp.zeros((part.shape[0], LANES - (stop - start)), part.dtype)
            part = jnp.concatenate([part, rest], axis=1)
        return part

    def widened(which):
        return jnp.broadcast_to(which.astype(jnp.float32), (count, LANES)).astype(jnp.bfloat16) != 0

    tiles = -(-columns // LANES)
    for g in range(-(-columns // SPAN)):
        slide = (LANES - SPAN) * g
        place = (lane + slide) % LANES
        used = (place < SPAN) & (SPAN * g + place < columns)
        prior = lane >= LANES - slide
        sides = [t for t in (g - 1, g) if 0 <= t < tiles]

        def joined(value):
            parts = [tile(value, t) for t in sides]
            if len(parts) == 1:
                return parts[0]
            which = prior if value.shape[0] == 1 else widened(prior)
            return jnp.where(which, parts[0], parts[1])

        keep = widened(used & (joined(mask) != 0))
        for k in range(2):
            row = jnp.where(keep, joined(image[k]), zero)
            put(g, k, pltpu.roll(row, slide + LOOK * skew, 1))


def fetched(image_ref, mask_ref, rows_ref, masks_ref, sems, order):
    mask_copy = pltpu.make_async_copy(mask_ref, masks_ref, sems.at[len(order)])
    mask_copy.start()
    copies = [pltpu.make_async_copy(image_ref.at[row], rows_ref.at[at], sems.at[at]) for at, row in enumerate(order)]
    for copy in copies:
        copy.start()
    mask_copy.wait()
    return copies


EDGE = tuple(range(AFTER)) + tuple(range(ROWS - BEFORE, ROWS))


def edge_kernel(image_ref, mask_ref, top_ref, low_ref, rows_ref, masks_ref, turned_ref, in_sems, out_sems):
    fetches = fetched(image_ref, mask_ref, rows_ref, masks_ref, in_sems, EDGE)
    stores = []
    for at, row in enumerate(EDGE):
        fetches[at].wait()

        def put(g, k, value):
            turned_ref[at, g, k] = value

        turned([rows_ref.at[at, 0], rows_ref.at[at, 1]], masks_ref[row : row + 1, :], SKEW[row], masks_ref.shape[1], put)
        target = top_ref.at[row] if row < AFTER else low_ref.at[row - (ROWS - BEFORE)]
        store = pltpu.make_async_copy(turned_ref.at[at], target, out_sems.at[at])
        store.start()
        stores.append(store)
    for store in stores:
        store.wait()


def rows_shape(rows, groups, count):
    return jax.ShapeDtypeStruct((rows, groups, 2, count, LANES), jnp.bfloat16)


def edge_rows(images, valid_mask, groups):
    count = images.shape[2]
    far = pl.BlockSpec(memory_space=pl.ANY)
    return pl.pallas_call(
        edge_kernel,
        in_specs=[far, far],
        out_specs=[far] * 2,
        out_shape=[
            rows_shape(AFTER, groups, count),
            rows_shape(BEFORE, groups, count),
        ],
        scratch_shapes=[
            pltpu.VMEM((len(EDGE),) + images.shape[1:], jnp.bfloat16),
            pltpu.VMEM(valid_mask.shape, jnp.int32),
            pltpu.VMEM((len(EDGE), groups, 2, count, LANES), jnp.bfloat16),
            pltpu.SemaphoreType.DMA((len(EDGE) + 1,)),
            pltpu.SemaphoreType.DMA((len(EDGE),)),
        ],
        compiler_params=pltpu.CompilerParams(vmem_limit_bytes=61 * 2**20),
        cost_estimate=pl.CostEstimate(flops=10**6, bytes_accessed=4 * 10**6, transcendentals=0),
        name="edge_rows",
    )(images, valid_mask)


def middle_kernel(cut, image_ref, mask_ref, low_ref, mid_ref, gram_ref, again_ref, first_ref, second_ref, *scratch):
    rows_ref, masks_ref, turned_ref, z_ref, in_sems, out_sems = scratch
    groups = mid_ref.shape[1]
    count, columns = image_ref.shape[2:]
    order = tuple(range(AFTER, ROWS - BEFORE)) + EDGE
    fetches = fetched(image_ref, mask_ref, rows_ref, masks_ref, in_sems, order)
    stores = []
    for target, start, stop in ((first_ref, 0, cut), (second_ref, cut, groups), (again_ref, 0, groups)):
        sem = out_sems.at[ROWS - AFTER - BEFORE + len(stores)]
        stores.append(pltpu.make_async_copy(low_ref.at[:, start:stop], target, sem))
        stores[-1].start()
    z_ref[...] = jnp.zeros_like(z_ref)
    zero = jnp.zeros((count, columns), jnp.bfloat16)
    total = None
    wide = groups * LANES
    for at, row in enumerate(order):
        fetches[at].wait()
        mask = masks_ref[row : row + 1, :]
        if AFTER <= row < ROWS - BEFORE:

            def put(g, k, value):
                turned_ref[at, g, k] = value
                z_ref[pl.ds(k * LANES, count), pl.ds(at * wide + g * LANES, LANES)] = value

            turned([rows_ref.at[at, 0], rows_ref.at[at, 1]], mask, SKEW[row], columns, put)
            store = pltpu.make_async_copy(turned_ref.at[at], mid_ref.at[row - AFTER], out_sems.at[at])
            store.start()
            stores.append(store)
        else:
            keep = jnp.broadcast_to((mask != 0).astype(jnp.float32), (count, columns)).astype(jnp.bfloat16) != 0
            for k in range(2):
                z_ref[pl.ds(k * LANES, count), pl.ds(at * wide, columns)] = jnp.where(keep, rows_ref[at, k], zero)
        if at % 2:
            z = z_ref[:, pl.ds((at - 1) * wide, 2 * wide)]
            part = lax.dot_general(z, z, NT, preferred_element_type=jnp.float32)
            total = part if total is None else total + part
    real = total[:LANES, :LANES] + total[LANES:, LANES:]
    imag = total[LANES:, :LANES] - total[:LANES, LANES:]
    i = lax.broadcasted_iota(jnp.int32, real.shape, 0)
    j = lax.broadcasted_iota(jnp.int32, real.shape, 1)
    gram_ref[...] = jnp.where(i <= j, real, imag)
    for store in stores:
        store.wait()


def middle_rows(images, valid_mask, low, cut):
    count = images.shape[2]
    groups = low.shape[1]
    rows = ROWS - AFTER - BEFORE
    far = pl.BlockSpec(memory_space=pl.ANY)
    return pl.pallas_call(
        functools.partial(middle_kernel, cut),
        in_specs=[far, far, far],
        out_specs=[far, pl.BlockSpec(memory_space=pltpu.VMEM), far, far, far],
        out_shape=[
            rows_shape(rows, groups, count),
            jax.ShapeDtypeStruct((LANES, LANES), jnp.float32),
            jax.ShapeDtypeStruct(low.shape, low.dtype),
            rows_shape(BEFORE, cut, count),
            rows_shape(BEFORE, groups - cut, count),
        ],
        scratch_shapes=[
            pltpu.VMEM(images.shape, jnp.bfloat16),
            pltpu.VMEM(valid_mask.shape, jnp.int32),
            pltpu.VMEM((rows, groups, 2, count, LANES), jnp.bfloat16),
            pltpu.VMEM((2 * LANES, ROWS * groups * LANES), jnp.bfloat16),
            pltpu.SemaphoreType.DMA((ROWS + 1,)),
            pltpu.SemaphoreType.DMA((rows + 3,)),
        ],
        compiler_params=pltpu.CompilerParams(vmem_limit_bytes=49 * 2**20),
        cost_estimate=pl.CostEstimate(flops=10**9, bytes_accessed=5 * 10**6, transcendentals=0),
        name="middle_rows",
    )(images, valid_mask, low)


def added(terms):
    if len(terms) == 4:
        return (terms[0] + terms[2]) + (terms[1] + terms[3])
    return functools.reduce(jnp.add, terms)


def slab_values(terms):
    packed = added(terms)
    flipped = packed.T
    i = lax.broadcasted_iota(jnp.int32, packed.shape, 0)
    j = lax.broadcasted_iota(jnp.int32, packed.shape, 1)
    real = jnp.where(i <= j, packed, flipped)
    imag = jnp.where(i > j, packed, jnp.where(i < j, -flipped, 0.0))
    powers = jnp.where(i == j, packed, 0.0)
    scaled = jnp.sqrt(jnp.sum(powers, axis=1, keepdims=True) * jnp.sum(powers, axis=0, keepdims=True))
    return real / scaled, imag / scaled


INNER = (1, 2, 3, 4, 5)
HALVES = (
    ((-3, -2, -1, 0), (((1, 2, 3), None), (None, (-1, 0)))),
    ((6, 7, 8, 9), ((None, (6, 7)), ((3, 4, 5), None))),
)


def looks_kernel(half, aliased, terms, slab, *refs):
    other_ref, top_ref, mid_ref, low_ref = refs[:4]
    refs = refs[4 + aliased :]
    term_refs, refs = refs[:terms], refs[terms:]
    out_ref, extra_ref, w_ref = refs
    count = top_ref.shape[3]

    @pl.when(pl.program_id(0) == 0)
    def _():
        w_ref[...] = jnp.zeros_like(w_ref)
        if slab:
            real, imag = slab_values([t[...] for t in term_refs])
            extra_ref[0] = real[:count, :count]
            extra_ref[1] = imag[:count, :count]
        elif terms:
            extra_ref[...] = added([t[...] for t in term_refs])
        else:
            extra_ref[...] = jnp.zeros_like(extra_ref)

    rows = {}
    for r in range(ROWS):
        if r < AFTER:
            rows[r] = top_ref.at[r, 0]
        elif r >= ROWS - BEFORE:
            rows[r] = low_ref.at[r - (ROWS - BEFORE), 0]
        else:
            rows[r] = mid_ref.at[r - AFTER, 0]
    for r in range(other_ref.shape[0]):
        rows[ROWS + r if half else r - BEFORE] = other_ref.at[r, 0]

    lane = lax.broadcasted_iota(jnp.int32, (1, LANES), 1)

    def lanes_of(turn):
        place = lane + (-LOOK * turn) % LANES
        place = jnp.where(place >= LANES, place - LANES, place)
        return place < LOOK

    def widened(which):
        return jnp.broadcast_to(which.astype(jnp.float32), (count, LANES)).astype(jnp.bfloat16) != 0

    single = [lanes_of(t) for t in range(2 * PER - 1)]
    wide = [widened(s) for s in single]

    def turn(l, r):
        return l + SKEW[r % ROWS]

    def gathered(l, k, which):
        out = rows[which[0]][k]
        for r in which[1:]:
            out = jnp.where(wide[turn(l, r)], rows[r][k], out)
        return out

    def kept(l, which):
        select = single[turn(l, which[0])]
        for r in which[1:]:
            select = select | single[turn(l, r)]
        return select.astype(jnp.float32)

    eight = (8, LANES)
    along = lax.broadcasted_iota(jnp.int32, eight, 1)
    on_eye = along % 8 == lax.broadcasted_iota(jnp.int32, eight, 0)
    block = along // 8

    def normalised(real, imag, w, l):
        picked = real[:8]
        for v in range(1, count // 8):
            picked = jnp.where(block == v, real[8 * v : 8 * v + 8], picked)
        power = jnp.sum(jnp.where(on_eye, picked, 0.0), axis=0, keepdims=True)
        across = lax.rsqrt(jnp.maximum(power, floor_power))
        diagonal = jnp.where(on_eye, across, 0.0)
        spread = jnp.concatenate([jnp.where(block == v, diagonal, 0.0) for v in range(count // 8)], axis=0)
        scale = jnp.sum(spread, axis=1, keepdims=True) * across
        out_ref[w, l, 0] = (real * scale).astype(jnp.bfloat16)[:, :count]
        out_ref[w, l, 1] = (imag * scale).astype(jnp.bfloat16)[:, :count]

    outer_rows, windows = HALVES[half]
    for l in range(PER):
        slot = l % 2
        for k in range(2):
            w_ref[slot, k, pl.ds(0, count), pl.ds(0, LANES)] = gathered(l, k, INNER)
            w_ref[slot, k, pl.ds(0, count), pl.ds(LANES, LANES)] = gathered(l, k, outer_rows)
        every = w_ref[slot].reshape(2 * LANES, 2 * LANES)
        nothing = jnp.zeros_like(every)
        reads = []
        for inner_rows, rest_rows in windows:
            lanes = jnp.concatenate([kept(l, inner_rows or INNER), kept(l, rest_rows or outer_rows)], axis=1)
            lanes = jnp.broadcast_to(lanes, every.shape).astype(jnp.bfloat16) != 0
            read = jnp.where(lanes, every, nothing)
            for start in range(0, count, TILE):
                stop = min(start + TILE, count)
                reads.append(read[start:stop])
                reads.append(read[LANES + start : LANES + stop])
        gram = lax.dot_general(jnp.concatenate(reads, axis=0), every, NT, preferred_element_type=jnp.float32)
        for w in range(2):
            real, imag = [], []
            for start in range(0, count, TILE):
                height = min(TILE, count - start)
                base = 2 * (w * count + start)
                re, im = gram[base : base + height], gram[base + height : base + 2 * height]
                real.append(re[:, :LANES] + im[:, LANES:])
                imag.append(im[:, :LANES] - re[:, LANES:])
            normalised(jnp.concatenate(real, axis=0), jnp.concatenate(imag, axis=0), w, l)


def looked(half, other, top, mid, low, first, groups, looks, previous, terms, slab):
    count = other.shape[3]

    def spec(array):
        offset = 0 if array is other else first
        return pl.BlockSpec((array.shape[0], 1) + array.shape[2:], lambda s: (0, s + offset, 0, 0, 0))

    operands = [other, top, mid, low]
    in_specs = [spec(a) for a in operands]
    aliases = {}
    if previous is not None:
        aliases = {len(operands): 0}
        operands.append(previous)
        in_specs.append(pl.BlockSpec(memory_space=pl.ANY))
    for term in terms:
        operands.append(term)
        in_specs.append(pl.BlockSpec(term.shape, lambda s: (0, 0)))
    extra = (2, count, count) if slab else (LANES, LANES)
    out_specs = [
        pl.BlockSpec((2, PER, 2, count, count), lambda s: (half, s + first, 0, 0, 0)),
        pl.BlockSpec(extra, lambda s: (0,) * len(extra)),
    ]
    out_shape = [
        jax.ShapeDtypeStruct((ROWS // 2, looks, 2, count, count), jnp.bfloat16),
        jax.ShapeDtypeStruct(extra, jnp.float32),
    ]
    return pl.pallas_call(
        functools.partial(looks_kernel, half, previous is not None, len(terms), slab),
        grid=(groups,),
        in_specs=in_specs,
        out_specs=out_specs,
        out_shape=out_shape,
        input_output_aliases=aliases,
        scratch_shapes=[
            pltpu.VMEM((2, 2, LANES, 2 * LANES), jnp.bfloat16),
        ],
        compiler_params=pltpu.CompilerParams(vmem_limit_bytes=48 * 2**20),
        cost_estimate=pl.CostEstimate(
            flops=groups * PER * 2 * 512 * 256 * 256, bytes_accessed=groups * 10**6, transcendentals=0
        ),
        name="looks",
    )(*operands)


def rounds(size):
    found = []
    stride = 1
    while stride < size:
        radix = 4 if size // stride % 4 == 0 else 2
        if size // stride % radix:
            return None
        found.append((stride, radix))
        stride *= radix
    return found[::-1]


def round_terms(value, axis, stride, radix):
    size = lax.axis_size(axis)
    terms = [value]
    for shift in range(1, radix):
        pairs = []
        for i in range(size):
            place = (i // stride) % radix
            pairs.append((i, i + ((place + shift) % radix - place) * stride))
        terms.append(lax.ppermute(value, axis, pairs))
    return terms


def shards(images, valid_mask):
    looks = images.shape[3] // LOOK
    groups = -(-looks // PER)
    cut = -(-groups // 2)
    size = lax.axis_size("pix")
    forward = [(i, i + 1) for i in range(size - 1)]
    backward = [(i + 1, i) for i in range(size - 1)]
    top, low = edge_rows(images, valid_mask, groups)
    after = lax.ppermute(top, "pix", backward)
    mid, total, low, low0, low1 = middle_rows(images, valid_mask, low, cut)
    before0 = lax.ppermute(low0, "pix", forward)
    before1 = lax.ppermute(low1, "pix", forward)
    steps = rounds(size)
    if steps is None:
        terms, steps = [lax.psum(total, "pix")], []
    else:
        terms = round_terms(total, "pix", *steps[0]) if steps else [total]
    out, zeros = looked(1, after, top, mid, low, 0, groups, looks, None, [], False)
    for step in steps[1:]:
        terms = round_terms(added(terms) + zeros, "pix", *step)
    out, _ = looked(0, before0, top, mid, low, 0, cut, looks, out, [], False)
    out, slab = looked(0, before1, top, mid, low, cut, groups - cut, looks, out, terms, True)
    return (out, slab)


def solution(mesh):
    in_specs = (P(("group", "pix"), None, None, None), P(("group", "pix"), None))
    out_specs = (P(("group", "pix"), None, None, None, None), P("group", None, None))
    return jax.shard_map(shards, mesh=mesh, in_specs=in_specs, out_specs=out_specs, check_vma=False)
```

```python
import functools
import jax
import jax.numpy as jnp
from jax import lax
from jax.experimental import pallas as pl
from jax.experimental.pallas import tpu as pltpu
from jax.sharding import PartitionSpec as P

floor_power = 30.0

LOOK = 21
LANES = 128
TILE = 16
PER = LANES // LOOK
SPAN = PER * LOOK
ROWS = 8
SKEW = (5, 0, 1, 2, 3, 4, 1, 2)
BEFORE, AFTER = 3, 2
NT = (((1,), (1,)), ((), ()))


def turned(image, mask, skew, columns, put):
    count = image[0].shape[0]
    zero = jnp.zeros((count, LANES), jnp.bfloat16)
    lane = lax.broadcasted_iota(jnp.int32, (1, LANES), 1)

    def tile(value, g):
        start, stop = g * LANES, min((g + 1) * LANES, columns)
        part = value[:, start:stop]
        if stop - start < LANES:
            rest = jnp.zeros((part.shape[0], LANES - (stop - start)), part.dtype)
            part = jnp.concatenate([part, rest], axis=1)
        return part

    def widened(which):
        return jnp.broadcast_to(which.astype(jnp.float32), (count, LANES)).astype(jnp.bfloat16) != 0

    tiles = -(-columns // LANES)
    for g in range(-(-columns // SPAN)):
        slide = (LANES - SPAN) * g
        place = (lane + slide) % LANES
        used = (place < SPAN) & (SPAN * g + place < columns)
        prior = lane >= LANES - slide
        sides = [t for t in (g - 1, g) if 0 <= t < tiles]

        def joined(value):
            parts = [tile(value, t) for t in sides]
            if len(parts) == 1:
                return parts[0]
            which = prior if value.shape[0] == 1 else widened(prior)
            return jnp.where(which, parts[0], parts[1])

        keep = widened(used & (joined(mask) != 0))
        for k in range(2):
            row = jnp.where(keep, joined(image[k]), zero)
            put(g, k, pltpu.roll(row, slide + LOOK * skew, 1))


def fetched(image_ref, mask_ref, rows_ref, masks_ref, sems, order):
    mask_copy = pltpu.make_async_copy(mask_ref, masks_ref, sems.at[len(order)])
    mask_copy.start()
    copies = [pltpu.make_async_copy(image_ref.at[row], rows_ref.at[at], sems.at[at]) for at, row in enumerate(order)]
    for copy in copies:
        copy.start()
    mask_copy.wait()
    return copies


EDGE = tuple(range(AFTER)) + tuple(range(ROWS - BEFORE, ROWS))


def edge_kernel(image_ref, mask_ref, top_ref, low_ref, rows_ref, masks_ref, turned_ref, in_sems, out_sems):
    fetches = fetched(image_ref, mask_ref, rows_ref, masks_ref, in_sems, EDGE)
    stores = []
    for at, row in enumerate(EDGE):
        fetches[at].wait()

        def put(g, k, value):
            turned_ref[at, g, k] = value

        turned([rows_ref.at[at, 0], rows_ref.at[at, 1]], masks_ref[row : row + 1, :], SKEW[row], masks_ref.shape[1], put)
        target = top_ref.at[row] if row < AFTER else low_ref.at[row - (ROWS - BEFORE)]
        store = pltpu.make_async_copy(turned_ref.at[at], target, out_sems.at[at])
        store.start()
        stores.append(store)
    for store in stores:
        store.wait()


def rows_shape(rows, groups, count):
    return jax.ShapeDtypeStruct((rows, groups, 2, count, LANES), jnp.bfloat16)


def edge_rows(images, valid_mask, groups):
    count = images.shape[2]
    far = pl.BlockSpec(memory_space=pl.ANY)
    return pl.pallas_call(
        edge_kernel,
        in_specs=[far, far],
        out_specs=[far] * 2,
        out_shape=[
            rows_shape(AFTER, groups, count),
            rows_shape(BEFORE, groups, count),
        ],
        scratch_shapes=[
            pltpu.VMEM((len(EDGE),) + images.shape[1:], jnp.bfloat16),
            pltpu.VMEM(valid_mask.shape, jnp.int32),
            pltpu.VMEM((len(EDGE), groups, 2, count, LANES), jnp.bfloat16),
            pltpu.SemaphoreType.DMA((len(EDGE) + 1,)),
            pltpu.SemaphoreType.DMA((len(EDGE),)),
        ],
        compiler_params=pltpu.CompilerParams(vmem_limit_bytes=61 * 2**20),
        cost_estimate=pl.CostEstimate(flops=10**6, bytes_accessed=4 * 10**6, transcendentals=0),
        name="edge_rows",
    )(images, valid_mask)


def middle_kernel(cut, image_ref, mask_ref, low_ref, mid_ref, gram_ref, again_ref, first_ref, second_ref, *scratch):
    rows_ref, masks_ref, turned_ref, z_ref, in_sems, out_sems = scratch
    groups = mid_ref.shape[1]
    count, columns = image_ref.shape[2:]
    order = tuple(range(AFTER, ROWS - BEFORE)) + EDGE
    fetches = fetched(image_ref, mask_ref, rows_ref, masks_ref, in_sems, order)
    stores = []
    for target, start, stop in ((first_ref, 0, cut), (second_ref, cut, groups), (again_ref, 0, groups)):
        sem = out_sems.at[ROWS - AFTER - BEFORE + len(stores)]
        stores.append(pltpu.make_async_copy(low_ref.at[:, start:stop], target, sem))
        stores[-1].start()
    z_ref[...] = jnp.zeros_like(z_ref)
    zero = jnp.zeros((count, columns), jnp.bfloat16)
    total = None
    wide = groups * LANES
    for at, row in enumerate(order):
        fetches[at].wait()
        mask = masks_ref[row : row + 1, :]
        if AFTER <= row < ROWS - BEFORE:

            def put(g, k, value):
                turned_ref[at, g, k] = value
                z_ref[pl.ds(k * LANES, count), pl.ds(at * wide + g * LANES, LANES)] = value

            turned([rows_ref.at[at, 0], rows_ref.at[at, 1]], mask, SKEW[row], columns, put)
            store = pltpu.make_async_copy(turned_ref.at[at], mid_ref.at[row - AFTER], out_sems.at[at])
            store.start()
            stores.append(store)
        else:
            keep = jnp.broadcast_to((mask != 0).astype(jnp.float32), (count, columns)).astype(jnp.bfloat16) != 0
            for k in range(2):
                z_ref[pl.ds(k * LANES, count), pl.ds(at * wide, columns)] = jnp.where(keep, rows_ref[at, k], zero)
        if at % 2:
            z = z_ref[:, pl.ds((at - 1) * wide, 2 * wide)]
            part = lax.dot_general(z, z, NT, preferred_element_type=jnp.float32)
            total = part if total is None else total + part
    real = total[:LANES, :LANES] + total[LANES:, LANES:]
    imag = total[LANES:, :LANES] - total[:LANES, LANES:]
    i = lax.broadcasted_iota(jnp.int32, real.shape, 0)
    j = lax.broadcasted_iota(jnp.int32, real.shape, 1)
    gram_ref[...] = jnp.where(i <= j, real, imag)
    for store in stores:
        store.wait()


def middle_rows(images, valid_mask, low, cut):
    count = images.shape[2]
    groups = low.shape[1]
    rows = ROWS - AFTER - BEFORE
    far = pl.BlockSpec(memory_space=pl.ANY)
    return pl.pallas_call(
        functools.partial(middle_kernel, cut),
        in_specs=[far, far, far],
        out_specs=[far, pl.BlockSpec(memory_space=pltpu.VMEM), far, far, far],
        out_shape=[
            rows_shape(rows, groups, count),
            jax.ShapeDtypeStruct((LANES, LANES), jnp.float32),
            jax.ShapeDtypeStruct(low.shape, low.dtype),
            rows_shape(BEFORE, cut, count),
            rows_shape(BEFORE, groups - cut, count),
        ],
        scratch_shapes=[
            pltpu.VMEM(images.shape, jnp.bfloat16),
            pltpu.VMEM(valid_mask.shape, jnp.int32),
            pltpu.VMEM((rows, groups, 2, count, LANES), jnp.bfloat16),
            pltpu.VMEM((2 * LANES, ROWS * groups * LANES), jnp.bfloat16),
            pltpu.SemaphoreType.DMA((ROWS + 1,)),
            pltpu.SemaphoreType.DMA((rows + 3,)),
        ],
        compiler_params=pltpu.CompilerParams(vmem_limit_bytes=49 * 2**20),
        cost_estimate=pl.CostEstimate(flops=10**9, bytes_accessed=5 * 10**6, transcendentals=0),
        name="middle_rows",
    )(images, valid_mask, low)


def added(terms):
    if len(terms) == 4:
        return (terms[0] + terms[2]) + (terms[1] + terms[3])
    return functools.reduce(jnp.add, terms)


def slab_values(terms):
    packed = added(terms)
    flipped = packed.T
    i = lax.broadcasted_iota(jnp.int32, packed.shape, 0)
    j = lax.broadcasted_iota(jnp.int32, packed.shape, 1)
    real = jnp.where(i <= j, packed, flipped)
    imag = jnp.where(i > j, packed, jnp.where(i < j, -flipped, 0.0))
    powers = jnp.where(i == j, packed, 0.0)
    scaled = jnp.sqrt(jnp.sum(powers, axis=1, keepdims=True) * jnp.sum(powers, axis=0, keepdims=True))
    return real / scaled, imag / scaled


INNER = (1, 2, 3, 4, 5)
HALVES = (
    ((-3, -2, -1, 0), (((1, 2, 3), None), (None, (-1, 0)))),
    ((6, 7, 8, 9), ((None, (6, 7)), ((3, 4, 5), None))),
)


def looks_kernel(half, aliased, terms, slab, *refs):
    other_ref, top_ref, mid_ref, low_ref = refs[:4]
    refs = refs[4 + aliased :]
    term_refs, refs = refs[:terms], refs[terms:]
    out_ref, extra_ref, w_ref = refs
    count = top_ref.shape[3]

    @pl.when(pl.program_id(0) == 0)
    def _():
        w_ref[...] = jnp.zeros_like(w_ref)
        if slab:
            real, imag = slab_values([t[...] for t in term_refs])
            extra_ref[0] = real[:count, :count]
            extra_ref[1] = imag[:count, :count]
        elif terms:
            extra_ref[...] = added([t[...] for t in term_refs])
        else:
            extra_ref[...] = jnp.zeros_like(extra_ref)

    rows = {}
    for r in range(ROWS):
        if r < AFTER:
            rows[r] = top_ref.at[r, 0]
        elif r >= ROWS - BEFORE:
            rows[r] = low_ref.at[r - (ROWS - BEFORE), 0]
        else:
            rows[r] = mid_ref.at[r - AFTER, 0]
    for r in range(other_ref.shape[0]):
        rows[ROWS + r if half else r - BEFORE] = other_ref.at[r, 0]

    lane = lax.broadcasted_iota(jnp.int32, (1, LANES), 1)

    def lanes_of(turn):
        place = lane + (-LOOK * turn) % LANES
        place = jnp.where(place >= LANES, place - LANES, place)
        return place < LOOK

    def widened(which):
        return jnp.broadcast_to(which.astype(jnp.float32), (count, LANES)).astype(jnp.bfloat16) != 0

    single = [lanes_of(t) for t in range(2 * PER - 1)]
    wide = [widened(s) for s in single]

    def turn(l, r):
        return l + SKEW[r % ROWS]

    def gathered(l, k, which):
        out = rows[which[0]][k]
        for r in which[1:]:
            out = jnp.where(wide[turn(l, r)], rows[r][k], out)
        return out

    def kept(l, which):
        select = single[turn(l, which[0])]
        for r in which[1:]:
            select = select | single[turn(l, r)]
        return select.astype(jnp.float32)

    eight = (8, LANES)
    along = lax.broadcasted_iota(jnp.int32, eight, 1)
    on_eye = along % 8 == lax.broadcasted_iota(jnp.int32, eight, 0)
    block = along // 8

    def normalised(real, imag, w, l):
        picked = real[:8]
        for v in range(1, count // 8):
            picked = jnp.where(block == v, real[8 * v : 8 * v + 8], picked)
        power = jnp.sum(jnp.where(on_eye, picked, 0.0), axis=0, keepdims=True)
        across = lax.rsqrt(jnp.maximum(power, floor_power))
        diagonal = jnp.where(on_eye, across, 0.0)
        spread = jnp.concatenate([jnp.where(block == v, diagonal, 0.0) for v in range(count // 8)], axis=0)
        scale = jnp.sum(spread, axis=1, keepdims=True) * across
        out_ref[w, l, 0] = (real * scale).astype(jnp.bfloat16)[:, :count]
        out_ref[w, l, 1] = (imag * scale).astype(jnp.bfloat16)[:, :count]

    outer_rows, windows = HALVES[half]
    for l in range(PER):
        slot = l % 2
        for k in range(2):
            w_ref[slot, k, pl.ds(0, count), pl.ds(0, LANES)] = gathered(l, k, INNER)
            w_ref[slot, k, pl.ds(0, count), pl.ds(LANES, LANES)] = gathered(l, k, outer_rows)
        every = w_ref[slot].reshape(2 * LANES, 2 * LANES)
        nothing = jnp.zeros_like(every)
        reads = []
        for inner_rows, rest_rows in windows:
            lanes = jnp.concatenate([kept(l, inner_rows or INNER), kept(l, rest_rows or outer_rows)], axis=1)
            lanes = jnp.broadcast_to(lanes, every.shape).astype(jnp.bfloat16) != 0
            read = jnp.where(lanes, every, nothing)
            for start in range(0, count, TILE):
                stop = min(start + TILE, count)
                reads.append(read[start:stop])
                reads.append(read[LANES + start : LANES + stop])
        gram = lax.dot_general(jnp.concatenate(reads, axis=0), every, NT, preferred_element_type=jnp.float32)
        for w in range(2):
            real, imag = [], []
            for start in range(0, count, TILE):
                height = min(TILE, count - start)
                base = 2 * (w * count + start)
                re, im = gram[base : base + height], gram[base + height : base + 2 * height]
                real.append(re[:, :LANES] + im[:, LANES:])
                imag.append(im[:, :LANES] - re[:, LANES:])
            normalised(jnp.concatenate(real, axis=0), jnp.concatenate(imag, axis=0), w, l)


def looked(half, other, top, mid, low, first, groups, looks, previous, terms, slab):
    count = other.shape[3]

    def spec(array):
        offset = 0 if array is other else first
        return pl.BlockSpec((array.shape[0], 1) + array.shape[2:], lambda s: (0, s + offset, 0, 0, 0))

    operands = [other, top, mid, low]
    in_specs = [spec(a) for a in operands]
    aliases = {}
    if previous is not None:
        aliases = {len(operands): 0}
        operands.append(previous)
        in_specs.append(pl.BlockSpec(memory_space=pl.ANY))
    for term in terms:
        operands.append(term)
        in_specs.append(pl.BlockSpec(term.shape, lambda s: (0, 0)))
    extra = (2, count, count) if slab else (LANES, LANES)
    out_specs = [
        pl.BlockSpec((2, PER, 2, count, count), lambda s: (half, s + first, 0, 0, 0)),
        pl.BlockSpec(extra, lambda s: (0,) * len(extra)),
    ]
    out_shape = [
        jax.ShapeDtypeStruct((ROWS // 2, looks, 2, count, count), jnp.bfloat16),
        jax.ShapeDtypeStruct(extra, jnp.float32),
    ]
    return pl.pallas_call(
        functools.partial(looks_kernel, half, previous is not None, len(terms), slab),
        grid=(groups,),
        in_specs=in_specs,
        out_specs=out_specs,
        out_shape=out_shape,
        input_output_aliases=aliases,
        scratch_shapes=[
            pltpu.VMEM((2, 2, LANES, 2 * LANES), jnp.bfloat16),
        ],
        compiler_params=pltpu.CompilerParams(vmem_limit_bytes=48 * 2**20),
        cost_estimate=pl.CostEstimate(
            flops=groups * PER * 2 * 512 * 256 * 256, bytes_accessed=groups * 10**6, transcendentals=0
        ),
        name="looks",
    )(*operands)


def rounds(size):
    found = []
    stride = 1
    while stride < size:
        radix = 4 if size // stride % 4 == 0 else 2
        if size // stride % radix:
            return None
        found.append((stride, radix))
        stride *= radix
    return found[::-1]


def round_terms(value, axis, stride, radix):
    size = lax.axis_size(axis)
    terms = [value]
    for shift in range(1, radix):
        pairs = []
        for i in range(size):
            place = (i // stride) % radix
            pairs.append((i, i + ((place + shift) % radix - place) * stride))
        terms.append(lax.ppermute(value, axis, pairs))
    return terms


def shards(images, valid_mask):
    looks = images.shape[3] // LOOK
    groups = -(-looks // PER)
    cut = groups // 2
    size = lax.axis_size("pix")
    forward = [(i, i + 1) for i in range(size - 1)]
    backward = [(i + 1, i) for i in range(size - 1)]
    top, low = edge_rows(images, valid_mask, groups)
    after = lax.ppermute(top, "pix", backward)
    mid, total, low, low0, low1 = middle_rows(images, valid_mask, low, cut)
    before0 = lax.ppermute(low0, "pix", forward)
    before1 = lax.ppermute(low1, "pix", forward)
    steps = rounds(size)
    if steps is None:
        terms, steps = [lax.psum(total, "pix")], []
    else:
        terms = round_terms(total, "pix", *steps[0]) if steps else [total]
    out, zeros = looked(1, after, top, mid, low, 0, groups, looks, None, [], False)
    for step in steps[1:]:
        terms = round_terms(added(terms) + zeros, "pix", *step)
    out, _ = looked(0, before0, top, mid, low, 0, cut, looks, out, [], False)
    out, slab = looked(0, before1, top, mid, low, cut, groups - cut, looks, out, terms, True)
    return (out, slab)


def solution(mesh):
    in_specs = (P(("group", "pix"), None, None, None), P(("group", "pix"), None))
    out_specs = (P(("group", "pix"), None, None, None, None), P("group", None, None))
    return jax.shard_map(shards, mesh=mesh, in_specs=in_specs, out_specs=out_specs, check_vma=False)
```
